32 devices in a mesh: grp: 8 (over z, x), row: 4 (over y, core).
Axes of the slice: x: 2, y: 2, z: 4, core: 2. Of those that a mesh axis runs over, the one named last changes fastest.
Arguments:
- features: bfloat16 [262144, 512], P(('grp', 'row')), may hold values from -6 to 6
- precinct: int32 [262144], P(('grp', 'row')), may hold values from 0 to 1023
- outcome: int32 [262144], P(('grp', 'row')), may hold values from 0 to 7
- row_counts: int32 [8, 4], P('grp', 'row'), may hold values from 2048 to 8192, as said below
- beta: float32 [512], replicated, may hold values from -0.125 to 0.125
- nation_coef: float32 [4, 512], replicated, may hold values from -0.125 to 0.125
- state_coef: float32 [64, 512], replicated, may hold values from -0.125 to 0.125
- county_coef: float32 [2048, 512], P('grp'), may hold values from -0.125 to 0.125
- precinct_coef: float32 [8192], P('grp'), may hold values from -3 to 3
- precinct_county: int32 [8192], P('grp'), may hold values from 0 to 255, as said below
- county_state: int32 [2048], replicated, may hold values from 0 to 63, as said below
- state_nation: int32 [64], replicated, may hold values from 0 to 3, as said below
Outputs:
- county_grad: float32 [2048, 512], P(('grp', 'row'))
- precinct_grad: float32 [8192], P('grp')
- state_grad: float32 [64, 512], replicated
- nation_grad: float32 [4, 512], replicated
- beta_grad: float32 [512], replicated
The draws below stay inside these ranges and needn't reach their ends.
Inputs may be any that keep to these rules, and one draw needn't show every extreme that they name: `precinct_county`: non-decreasing within each block of 1024 precincts; each block has 0 first and 255 last. `county_state`: non-decreasing, 0 first and 63 last. `state_nation`: non-decreasing, 0 first and 3 last. `row_counts`: some device block is full and some other holds exactly 2048 live rows.
All inputs are finite; a program needn't handle non-finite values.
Results may differ from the reference program's by a relative error of at most 0.006.
Values sent between devices are 32-bit elements; how exact they have to be, the bound alone decides.
No kernel may reach another device: no remote copies, remote signals or barrier semaphores. Data moves between devices by JAX's collectives and lax.ppermute only.
A program may use at most 64 MiB of HBM per device.

```python
import math
import jax
import jax.numpy as jnp
import numpy as np
from jax import lax

P_SIZE = 512
STATES = 64
NATIONS = 4
ROW_DEV = 8192
CNT_DEV = 256
PREC_DEV = 1024
ROWS = 262144
COUNTIES = 2048
PRECINCTS = 8192


def sorted_ends(key, rows, width, top):
    values = jnp.sort(jax.random.randint(key, (rows, width), 0, top), axis=1)
    values = values.at[:, 0].set(0)
    return values.at[:, -1].set(top - 1).reshape(-1).astype(jnp.int32)


def draw_precinct_county(key, part):
    key = jax.random.fold_in(key, 11)
    return sorted_ends(key, PRECINCTS // PREC_DEV, PREC_DEV, CNT_DEV)


def draw_county_state(key, part):
    key = jax.random.fold_in(key, 12)
    return sorted_ends(key, 1, COUNTIES, STATES)


def draw_state_nation(key, part):
    key = jax.random.fold_in(key, 13)
    return sorted_ends(key, 1, STATES, NATIONS)


def draw_row_counts(key, part):
    key = jax.random.fold_in(key, 14)
    groups = COUNTIES // CNT_DEV
    splits = ROWS // ROW_DEV // groups
    total = groups * splits
    first, second, third = jax.random.split(key, 3)
    flat = jax.random.randint(first, (total,), ROW_DEV // 4, ROW_DEV + 1)
    chosen = jax.random.randint(second, (), 0, total)
    other = (chosen + jax.random.randint(third, (), 1, total)) % total
    places = jnp.arange(total)
    flat = jnp.where(places == chosen, ROW_DEV, flat)
    flat = jnp.where(places == other, ROW_DEV // 4, flat)
    return flat.reshape(groups, splits).astype(jnp.int32)


def place_ends(values, rng, low, largest):
    longest = values.shape.index(max(values.shape))
    spots = []
    for shift in (0, 1):
        where = [jax.random.randint(jax.random.fold_in(rng, axis), (), 0, length) for axis, length in enumerate(values.shape)]
        where[longest] = (where[longest] + shift) % values.shape[longest]
        spots.append(tuple(where))
    return values.at[spots[0]].set(low).at[spots[1]].set(largest)


def level_of(rng, extent, cuts, least, largest):
    def one(axis_at, blocks):
        heights = jax.random.uniform(jax.random.fold_in(jax.random.fold_in(rng, 6), axis_at), (blocks,), jnp.float32, least / len(cuts), largest / len(cuts))
        return jnp.repeat(jnp.exp(heights), extent[axis_at] // blocks).reshape((-1,) + (1,) * (len(extent) - axis_at - 1))

    loudness = one(*cuts[0])
    for cut in cuts[1:]:
        loudness = loudness * one(*cut)
    return loudness


def rank_table(amount, lean):
    weights = [(1 << 20) // math.isqrt(grade ** lean) + 1 for grade in range(1, amount + 1)]
    scale = 1 + sum(weights) // (1 << 30)
    return np.cumsum(np.array([max(1, weight // scale) for weight in weights]))


def skewed_ids(rng, shape, count, slope):
    table = rank_table(count, slope)
    lot = jax.random.randint(jax.random.fold_in(rng, 1), shape, 0, int(table[count - 1]))
    rank = jnp.searchsorted(jnp.asarray(table, jnp.int32), lot, side="right")
    return jax.random.permutation(jax.random.fold_in(rng, 2), count)[rank].astype(jnp.int32)


def gaussian(rng, extent, deviation, limit, shards=(), kind=jnp.bfloat16):
    drawn = jax.random.normal(rng, extent, jnp.float32) * deviation
    if len(shards) > 0:
        drawn = level_of(rng, extent, shards, -0.22, 0.18) * drawn
    return jnp.clip(drawn, min=-limit, max=limit).astype(kind)


def setup_inputs(seed: int = 0) -> dict:
    streams_of = jax.random.split(jax.random.key(seed), 13)
    features = gaussian(streams_of[0], (ROWS, P_SIZE), 1.0, 6.0, ((0, 32),))
    precinct = place_ends(skewed_ids(streams_of[1], (ROWS,), PREC_DEV, 2), jax.random.fold_in(streams_of[1], 3), 0, PREC_DEV - 1).astype(jnp.int32)
    outcome = place_ends(jax.random.randint(streams_of[2], (ROWS,), 0, 8), jax.random.fold_in(streams_of[2], 1), 0, 7).astype(jnp.int32)
    row_counts = draw_row_counts(jax.random.fold_in(streams_of[12], 71), 0)
    beta = gaussian(streams_of[4], (P_SIZE,), (4 * P_SIZE) ** -0.5, 0.125, (), jnp.float32)
    nation_coef = gaussian(streams_of[5], (NATIONS, P_SIZE), (4 * P_SIZE) ** -0.5, 0.125, (), jnp.float32)
    state_coef = gaussian(streams_of[6], (STATES, P_SIZE), (4 * P_SIZE) ** -0.5, 0.125, (), jnp.float32)
    county_coef = gaussian(streams_of[7], (COUNTIES, P_SIZE), (4 * P_SIZE) ** -0.5, 0.125, ((0, 8),), jnp.float32)
    precinct_coef = gaussian(streams_of[8], (PRECINCTS,), 0.5, 3.0, ((0, 8),), jnp.float32)
    precinct_county = draw_precinct_county(jax.random.fold_in(streams_of[12], 71), 0)
    county_state = draw_county_state(jax.random.fold_in(streams_of[12], 71), 0)
    state_nation = draw_state_nation(jax.random.fold_in(streams_of[12], 71), 0)
    return dict(features=features, precinct=precinct, outcome=outcome, row_counts=row_counts, beta=beta, nation_coef=nation_coef, state_coef=state_coef, county_coef=county_coef, precinct_coef=precinct_coef, precinct_county=precinct_county, county_state=county_state, state_nation=state_nation)


def reference(features, precinct, outcome, row_counts, beta, nation_coef, state_coef, county_coef, precinct_coef, precinct_county, county_state, state_nation):
    groups = COUNTIES // CNT_DEV
    rows_grp = ROWS // groups
    upper_coef = state_coef + nation_coef[state_nation]
    coef_table = (county_coef + upper_coef[county_state] + beta[None, :]).astype(jnp.bfloat16)

    def per_group(grp_index):
        feats = lax.dynamic_slice_in_dim(features, grp_index * rows_grp, rows_grp, 0).astype(jnp.float32)
        prec_rows = lax.dynamic_slice_in_dim(precinct, grp_index * rows_grp, rows_grp, 0)
        counts_here = lax.dynamic_slice_in_dim(outcome, grp_index * rows_grp, rows_grp, 0)
        prec_map = lax.dynamic_slice_in_dim(precinct_county, grp_index * PREC_DEV, PREC_DEV, 0)
        prec_vals = lax.dynamic_slice_in_dim(precinct_coef, grp_index * PREC_DEV, PREC_DEV, 0)
        local_table = lax.dynamic_slice_in_dim(coef_table, grp_index * CNT_DEV, CNT_DEV, 0)
        county_rows = prec_map[prec_rows]
        linear = jnp.sum(feats * local_table[county_rows].astype(jnp.float32), axis=1) + prec_vals[prec_rows]
        limits = row_counts[grp_index]
        live_rows = (jnp.arange(ROW_DEV, dtype=jnp.int32)[None, :] < limits[:, None]).reshape(-1)
        residual = jnp.where(live_rows, counts_here.astype(jnp.float32) - jnp.exp(linear), jnp.float32(0.0))
        rounded = lax.optimization_barrier(residual.astype(jnp.bfloat16)).astype(jnp.float32)
        county_part = jax.ops.segment_sum(rounded[:, None] * feats, county_rows, num_segments=CNT_DEV)
        precinct_part = jax.ops.segment_sum(residual, prec_rows, num_segments=PREC_DEV)
        return county_part, precinct_part

    county_parts, precinct_parts = lax.map(per_group, jnp.arange(groups, dtype=jnp.int32))
    county_total = county_parts.reshape(COUNTIES, P_SIZE)
    precinct_total = precinct_parts.reshape(PRECINCTS)
    state_total = jax.ops.segment_sum(county_total, county_state, num_segments=STATES)
    nation_total = jax.ops.segment_sum(state_total, state_nation, num_segments=NATIONS)
    beta_total = jnp.sum(nation_total, axis=0)
    return (county_total - county_coef, precinct_total - precinct_coef, state_total - state_coef, nation_total - nation_coef, beta_total - beta)
```

```python
import functools

import jax
import jax.numpy as jnp
from jax import lax
from jax.experimental import pallas as pl
from jax.experimental.pallas import tpu as pltpu
from jax.sharding import PartitionSpec as P

LANES = 128
ROW_STEP = 1024
ROW_CHUNK = 512
F32 = jnp.float32
BF16 = jnp.bfloat16


def split3(x):
    a = x.astype(BF16)
    r = x - a.astype(F32)
    b = r.astype(BF16)
    c = (r - b.astype(F32)).astype(BF16)
    return a, b, c


def hot_dot(hot, x, dims):
    out = None
    for part in reversed(split3(x)):
        term = lax.dot_general(hot, part, (dims, ((), ())), preferred_element_type=F32)
        out = term if out is None else out + term
    return out


def iota_rows(n):
    return lax.broadcasted_iota(jnp.int32, (n, 1), 0)


def main_kernel(
    count_ref,
    features_ref,
    precinct_ref,
    outcome_ref,
    beta_ref,
    nation_ref,
    state_ref,
    county_ref,
    prec_ref,
    map_ref,
    county_state_ref,
    state_nation_ref,
    county_out,
    state_out,
    table,
    lookup,
    county_acc,
    prec_acc,
):
    step = pl.program_id(0)
    steps = pl.num_programs(0)
    n_states = state_ref.shape[0]
    n_nations = nation_ref.shape[0]
    n_cnt, p_size = county_ref.shape
    n_hi = prec_ref.shape[0]
    group = lax.axis_index("grp")
    states = county_state_ref[group]
    state_hot = (iota_rows(n_states) == states).astype(F32).astype(BF16)

    @pl.when(step == 0)
    def _():
        nation_hot = (iota_rows(n_nations) == state_nation_ref[...]).astype(F32).astype(BF16)
        upper = state_ref[...] + hot_dot(nation_hot, nation_ref[...], ((0,), (0,)))
        table[...] = (
            county_ref[...] + hot_dot(state_hot, upper, ((0,), (0,))) + beta_ref[...]
        ).astype(BF16)
        lookup[...] = jnp.concatenate(
            [x.astype(F32) for x in split3(prec_ref[...])] + [map_ref[...].astype(F32)], axis=0
        ).astype(BF16)
        county_acc[...] = jnp.zeros_like(county_acc)
        prec_acc[...] = jnp.zeros_like(prec_acc)

    chunk = ROW_CHUNK
    for at in range(0, ROW_STEP, chunk):
        feats = features_ref[at : at + chunk, :]
        prec = precinct_ref[0, :, at : at + chunk]
        count = outcome_ref[0, :, at : at + chunk].astype(F32)
        low = jnp.bitwise_and(prec, LANES - 1)
        high = jnp.right_shift(prec, 7)
        low_hot = (iota_rows(LANES) == low).astype(F32).astype(BF16)
        high_hot = iota_rows(n_hi) == high
        found = jnp.dot(lookup[...], low_hot, preferred_element_type=F32)
        coef = found[:n_hi] + found[n_hi : 2 * n_hi] + found[2 * n_hi : 3 * n_hi]
        intercept = jnp.sum(jnp.where(high_hot, coef, 0.0), axis=0, keepdims=True)
        county = jnp.sum(
            jnp.where(high_hot, found[3 * n_hi :], 0.0), axis=0, keepdims=True
        ).astype(jnp.int32)
        county_hot = iota_rows(n_cnt) == county
        scores = lax.dot_general(
            table[...], feats, (((1,), (1,)), ((), ())), preferred_element_type=F32
        )
        linear = jnp.sum(jnp.where(county_hot, scores, 0.0), axis=0, keepdims=True) + intercept
        row = step * ROW_STEP + at + lax.broadcasted_iota(jnp.int32, (1, chunk), 1)
        residual = jnp.where(row < count_ref[0, 0], count - jnp.exp(linear), 0.0)
        rounded = residual.astype(BF16).astype(F32)
        weighted = jnp.where(county_hot, rounded, 0.0).astype(BF16)
        county_acc[...] += jnp.dot(weighted, feats, preferred_element_type=F32)
        by_high = jnp.concatenate(
            [jnp.where(high_hot, x.astype(F32), 0.0) for x in split3(residual)], axis=0
        ).astype(BF16)
        prec_acc[...] += lax.dot_general(
            by_high, low_hot, (((1,), (1,)), ((), ())), preferred_element_type=F32
        )

    @pl.when(step == steps - 1)
    def _():
        n_row, padded, _ = county_out.shape
        share = n_cnt // n_row
        total = county_acc[...]
        prec_sum = prec_acc[:n_hi] + prec_acc[n_hi : 2 * n_hi] + prec_acc[2 * n_hi :]
        for r in range(n_row):
            county_out[r, :share, :] = total[r * share : (r + 1) * share, :]
            county_out[r, share:, :LANES] = prec_sum
            county_out[r, share:, LANES:] = jnp.zeros((padded - share, p_size - LANES), F32)
        state_sum = hot_dot(state_hot, total, ((1,), (0,)))
        pieces, per, _ = state_out.shape
        blocks = p_size // LANES
        for k in range(pieces):
            top = k // blocks * per
            left = k % blocks * LANES
            state_out[k] = state_sum[top : top + per, left : left + LANES]


def end_kernel(
    state_nation_ref, gathered_ref, state_ref, nation_ref, beta_ref, state_out, nation_out, beta_out, total
):
    pieces, per, _ = gathered_ref.shape
    blocks = total.shape[1] // LANES
    for k in range(pieces):
        top = k // blocks * per
        left = k % blocks * LANES
        total[top : top + per, left : left + LANES] = gathered_ref[k]
    n_nations = nation_ref.shape[0]
    nation_hot = (iota_rows(n_nations) == state_nation_ref[...]).astype(F32).astype(BF16)
    sums = total[...]
    nation_total = hot_dot(nation_hot, sums, ((1,), (0,)))
    state_out[...] = sums - state_ref[...]
    nation_out[...] = nation_total - nation_ref[...]
    beta_out[...] = jnp.sum(nation_total, axis=0, keepdims=True) - beta_ref[...]


def whole(shape):
    return pl.BlockSpec(shape, lambda i: (0,) * len(shape))


def on_device(
    features,
    precinct,
    outcome,
    row_counts,
    beta,
    nation_coef,
    state_coef,
    county_coef,
    precinct_coef,
    precinct_county,
    county_state,
    state_nation,
):
    rows_here, p_size = features.shape
    cnt_here = county_coef.shape[0]
    prec_here = precinct_coef.shape[0]
    n_states = state_coef.shape[0]
    n_row = lax.axis_size("row")
    n_grp = lax.axis_size("grp")
    row_index = lax.axis_index("row")
    share = cnt_here // n_row
    n_hi = prec_here // LANES
    steps = rows_here // ROW_STEP
    pieces = n_row * n_grp
    per = n_states * p_size // LANES // pieces
    nations = nation_coef.shape[0]

    precinct3 = precinct.reshape(steps, 1, ROW_STEP)
    outcome3 = outcome.reshape(steps, 1, ROW_STEP)
    states3 = county_state.reshape(n_grp, 1, cnt_here)
    prec2 = precinct_coef.reshape(n_hi, LANES)
    map2 = precinct_county.reshape(n_hi, LANES)
    beta2 = beta.reshape(1, p_size)
    nation_row = state_nation.reshape(1, n_states)

    county_pack, state_pack = pl.pallas_call(
        main_kernel,
        grid=(steps,),
        in_specs=[
            pl.BlockSpec(memory_space=pltpu.SMEM),
            pl.BlockSpec((ROW_STEP, p_size), lambda i: (i, 0)),
            pl.BlockSpec((1, 1, ROW_STEP), lambda i: (i, 0, 0)),
            pl.BlockSpec((1, 1, ROW_STEP), lambda i: (i, 0, 0)),
            whole(beta2.shape),
            whole(nation_coef.shape),
            whole(state_coef.shape),
            whole(county_coef.shape),
            whole(prec2.shape),
            whole(map2.shape),
            whole(states3.shape),
            whole(nation_row.shape),
        ],
        out_specs=[whole((n_row, share + n_hi, p_size)), whole((pieces, per, LANES))],
        out_shape=[
            jax.ShapeDtypeStruct((n_row, share + n_hi, p_size), F32),
            jax.ShapeDtypeStruct((pieces, per, LANES), F32),
        ],
        scratch_shapes=[
            pltpu.VMEM((cnt_here, p_size), BF16),
            pltpu.VMEM((4 * n_hi, LANES), BF16),
            pltpu.VMEM((cnt_here, p_size), F32),
            pltpu.VMEM((3 * n_hi, LANES), F32),
        ],
        compiler_params=pltpu.CompilerParams(vmem_limit_bytes=32 * 1024 * 1024),
        name="local_sums",
    )(
        row_counts,
        features,
        precinct3,
        outcome3,
        beta2,
        nation_coef,
        state_coef,
        county_coef,
        prec2,
        map2,
        states3,
        nation_row,
    )

    state_parts = lax.all_to_all(state_pack, ("grp", "row"), 0, 0, tiled=True)
    county_parts = lax.all_to_all(county_pack, "row", 0, 0, tiled=True)
    state_piece = jnp.sum(state_parts, axis=0, keepdims=True)
    gathered = lax.all_gather(state_piece, ("grp", "row"), axis=0, tiled=True)
    county_sum = jnp.sum(county_parts, axis=0)
    own_coef = lax.dynamic_slice_in_dim(county_coef, row_index * share, share, 0)
    county_grad = county_sum[:share] - own_coef
    precinct_grad = county_sum[share:, :LANES].reshape(prec_here) - precinct_coef

    state_grad, nation_grad, beta_grad = pl.pallas_call(
        end_kernel,
        out_shape=[
            jax.ShapeDtypeStruct(state_coef.shape, F32),
            jax.ShapeDtypeStruct(nation_coef.shape, F32),
            jax.ShapeDtypeStruct((1, p_size), F32),
        ],
        scratch_shapes=[pltpu.VMEM(state_coef.shape, F32)],
        name="upper_totals",
    )(nation_row, gathered, state_coef, nation_coef, beta2)
    return county_grad, precinct_grad, state_grad, nation_grad, beta_grad.reshape(p_size)


def solution(mesh):
    placed = (
        P(("grp", "row"), None),
        P(("grp", "row")),
        P(("grp", "row")),
        P("grp", "row"),
        P(),
        P(),
        P(),
        P("grp", None),
        P("grp"),
        P("grp"),
        P(),
        P(),
    )
    return jax.shard_map(
        on_device,
        mesh=mesh,
        in_specs=placed,
        out_specs=(P(("grp", "row"), None), P("grp"), P(), P(), P()),
        check_vma=False,
    )
```

```python
import functools

import jax
import jax.numpy as jnp
from jax import lax
from jax.experimental import pallas as pl
from jax.experimental.pallas import tpu as pltpu
from jax.sharding import PartitionSpec as P

LANES = 128
ROW_STEP = 1024
ROW_CHUNK = 512
VMEM_LIMIT = 60 * 1024 * 1024
F32 = jnp.float32
BF16 = jnp.bfloat16


def split3(x):
    a = x.astype(BF16)
    r = x - a.astype(F32)
    b = r.astype(BF16)
    c = (r - b.astype(F32)).astype(BF16)
    return a, b, c


def hot_dot(hot, x, dims):
    out = None
    for part in reversed(split3(x)):
        term = lax.dot_general(hot, part, (dims, ((), ())), preferred_element_type=F32)
        out = term if out is None else out + term
    return out


def iota_rows(n):
    return lax.broadcasted_iota(jnp.int32, (n, 1), 0)


def main_kernel(
    count_ref,
    features_ref,
    precinct_ref,
    outcome_ref,
    beta_ref,
    nation_ref,
    state_ref,
    county_ref,
    prec_ref,
    map_ref,
    county_state_ref,
    state_nation_ref,
    *rest,
):
    *outs, table, lookup, county_acc, prec_acc, state_acc = rest
    n_row = len(outs) // 2
    state_outs, county_outs = outs[:n_row], outs[n_row:]
    step = pl.program_id(0)
    steps = pl.num_programs(0)
    n_states = state_ref.shape[0]
    n_nations = nation_ref.shape[0]
    n_cnt, p_size = county_ref.shape
    n_hi = prec_ref.shape[0]
    group = lax.axis_index("grp")
    states = county_state_ref[group]
    state_hot = (iota_rows(n_states) == states).astype(F32).astype(BF16)

    @pl.when(step == 0)
    def _():
        nation_hot = (iota_rows(n_nations) == state_nation_ref[...]).astype(F32).astype(BF16)
        upper = state_ref[...] + hot_dot(nation_hot, nation_ref[...], ((0,), (0,)))
        table[...] = (
            county_ref[...] + hot_dot(state_hot, upper, ((0,), (0,))) + beta_ref[...]
        ).astype(BF16)
        lookup[...] = jnp.concatenate(
            [x.astype(F32) for x in split3(prec_ref[...])] + [map_ref[...].astype(F32)], axis=0
        ).astype(BF16)
        county_acc[...] = jnp.zeros_like(county_acc)
        prec_acc[...] = jnp.zeros_like(prec_acc)

    chunk = ROW_CHUNK
    for at in range(0, ROW_STEP, chunk):
        feats = features_ref[at : at + chunk, :]
        prec = precinct_ref[0, :, at : at + chunk]
        count = outcome_ref[0, :, at : at + chunk].astype(F32)
        low = jnp.bitwise_and(prec, LANES - 1)
        high = jnp.right_shift(prec, 7)
        low_hot = (iota_rows(LANES) == low).astype(F32).astype(BF16)
        high_hot = iota_rows(n_hi) == high
        found = jnp.dot(lookup[...], low_hot, preferred_element_type=F32)
        coef = found[:n_hi] + found[n_hi : 2 * n_hi] + found[2 * n_hi : 3 * n_hi]
        intercept = jnp.sum(jnp.where(high_hot, coef, 0.0), axis=0, keepdims=True)
        county = jnp.sum(
            jnp.where(high_hot, found[3 * n_hi :], 0.0), axis=0, keepdims=True
        ).astype(jnp.int32)
        county_hot = iota_rows(n_cnt) == county
        scores = lax.dot_general(
            table[...], feats, (((1,), (1,)), ((), ())), preferred_element_type=F32
        )
        linear = jnp.sum(jnp.where(county_hot, scores, 0.0), axis=0, keepdims=True) + intercept
        row = step * ROW_STEP + at + lax.broadcasted_iota(jnp.int32, (1, chunk), 1)
        residual = jnp.where(row < count_ref[0, 0], count - jnp.exp(linear), 0.0)
        rounded = residual.astype(BF16).astype(F32)
        weighted = jnp.where(county_hot, rounded, 0.0).astype(BF16)
        county_acc[...] += jnp.dot(weighted, feats, preferred_element_type=F32)
        by_high = jnp.concatenate(
            [jnp.where(high_hot, x.astype(F32), 0.0) for x in split3(residual)], axis=0
        ).astype(BF16)
        prec_acc[...] += lax.dot_general(
            by_high, low_hot, (((1,), (1,)), ((), ())), preferred_element_type=F32
        )

    @pl.when(step == steps - 1)
    def _():
        me = lax.axis_index("row")
        share = n_cnt // n_row
        per = n_states // n_row
        prec_sum = prec_acc[:n_hi] + prec_acc[n_hi : 2 * n_hi] + prec_acc[2 * n_hi :]
        state_acc[...] = hot_dot(state_hot, county_acc[...], ((1,), (0,)))
        for d in range(n_row):
            peer = jnp.bitwise_xor(me, d)
            state_outs[d][...] = state_acc[pl.ds(pl.multiple_of(peer * per, per), per), :]
            county_outs[d][:share, :] = county_acc[pl.ds(pl.multiple_of(peer * share, share), share), :]
            county_outs[d][share:, :LANES] = prec_sum
            county_outs[d][share:, LANES:] = jnp.zeros((n_hi, p_size - LANES), F32)


def end_kernel(*refs):
    state_nation_ref, *gathered, state_ref, nation_ref, beta_ref, state_out, nation_out, beta_out, total = refs
    me = lax.axis_index("row")
    per = gathered[0].shape[0]
    for d, part in enumerate(gathered):
        peer = jnp.bitwise_xor(me, d)
        total[pl.ds(pl.multiple_of(peer * per, per), per), :] = part[...]
    n_nations = nation_ref.shape[0]
    nation_hot = (iota_rows(n_nations) == state_nation_ref[...]).astype(F32).astype(BF16)
    sums = total[...]
    nation_total = hot_dot(nation_hot, sums, ((1,), (0,)))
    state_out[...] = sums - state_ref[...]
    nation_out[...] = nation_total - nation_ref[...]
    beta_out[...] = jnp.sum(nation_total, axis=0, keepdims=True) - beta_ref[...]


def swap(x, axis, d):
    n = lax.axis_size(axis)
    return lax.ppermute(x, axis, [(i, i ^ d) for i in range(n)])


def gather_by(x, axis):
    return [x] + [swap(x, axis, d) for d in range(1, lax.axis_size(axis))]


def total_of(parts):
    while len(parts) > 1:
        parts = [sum(parts[i : i + 2][1:], parts[i]) for i in range(0, len(parts), 2)]
    return parts[0]


def whole(shape):
    return pl.BlockSpec(shape, lambda i: (0,) * len(shape))


def on_device(
    features,
    precinct,
    outcome,
    row_counts,
    beta,
    nation_coef,
    state_coef,
    county_coef,
    precinct_coef,
    precinct_county,
    county_state,
    state_nation,
):
    rows_here, p_size = features.shape
    cnt_here = county_coef.shape[0]
    prec_here = precinct_coef.shape[0]
    n_states = state_coef.shape[0]
    n_row = lax.axis_size("row")
    n_grp = lax.axis_size("grp")
    row_index = lax.axis_index("row")
    share = cnt_here // n_row
    n_hi = prec_here // LANES
    steps = rows_here // ROW_STEP
    per = n_states // n_row

    precinct3 = precinct.reshape(steps, 1, ROW_STEP)
    outcome3 = outcome.reshape(steps, 1, ROW_STEP)
    states3 = county_state.reshape(n_grp, 1, cnt_here)
    prec2 = precinct_coef.reshape(n_hi, LANES)
    map2 = precinct_county.reshape(n_hi, LANES)
    beta2 = beta.reshape(1, p_size)
    nation_row = state_nation.reshape(1, n_states)

    outs = pl.pallas_call(
        main_kernel,
        grid=(steps,),
        in_specs=[
            pl.BlockSpec(memory_space=pltpu.SMEM),
            pl.BlockSpec((ROW_STEP, p_size), lambda i: (i, 0)),
            pl.BlockSpec((1, 1, ROW_STEP), lambda i: (i, 0, 0)),
            pl.BlockSpec((1, 1, ROW_STEP), lambda i: (i, 0, 0)),
            whole(beta2.shape),
            whole(nation_coef.shape),
            whole(state_coef.shape),
            whole(county_coef.shape),
            whole(prec2.shape),
            whole(map2.shape),
            whole(states3.shape),
            whole(nation_row.shape),
        ],
        out_specs=[whole((per, p_size))] * n_row + [whole((share + n_hi, p_size))] * n_row,
        out_shape=[jax.ShapeDtypeStruct((per, p_size), F32)] * n_row
        + [jax.ShapeDtypeStruct((share + n_hi, p_size), F32)] * n_row,
        scratch_shapes=[
            pltpu.VMEM((cnt_here, p_size), BF16),
            pltpu.VMEM((4 * n_hi, LANES), BF16),
            pltpu.VMEM((cnt_here, p_size), F32),
            pltpu.VMEM((3 * n_hi, LANES), F32),
            pltpu.VMEM(state_coef.shape, F32),
        ],
        compiler_params=pltpu.CompilerParams(vmem_limit_bytes=VMEM_LIMIT),
        name="local_sums",
    )(
        row_counts,
        features,
        precinct3,
        outcome3,
        beta2,
        nation_coef,
        state_coef,
        county_coef,
        prec2,
        map2,
        states3,
        nation_row,
    )

    state_parts = [outs[0]] + [swap(outs[d], "row", d) for d in range(1, n_row)]
    state_piece = total_of(state_parts)
    state_piece = total_of(gather_by(state_piece, "grp"))
    gathered = gather_by(state_piece, "row")
    county_parts = [outs[n_row]] + [swap(outs[n_row + d], "row", d) for d in range(1, n_row)]
    county_sum = total_of(county_parts)
    own_coef = lax.dynamic_slice_in_dim(county_coef, row_index * share, share, 0)
    county_grad = county_sum[:share] - own_coef
    precinct_grad = county_sum[share:, :LANES].reshape(prec_here) - precinct_coef

    state_grad, nation_grad, beta_grad = pl.pallas_call(
        end_kernel,
        out_shape=[
            jax.ShapeDtypeStruct(state_coef.shape, F32),
            jax.ShapeDtypeStruct(nation_coef.shape, F32),
            jax.ShapeDtypeStruct((1, p_size), F32),
        ],
        scratch_shapes=[pltpu.VMEM(state_coef.shape, F32)],
        name="upper_totals",
    )(nation_row, *gathered, state_coef, nation_coef, beta2)
    return county_grad, precinct_grad, state_grad, nation_grad, beta_grad.reshape(p_size)


def solution(mesh):
    placed = (
        P(("grp", "row"), None),
        P(("grp", "row")),
        P(("grp", "row")),
        P("grp", "row"),
        P(),
        P(),
        P(),
        P("grp", None),
        P("grp"),
        P("grp"),
        P(),
        P(),
    )
    return jax.shard_map(
        on_device,
        mesh=mesh,
        in_specs=placed,
        out_specs=(P(("grp", "row"), None), P("grp"), P(), P(), P()),
        check_vma=False,
    )
```

```python
import functools

import jax
import jax.numpy as jnp
from jax import lax
from jax.experimental import pallas as pl
from jax.experimental.pallas import tpu as pltpu
from jax.sharding import PartitionSpec as P

LANES = 128
ROW_STEP = 1024
VMEM_LIMIT = 60 * 1024 * 1024
F32 = jnp.float32
BF16 = jnp.bfloat16


def split3(x):
    a = x.astype(BF16)
    r = x - a.astype(F32)
    b = r.astype(BF16)
    c = (r - b.astype(F32)).astype(BF16)
    return a, b, c


def hot_dot(hot, x, dims):
    out = None
    for part in reversed(split3(x)):
        term = lax.dot_general(hot, part, (dims, ((), ())), preferred_element_type=F32)
        out = term if out is None else out + term
    return out


def iota_rows(n):
    return lax.broadcasted_iota(jnp.int32, (n, 1), 0)


def pick(values, low, high_hot):
    found = []
    for at in range(0, low.shape[1], LANES):
        index = jnp.broadcast_to(low[:, at : at + LANES], values.shape)
        found.append(jnp.take_along_axis(values, index, axis=1, mode="promise_in_bounds"))
    return jnp.sum(
        jnp.where(high_hot, jnp.concatenate(found, axis=1), jnp.zeros((), values.dtype)),
        axis=0,
        keepdims=True,
    )


def main_kernel(
    count_ref,
    features_ref,
    precinct_ref,
    outcome_ref,
    beta_ref,
    nation_ref,
    state_ref,
    county_ref,
    prec_ref,
    map_ref,
    county_state_ref,
    state_nation_ref,
    *rest,
):
    *outs, feats, table, s0, s1, h0, h1, b0, b1, r0, r1, w0, w1, county_acc, prec_acc, state_acc, sems = rest
    scores, hot_rows, bases, residuals, weights = (s0, s1), (h0, h1), (b0, b1), (r0, r1), (w0, w1)
    n_row = len(outs) // 2
    state_outs, county_outs = outs[:n_row], outs[n_row:]
    n_states = state_ref.shape[0]
    n_nations = nation_ref.shape[0]
    n_cnt, p_size = county_ref.shape
    n_hi = prec_ref.shape[0]
    chunks = precinct_ref.shape[0]
    size = precinct_ref.shape[2]

    def fetch(j):
        rows = pl.ds(pl.multiple_of(j * size, size), size)
        return pltpu.make_async_copy(features_ref.at[rows], feats.at[rows], sems.at[j])

    for j in range(chunks):
        fetch(j).start()

    states = county_state_ref[lax.axis_index("grp")]
    state_hot = (iota_rows(n_states) == states).astype(F32).astype(BF16)
    nation_hot = (iota_rows(n_nations) == state_nation_ref[...]).astype(F32).astype(BF16)
    upper = state_ref[...] + hot_dot(nation_hot, nation_ref[...], ((0,), (0,)))
    table[...] = (county_ref[...] + hot_dot(state_hot, upper, ((0,), (0,))) + beta_ref[...]).astype(BF16)
    county_acc[...] = jnp.zeros_like(county_acc)
    prec_acc[...] = jnp.zeros_like(prec_acc)

    def block(j):
        return feats[pl.ds(pl.multiple_of(j * size, size), size), :]

    def parts_of(j):
        prec = precinct_ref[j]
        return jnp.bitwise_and(prec, LANES - 1), iota_rows(n_hi) == jnp.right_shift(prec, 7)

    def score(j, k):
        low, high_hot = parts_of(j)
        bases[k][...] = pick(prec_ref[...], low, high_hot)
        hot_rows[k][...] = pick(map_ref[...], low, high_hot)
        scores[k][...] = lax.dot_general(
            table[...], block(j), (((1,), (1,)), ((), ())), preferred_element_type=F32
        )

    def residue(j, k):
        county_hot = iota_rows(n_cnt) == hot_rows[k][...]
        linear = jnp.sum(jnp.where(county_hot, scores[k][...], 0.0), axis=0, keepdims=True)
        linear = linear + bases[k][...]
        row = j * size + lax.broadcasted_iota(jnp.int32, (1, size), 1)
        count = outcome_ref[j].astype(F32)
        residual = jnp.where(row < count_ref[0, 0], count - jnp.exp(linear), 0.0)
        residuals[k][...] = residual
        rounded = residual.astype(BF16).astype(F32)
        weights[k][...] = jnp.where(county_hot, rounded, 0.0).astype(BF16)

    def collect(j, k):
        county_acc[...] += jnp.dot(weights[k][...], block(j), preferred_element_type=F32)
        low, high_hot = parts_of(j)
        low_hot = (iota_rows(LANES) == low).astype(F32).astype(BF16)
        by_high = jnp.concatenate(
            [jnp.where(high_hot, x.astype(F32), 0.0) for x in split3(residuals[k][...])[:2]], axis=0
        ).astype(BF16)
        prec_acc[...] += lax.dot_general(
            by_high, low_hot, (((1,), (1,)), ((), ())), preferred_element_type=F32
        )

    fetch(0).wait()
    score(0, 0)
    fetch(1).wait()
    score(1, 1)
    residue(0, 0)

    def body(t, carry):
        j = 2 * t
        fetch(j).wait()
        fetch(j + 1).wait()
        residue(j - 1, 1)
        score(j, 0)
        collect(j - 2, 0)
        residue(j, 0)
        score(j + 1, 1)
        collect(j - 1, 1)
        return carry

    lax.fori_loop(1, chunks // 2, body, 0)
    residue(chunks - 1, 1)
    collect(chunks - 2, 0)
    collect(chunks - 1, 1)

    me = lax.axis_index("row")
    share = n_cnt // n_row
    per = n_states // n_row
    prec_sum = prec_acc[:n_hi] + prec_acc[n_hi:]
    state_acc[...] = hot_dot(state_hot, county_acc[...], ((1,), (0,)))
    for d in range(n_row):
        peer = jnp.bitwise_xor(me, d)
        state_outs[d][...] = state_acc[pl.ds(pl.multiple_of(peer * per, per), per), :]
        county_outs[d][:share, :] = county_acc[pl.ds(pl.multiple_of(peer * share, share), share), :]
        county_outs[d][share:, :LANES] = prec_sum
        county_outs[d][share:, LANES:] = jnp.zeros((n_hi, p_size - LANES), F32)


def end_kernel(*refs):
    state_nation_ref, *gathered, state_ref, nation_ref, beta_ref, state_out, nation_out, beta_out, total = refs
    me = lax.axis_index("row")
    per = gathered[0].shape[0]
    for d, part in enumerate(gathered):
        peer = jnp.bitwise_xor(me, d)
        total[pl.ds(pl.multiple_of(peer * per, per), per), :] = part[...]
    n_nations = nation_ref.shape[0]
    nation_hot = (iota_rows(n_nations) == state_nation_ref[...]).astype(F32).astype(BF16)
    sums = total[...]
    nation_total = hot_dot(nation_hot, sums, ((1,), (0,)))
    state_out[...] = sums - state_ref[...]
    nation_out[...] = nation_total - nation_ref[...]
    beta_out[...] = jnp.sum(nation_total, axis=0, keepdims=True) - beta_ref[...]


def swap(x, axis, d):
    n = lax.axis_size(axis)
    return lax.ppermute(x, axis, [(i, i ^ d) for i in range(n)])


def gather_by(x, axis):
    return [x] + [swap(x, axis, d) for d in range(1, lax.axis_size(axis))]


def total_of(parts):
    while len(parts) > 1:
        parts = [sum(parts[i : i + 2][1:], parts[i]) for i in range(0, len(parts), 2)]
    return parts[0]


def on_device(
    features,
    precinct,
    outcome,
    row_counts,
    beta,
    nation_coef,
    state_coef,
    county_coef,
    precinct_coef,
    precinct_county,
    county_state,
    state_nation,
):
    rows_here, p_size = features.shape
    cnt_here = county_coef.shape[0]
    prec_here = precinct_coef.shape[0]
    n_states = state_coef.shape[0]
    n_row = lax.axis_size("row")
    n_grp = lax.axis_size("grp")
    row_index = lax.axis_index("row")
    share = cnt_here // n_row
    n_hi = prec_here // LANES
    steps = rows_here // ROW_STEP
    per = n_states // n_row

    precinct3 = precinct.reshape(steps, 1, ROW_STEP)
    outcome3 = outcome.reshape(steps, 1, ROW_STEP)
    states3 = county_state.reshape(n_grp, 1, cnt_here)
    prec2 = precinct_coef.reshape(n_hi, LANES)
    map2 = precinct_county.reshape(n_hi, LANES)
    beta2 = beta.reshape(1, p_size)
    nation_row = state_nation.reshape(1, n_states)

    outs = pl.pallas_call(
        main_kernel,
        in_specs=[pl.BlockSpec(memory_space=pltpu.SMEM), pl.BlockSpec(memory_space=pl.ANY)]
        + [pl.BlockSpec(memory_space=pltpu.VMEM)] * 10,
        out_shape=[jax.ShapeDtypeStruct((per, p_size), F32)] * n_row
        + [jax.ShapeDtypeStruct((share + n_hi, p_size), F32)] * n_row,
        scratch_shapes=[
            pltpu.VMEM((rows_here, p_size), BF16),
            pltpu.VMEM((cnt_here, p_size), BF16),
            pltpu.VMEM((cnt_here, ROW_STEP), F32),
            pltpu.VMEM((cnt_here, ROW_STEP), F32),
            pltpu.VMEM((1, ROW_STEP), jnp.int32),
            pltpu.VMEM((1, ROW_STEP), jnp.int32),
            pltpu.VMEM((1, ROW_STEP), F32),
            pltpu.VMEM((1, ROW_STEP), F32),
            pltpu.VMEM((1, ROW_STEP), F32),
            pltpu.VMEM((1, ROW_STEP), F32),
            pltpu.VMEM((cnt_here, ROW_STEP), BF16),
            pltpu.VMEM((cnt_here, ROW_STEP), BF16),
            pltpu.VMEM((cnt_here, p_size), F32),
            pltpu.VMEM((2 * n_hi, LANES), F32),
            pltpu.VMEM(state_coef.shape, F32),
            pltpu.SemaphoreType.DMA((steps,)),
        ],
        compiler_params=pltpu.CompilerParams(vmem_limit_bytes=VMEM_LIMIT),
        name="local_sums",
    )(
        row_counts,
        features,
        precinct3,
        outcome3,
        beta2,
        nation_coef,
        state_coef,
        county_coef,
        prec2,
        map2,
        states3,
        nation_row,
    )

    state_parts = [outs[0]] + [swap(outs[d], "row", d) for d in range(1, n_row)]
    state_piece = total_of(state_parts)
    copies = jnp.broadcast_to(state_piece, (n_grp,) + state_piece.shape)
    state_piece = jnp.sum(lax.all_to_all(copies, "grp", 0, 0, tiled=True), axis=0)
    gathered = gather_by(state_piece, "row")
    county_parts = [outs[n_row]] + [swap(outs[n_row + d], "row", d) for d in range(1, n_row)]
    county_sum = total_of(county_parts)
    own_coef = lax.dynamic_slice_in_dim(county_coef, row_index * share, share, 0)
    county_grad = county_sum[:share] - own_coef
    precinct_grad = county_sum[share:, :LANES].reshape(prec_here) - precinct_coef

    *gathered, county_grad, precinct_grad = lax.optimization_barrier(
        (*gathered, county_grad, precinct_grad)
    )
    state_grad, nation_grad, beta_grad = pl.pallas_call(
        end_kernel,
        out_shape=[
            jax.ShapeDtypeStruct(state_coef.shape, F32),
            jax.ShapeDtypeStruct(nation_coef.shape, F32),
            jax.ShapeDtypeStruct((1, p_size), F32),
        ],
        scratch_shapes=[pltpu.VMEM(state_coef.shape, F32)],
        compiler_params=pltpu.CompilerParams(vmem_limit_bytes=VMEM_LIMIT),
        name="upper_totals",
    )(nation_row, *gathered, state_coef, nation_coef, beta2)
    return county_grad, precinct_grad, state_grad, nation_grad, beta_grad.reshape(p_size)


def solution(mesh):
    placed = (
        P(("grp", "row"), None),
        P(("grp", "row")),
        P(("grp", "row")),
        P("grp", "row"),
        P(),
        P(),
        P(),
        P("grp", None),
        P("grp"),
        P("grp"),
        P(),
        P(),
    )
    return jax.shard_map(
        on_device,
        mesh=mesh,
        in_specs=placed,
        out_specs=(P(("grp", "row"), None), P("grp"), P(), P(), P()),
        check_vma=False,
    )
```

```python
import functools

import jax
import jax.numpy as jnp
from jax import lax
from jax.experimental import pallas as pl
from jax.experimental.pallas import tpu as pltpu
from jax.sharding import PartitionSpec as P

LANES = 128
ROW_STEP = 1024
SMALL = 10
VMEM_LIMIT = 60 * 1024 * 1024
END_LIMIT = 16 * 1024 * 1024
F32 = jnp.float32
BF16 = jnp.bfloat16


def split3(x):
    a = x.astype(BF16)
    r = x - a.astype(F32)
    b = r.astype(BF16)
    c = (r - b.astype(F32)).astype(BF16)
    return a, b, c


def hot_dot(hot, x, dims):
    out = None
    for part in reversed(split3(x)):
        term = lax.dot_general(hot, part, (dims, ((), ())), preferred_element_type=F32)
        out = term if out is None else out + term
    return out


def iota_rows(n):
    return lax.broadcasted_iota(jnp.int32, (n, 1), 0)


def pick(values, low, high_hot):
    found = []
    for at in range(0, low.shape[1], LANES):
        index = jnp.broadcast_to(low[:, at : at + LANES], values.shape)
        found.append(jnp.take_along_axis(values, index, axis=1, mode="promise_in_bounds"))
    return jnp.sum(
        jnp.where(high_hot, jnp.concatenate(found, axis=1), jnp.zeros((), values.dtype)),
        axis=0,
        keepdims=True,
    )


def main_kernel(n_out, count_ref, features_ref, *args):
    small = args[:SMALL]
    out_refs = args[SMALL : SMALL + n_out]
    held = args[SMALL + n_out : 2 * SMALL + n_out]
    feats, table, s0, s1, h0, h1, b0, b1, r0, r1, w0, w1, county_acc, prec_acc, state_acc, *outs, small_sems, sems, out_sems = (
        args[2 * SMALL + n_out :]
    )
    (
        state_nation_ref,
        nation_ref,
        state_ref,
        county_state_ref,
        county_ref,
        beta_ref,
        precinct_ref,
        prec_ref,
        map_ref,
        outcome_ref,
    ) = held
    scores, hot_rows, bases, residuals, weights = (s0, s1), (h0, h1), (b0, b1), (r0, r1), (w0, w1)
    n_row = len(outs) // 2
    state_outs, county_outs = outs[:n_row], outs[n_row:]
    n_states = state_ref.shape[0]
    n_nations = nation_ref.shape[0]
    n_cnt, p_size = county_ref.shape
    n_hi = prec_ref.shape[0]
    chunks = precinct_ref.shape[0]
    size = precinct_ref.shape[2]

    def fetch(j):
        rows = pl.ds(pl.multiple_of(j * size, size), size)
        return pltpu.make_async_copy(features_ref.at[rows], feats.at[rows], sems.at[j])

    small_copies = [
        pltpu.make_async_copy(source, target, small_sems.at[k])
        for k, (source, target) in enumerate(zip(small, held))
    ]
    for copy in small_copies:
        copy.start()
    for j in range(chunks):
        fetch(j).start()
    for copy in small_copies:
        copy.wait()

    states = county_state_ref[lax.axis_index("grp")]
    state_hot = (iota_rows(n_states) == states).astype(F32).astype(BF16)
    nation_hot = (iota_rows(n_nations) == state_nation_ref[...]).astype(F32).astype(BF16)
    upper = state_ref[...] + hot_dot(nation_hot, nation_ref[...], ((0,), (0,)))
    table[...] = (county_ref[...] + hot_dot(state_hot, upper, ((0,), (0,))) + beta_ref[...]).astype(BF16)
    county_acc[...] = jnp.zeros_like(county_acc)
    prec_acc[...] = jnp.zeros_like(prec_acc)

    def block(j):
        return feats[pl.ds(pl.multiple_of(j * size, size), size), :]

    def parts_of(j):
        prec = precinct_ref[j]
        return jnp.bitwise_and(prec, LANES - 1), iota_rows(n_hi) == jnp.right_shift(prec, 7)

    def score(j, k):
        low, high_hot = parts_of(j)
        bases[k][...] = pick(prec_ref[...], low, high_hot)
        hot_rows[k][...] = pick(map_ref[...], low, high_hot)
        scores[k][...] = lax.dot_general(
            table[...], block(j), (((1,), (1,)), ((), ())), preferred_element_type=F32
        )

    def residue(j, k):
        county_hot = iota_rows(n_cnt) == hot_rows[k][...]
        linear = jnp.sum(jnp.where(county_hot, scores[k][...], 0.0), axis=0, keepdims=True)
        linear = linear + bases[k][...]
        row = j * size + lax.broadcasted_iota(jnp.int32, (1, size), 1)
        count = outcome_ref[j].astype(F32)
        residual = jnp.where(row < count_ref[...], count - jnp.exp(linear), 0.0)
        residuals[k][...] = residual
        rounded = residual.astype(BF16).astype(F32)
        weights[k][...] = jnp.where(county_hot, rounded, 0.0).astype(BF16)

    def collect(j, k):
        county_acc[...] += jnp.dot(weights[k][...], block(j), preferred_element_type=F32)
        low, high_hot = parts_of(j)
        low_hot = (iota_rows(LANES) == low).astype(F32).astype(BF16)
        by_high = jnp.concatenate(
            [jnp.where(high_hot, x.astype(F32), 0.0) for x in split3(residuals[k][...])[:2]], axis=0
        ).astype(BF16)
        prec_acc[...] += lax.dot_general(
            by_high, low_hot, (((1,), (1,)), ((), ())), preferred_element_type=F32
        )

    fetch(0).wait()
    score(0, 0)
    fetch(1).wait()
    score(1, 1)
    residue(0, 0)

    def body(t, carry):
        j = 2 * t
        fetch(j).wait()
        fetch(j + 1).wait()
        residue(j - 1, 1)
        score(j, 0)
        collect(j - 2, 0)
        residue(j, 0)
        score(j + 1, 1)
        collect(j - 1, 1)
        return carry

    lax.fori_loop(1, chunks // 2, body, 0)
    residue(chunks - 1, 1)
    collect(chunks - 2, 0)
    collect(chunks - 1, 1)

    me = lax.axis_index("row")
    share = n_cnt // n_row
    per = n_states // n_row
    prec_sum = prec_acc[:n_hi] + prec_acc[n_hi:]
    own_rows = pl.ds(pl.multiple_of(me * share, share), share)

    def send(k):
        copy = pltpu.make_async_copy(outs[k], out_refs[k], out_sems.at[k])
        copy.start()
        return copy

    copies = []
    for d in range(n_row):
        peer = jnp.bitwise_xor(me, d)
        sums = county_acc[pl.ds(pl.multiple_of(peer * share, share), share), :]
        county_outs[d][:share, :] = sums if d else sums - county_ref[own_rows, :]
        county_outs[d][share:, :LANES] = prec_sum if d else prec_sum - prec_ref[...]
        county_outs[d][share:, LANES:] = jnp.zeros((n_hi, p_size - LANES), F32)
        copies.append(send(n_row + d))
    state_acc[...] = hot_dot(state_hot, county_acc[...], ((1,), (0,)))
    for d in range(n_row):
        peer = jnp.bitwise_xor(me, d)
        state_outs[d][...] = state_acc[pl.ds(pl.multiple_of(peer * per, per), per), :]
        copies.append(send(d))
    for copy in copies:
        copy.wait()


def county_end_kernel(state_nation_ref, state_ref, nation_ref, beta_ref, *refs):
    *parts, county_out, prec_out, prior_out, hot_out = refs
    share = county_out.shape[0]
    n_states = state_ref.shape[0]
    n_nations = nation_ref.shape[0]
    prior_out[:n_states, :] = state_ref[...]
    prior_out[n_states : n_states + n_nations, :] = nation_ref[...]
    prior_out[n_states + n_nations :, :] = beta_ref[...]
    hot_out[...] = (iota_rows(n_nations) == state_nation_ref[...]).astype(F32)
    county_out[...] = total_of([part[:share, :] for part in parts])
    prec_out[...] = total_of([part[share:, :LANES] for part in parts])


def end_kernel(prior_ref, hot_ref, *refs):
    *gathered, state_out, nation_out, beta_out, total = refs
    me = lax.axis_index("row")
    per = gathered[0].shape[0]
    n_states = state_out.shape[0]
    n_nations = nation_out.shape[0]
    for d, part in enumerate(gathered):
        peer = jnp.bitwise_xor(me, d)
        total[pl.ds(pl.multiple_of(peer * per, per), per), :] = part[...]
    sums = total[...]
    nation_total = hot_dot(hot_ref[...].astype(BF16), sums, ((1,), (0,)))
    state_out[...] = sums - prior_ref[:n_states, :]
    nation_out[...] = nation_total - prior_ref[n_states : n_states + n_nations, :]
    beta_out[...] = jnp.sum(nation_total, axis=0, keepdims=True) - prior_ref[n_states + n_nations :, :]


def swap(x, axis, d):
    n = lax.axis_size(axis)
    return lax.ppermute(x, axis, [(i, i ^ d) for i in range(n)])


def gather_by(x, axis, distances):
    return [x] + [swap(x, axis, d) for d in distances]


def total_of(parts):
    while len(parts) > 1:
        parts = [sum(parts[i : i + 2][1:], parts[i]) for i in range(0, len(parts), 2)]
    return parts[0]


def on_device(
    features,
    precinct,
    outcome,
    row_counts,
    beta,
    nation_coef,
    state_coef,
    county_coef,
    precinct_coef,
    precinct_county,
    county_state,
    state_nation,
):
    rows_here, p_size = features.shape
    cnt_here = county_coef.shape[0]
    prec_here = precinct_coef.shape[0]
    n_states = state_coef.shape[0]
    n_row = lax.axis_size("row")
    n_grp = lax.axis_size("grp")
    share = cnt_here // n_row
    n_hi = prec_here // LANES
    steps = rows_here // ROW_STEP
    per = n_states // n_row

    precinct3 = precinct.reshape(steps, 1, ROW_STEP)
    outcome3 = outcome.reshape(steps, 1, ROW_STEP)
    states3 = county_state.reshape(n_grp, 1, cnt_here)
    prec2 = precinct_coef.reshape(n_hi, LANES)
    map2 = precinct_county.reshape(n_hi, LANES)
    beta2 = beta.reshape(1, p_size)
    nation_row = state_nation.reshape(1, n_states)

    n_nations = nation_coef.shape[0]
    small = (
        nation_row,
        nation_coef,
        state_coef,
        states3,
        county_coef,
        beta2,
        precinct3,
        prec2,
        map2,
        outcome3,
    )
    outs = pl.pallas_call(
        functools.partial(main_kernel, 2 * n_row),
        in_specs=[pl.BlockSpec(memory_space=pltpu.VMEM)]
        + [pl.BlockSpec(memory_space=pltpu.HBM)] * (SMALL + 1),
        out_specs=[pl.BlockSpec(memory_space=pltpu.HBM)] * (2 * n_row),
        out_shape=[jax.ShapeDtypeStruct((per, p_size), F32)] * n_row
        + [jax.ShapeDtypeStruct((share + n_hi, p_size), F32)] * n_row,
        scratch_shapes=[pltpu.VMEM(x.shape, x.dtype) for x in small]
        + [
            pltpu.VMEM((rows_here, p_size), BF16),
            pltpu.VMEM((cnt_here, p_size), BF16),
            pltpu.VMEM((cnt_here, ROW_STEP), F32),
            pltpu.VMEM((cnt_here, ROW_STEP), F32),
            pltpu.VMEM((1, ROW_STEP), jnp.int32),
            pltpu.VMEM((1, ROW_STEP), jnp.int32),
            pltpu.VMEM((1, ROW_STEP), F32),
            pltpu.VMEM((1, ROW_STEP), F32),
            pltpu.VMEM((1, ROW_STEP), F32),
            pltpu.VMEM((1, ROW_STEP), F32),
            pltpu.VMEM((cnt_here, ROW_STEP), BF16),
            pltpu.VMEM((cnt_here, ROW_STEP), BF16),
            pltpu.VMEM((cnt_here, p_size), F32),
            pltpu.VMEM((2 * n_hi, LANES), F32),
            pltpu.VMEM(state_coef.shape, F32),
        ]
        + [pltpu.VMEM((per, p_size), F32)] * n_row
        + [pltpu.VMEM((share + n_hi, p_size), F32)] * n_row
        + [
            pltpu.SemaphoreType.DMA((SMALL,)),
            pltpu.SemaphoreType.DMA((steps,)),
            pltpu.SemaphoreType.DMA((2 * n_row,)),
        ],
        compiler_params=pltpu.CompilerParams(vmem_limit_bytes=VMEM_LIMIT),
        name="local_sums",
    )(row_counts, features, *small)

    near = 1 << (n_grp.bit_length() // 2 - 1)
    state_parts = [outs[0]] + [swap(outs[d], "row", d) for d in range(1, n_row)]
    state_piece = total_of(state_parts)
    state_piece, *county_outs = lax.optimization_barrier((state_piece, *outs[n_row:]))
    county_parts = [county_outs[0]] + [swap(county_outs[d], "row", d) for d in range(1, n_row)]
    state_piece = total_of(gather_by(state_piece, "grp", range(1, near)))
    state_piece = total_of(gather_by(state_piece, "grp", range(near, n_grp, near)))
    gathered = gather_by(state_piece, "row", range(1, n_row))
    county_grad, precinct_grad, prior, nation_hot = pl.pallas_call(
        county_end_kernel,
        out_shape=[
            jax.ShapeDtypeStruct((share, p_size), F32),
            jax.ShapeDtypeStruct((n_hi, LANES), F32),
            jax.ShapeDtypeStruct((n_states + n_nations + 1, p_size), F32),
            jax.ShapeDtypeStruct((n_nations, n_states), F32),
        ],
        compiler_params=pltpu.CompilerParams(vmem_limit_bytes=END_LIMIT),
        name="county_totals",
    )(nation_row, state_coef, nation_coef, beta2, *county_parts)

    state_grad, nation_grad, beta_grad = pl.pallas_call(
        end_kernel,
        out_shape=[
            jax.ShapeDtypeStruct(state_coef.shape, F32),
            jax.ShapeDtypeStruct(nation_coef.shape, F32),
            jax.ShapeDtypeStruct((1, p_size), F32),
        ],
        scratch_shapes=[pltpu.VMEM(state_coef.shape, F32)],
        compiler_params=pltpu.CompilerParams(vmem_limit_bytes=END_LIMIT),
        name="upper_totals",
    )(prior, nation_hot, *gathered)
    return county_grad, precinct_grad.reshape(prec_here), state_grad, nation_grad, beta_grad.reshape(p_size)


def solution(mesh):
    placed = (
        P(("grp", "row"), None),
        P(("grp", "row")),
        P(("grp", "row")),
        P("grp", "row"),
        P(),
        P(),
        P(),
        P("grp", None),
        P("grp"),
        P("grp"),
        P(),
        P(),
    )
    return jax.shard_map(
        on_device,
        mesh=mesh,
        in_specs=placed,
        out_specs=(P(("grp", "row"), None), P("grp"), P(), P(), P()),
        check_vma=False,
    )
```

```python
import functools

import jax
import jax.numpy as jnp
from jax import lax
from jax.experimental import pallas as pl
from jax.experimental.pallas import tpu as pltpu
from jax.sharding import PartitionSpec as P

LANES = 128
ROW_STEP = 1024
SMALL = 10
VMEM_LIMIT = 60 * 1024 * 1024
END_LIMIT = 16 * 1024 * 1024
F32 = jnp.float32
BF16 = jnp.bfloat16


def split3(x):
    a = x.astype(BF16)
    r = x - a.astype(F32)
    b = r.astype(BF16)
    c = (r - b.astype(F32)).astype(BF16)
    return a, b, c


def hot_dot(hot, x, dims):
    out = None
    for part in reversed(split3(x)):
        term = lax.dot_general(hot, part, (dims, ((), ())), preferred_element_type=F32)
        out = term if out is None else out + term
    return out


def iota_rows(n):
    return lax.broadcasted_iota(jnp.int32, (n, 1), 0)


def pick(values, low, high_hot):
    found = []
    for at in range(0, low.shape[1], LANES):
        index = jnp.broadcast_to(low[:, at : at + LANES], values.shape)
        found.append(jnp.take_along_axis(values, index, axis=1, mode="promise_in_bounds"))
    return jnp.sum(
        jnp.where(high_hot, jnp.concatenate(found, axis=1), jnp.zeros((), values.dtype)),
        axis=0,
        keepdims=True,
    )


def main_kernel(n_out, count_ref, features_ref, *args):
    small = args[:SMALL]
    out_refs = args[SMALL : SMALL + n_out]
    held = args[SMALL + n_out : 2 * SMALL + n_out]
    feats, table, s0, s1, h0, h1, b0, b1, r0, r1, w0, w1, county_acc, prec_acc, state_acc, *outs, small_sems, sems, out_sems = (
        args[2 * SMALL + n_out :]
    )
    (
        state_nation_ref,
        nation_ref,
        state_ref,
        county_state_ref,
        county_ref,
        beta_ref,
        precinct_ref,
        prec_ref,
        map_ref,
        outcome_ref,
    ) = held
    scores, hot_rows, bases, residuals, weights = (s0, s1), (h0, h1), (b0, b1), (r0, r1), (w0, w1)
    n_row = len(outs) // 2
    state_outs, county_outs = outs[:n_row], outs[n_row:]
    n_states = state_ref.shape[0]
    n_nations = nation_ref.shape[0]
    n_cnt, p_size = county_ref.shape
    n_hi = prec_ref.shape[0]
    chunks = precinct_ref.shape[0]
    size = precinct_ref.shape[2]

    def fetch(j):
        rows = pl.ds(pl.multiple_of(j * size, size), size)
        return pltpu.make_async_copy(features_ref.at[rows], feats.at[rows], sems.at[j])

    small_copies = [
        pltpu.make_async_copy(source, target, small_sems.at[k])
        for k, (source, target) in enumerate(zip(small, held))
    ]
    for copy in small_copies:
        copy.start()
    for j in range(2):
        fetch(j).start()
    for copy in small_copies:
        copy.wait()
    for j in range(2, 4):
        fetch(j).start()

    states = county_state_ref[lax.axis_index("grp")]
    state_hot = (iota_rows(n_states) == states).astype(F32).astype(BF16)
    nation_hot = (iota_rows(n_nations) == state_nation_ref[...]).astype(F32).astype(BF16)
    upper = state_ref[...] + hot_dot(nation_hot, nation_ref[...], ((0,), (0,)))
    table[...] = (county_ref[...] + hot_dot(state_hot, upper, ((0,), (0,))) + beta_ref[...]).astype(BF16)
    county_acc[...] = jnp.zeros_like(county_acc)
    prec_acc[...] = jnp.zeros_like(prec_acc)

    def block(j):
        return feats[pl.ds(pl.multiple_of(j * size, size), size), :]

    def parts_of(j):
        prec = precinct_ref[j]
        return jnp.bitwise_and(prec, LANES - 1), iota_rows(n_hi) == jnp.right_shift(prec, 7)

    def score(j, k):
        low, high_hot = parts_of(j)
        bases[k][...] = pick(prec_ref[...], low, high_hot)
        hot_rows[k][...] = pick(map_ref[...], low, high_hot)
        scores[k][...] = lax.dot_general(
            table[...], block(j), (((1,), (1,)), ((), ())), preferred_element_type=F32
        )

    def residue(j, k):
        county_hot = iota_rows(n_cnt) == hot_rows[k][...]
        linear = jnp.sum(jnp.where(county_hot, scores[k][...], 0.0), axis=0, keepdims=True)
        linear = linear + bases[k][...]
        row = j * size + lax.broadcasted_iota(jnp.int32, (1, size), 1)
        count = outcome_ref[j].astype(F32)
        residual = jnp.where(row < count_ref[0], count - jnp.exp(linear), 0.0)
        residuals[k][...] = residual
        rounded = residual.astype(BF16).astype(F32)
        weights[k][...] = jnp.where(county_hot, rounded, 0.0).astype(BF16)

    def collect(j, k):
        county_acc[...] += jnp.dot(weights[k][...], block(j), preferred_element_type=F32)
        low, high_hot = parts_of(j)
        low_hot = (iota_rows(LANES) == low).astype(F32).astype(BF16)
        by_high = jnp.concatenate(
            [jnp.where(high_hot, x.astype(F32), 0.0) for x in split3(residuals[k][...])[:2]], axis=0
        ).astype(BF16)
        prec_acc[...] += lax.dot_general(
            by_high, low_hot, (((1,), (1,)), ((), ())), preferred_element_type=F32
        )

    fetch(0).wait()
    score(0, 0)
    fetch(1).wait()
    score(1, 1)
    residue(0, 0)

    def body(t, carry):
        j = 2 * t
        fetch(j).wait()
        fetch(j + 1).wait()

        @pl.when(j + 2 < chunks)
        def _():
            fetch(j + 2).start()
            fetch(j + 3).start()

        residue(j - 1, 1)
        score(j, 0)
        collect(j - 2, 0)
        residue(j, 0)
        score(j + 1, 1)
        collect(j - 1, 1)
        return carry

    lax.fori_loop(1, chunks // 2, body, 0)
    residue(chunks - 1, 1)
    collect(chunks - 2, 0)
    collect(chunks - 1, 1)

    me = lax.axis_index("row")
    share = n_cnt // n_row
    per = n_states // n_row
    prec_sum = prec_acc[:n_hi] + prec_acc[n_hi:]
    own_rows = pl.ds(pl.multiple_of(me * share, share), share)

    def send(k):
        copy = pltpu.make_async_copy(outs[k], out_refs[k], out_sems.at[k])
        copy.start()
        return copy

    copies = []
    for d in range(n_row):
        peer = jnp.bitwise_xor(me, d)
        sums = county_acc[pl.ds(pl.multiple_of(peer * share, share), share), :]
        county_outs[d][:share, :] = sums if d else sums - county_ref[own_rows, :]
        county_outs[d][share:, :LANES] = prec_sum if d else prec_sum - prec_ref[...]
        county_outs[d][share:, LANES:] = jnp.zeros((n_hi, p_size - LANES), F32)
        copies.append(send(n_row + d))
    state_acc[...] = hot_dot(state_hot, county_acc[...], ((1,), (0,)))
    for d in range(n_row):
        peer = jnp.bitwise_xor(me, d)
        state_outs[d][...] = state_acc[pl.ds(pl.multiple_of(peer * per, per), per), :]
        copies.append(send(d))
    for copy in copies:
        copy.wait()


def county_end_kernel(state_nation_ref, state_ref, nation_ref, beta_ref, *refs):
    *parts, county_out, prec_out, prior_out, hot_out = refs
    share = county_out.shape[0]
    n_states = state_ref.shape[0]
    n_nations = nation_ref.shape[0]
    prior_out[:n_states, :] = state_ref[...]
    prior_out[n_states : n_states + n_nations, :] = nation_ref[...]
    prior_out[n_states + n_nations :, :] = beta_ref[...]
    hot_out[...] = (iota_rows(n_nations) == state_nation_ref[...]).astype(F32)
    county_out[...] = total_of([part[:share, :] for part in parts])
    prec_out[...] = total_of([part[share:, :LANES] for part in parts])


def end_kernel(prior_ref, hot_ref, *refs):
    *gathered, state_out, nation_out, beta_out, total = refs
    me = lax.axis_index("row")
    per = gathered[0].shape[0]
    n_states = state_out.shape[0]
    n_nations = nation_out.shape[0]
    for d, part in enumerate(gathered):
        peer = jnp.bitwise_xor(me, d)
        total[pl.ds(pl.multiple_of(peer * per, per), per), :] = part[...]
    sums = total[...]
    nation_total = hot_dot(hot_ref[...].astype(BF16), sums, ((1,), (0,)))
    state_out[...] = sums - prior_ref[:n_states, :]
    nation_out[...] = nation_total - prior_ref[n_states : n_states + n_nations, :]
    beta_out[...] = jnp.sum(nation_total, axis=0, keepdims=True) - prior_ref[n_states + n_nations :, :]


def swap(x, axis, d):
    n = lax.axis_size(axis)
    return lax.ppermute(x, axis, [(i, i ^ d) for i in range(n)])


def gather_by(x, axis, distances):
    return [x] + [swap(x, axis, d) for d in distances]


def total_of(parts):
    while len(parts) > 1:
        parts = [sum(parts[i : i + 2][1:], parts[i]) for i in range(0, len(parts), 2)]
    return parts[0]


def on_device(
    features,
    precinct,
    outcome,
    row_counts,
    beta,
    nation_coef,
    state_coef,
    county_coef,
    precinct_coef,
    precinct_county,
    county_state,
    state_nation,
):
    rows_here, p_size = features.shape
    cnt_here = county_coef.shape[0]
    prec_here = precinct_coef.shape[0]
    n_states = state_coef.shape[0]
    n_row = lax.axis_size("row")
    n_grp = lax.axis_size("grp")
    share = cnt_here // n_row
    n_hi = prec_here // LANES
    steps = rows_here // ROW_STEP
    per = n_states // n_row

    precinct3 = precinct.reshape(steps, 1, ROW_STEP)
    outcome3 = outcome.reshape(steps, 1, ROW_STEP)
    states3 = county_state.reshape(n_grp, 1, cnt_here)
    prec2 = precinct_coef.reshape(n_hi, LANES)
    map2 = precinct_county.reshape(n_hi, LANES)
    beta2 = beta.reshape(1, p_size)
    nation_row = state_nation.reshape(1, n_states)

    n_nations = nation_coef.shape[0]
    small = (
        nation_row,
        nation_coef,
        state_coef,
        states3,
        county_coef,
        beta2,
        precinct3,
        prec2,
        map2,
        outcome3,
    )
    outs = pl.pallas_call(
        functools.partial(main_kernel, 2 * n_row),
        in_specs=[pl.BlockSpec(memory_space=pltpu.VMEM)]
        + [pl.BlockSpec(memory_space=pltpu.HBM)] * (SMALL + 1),
        out_specs=[pl.BlockSpec(memory_space=pltpu.HBM)] * (2 * n_row),
        out_shape=[jax.ShapeDtypeStruct((per, p_size), F32)] * n_row
        + [jax.ShapeDtypeStruct((share + n_hi, p_size), F32)] * n_row,
        scratch_shapes=[pltpu.VMEM(x.shape, x.dtype) for x in small]
        + [
            pltpu.VMEM((rows_here, p_size), BF16),
            pltpu.VMEM((cnt_here, p_size), BF16),
            pltpu.VMEM((cnt_here, ROW_STEP), F32),
            pltpu.VMEM((cnt_here, ROW_STEP), F32),
            pltpu.VMEM((1, ROW_STEP), jnp.int32),
            pltpu.VMEM((1, ROW_STEP), jnp.int32),
            pltpu.VMEM((1, ROW_STEP), F32),
            pltpu.VMEM((1, ROW_STEP), F32),
            pltpu.VMEM((1, ROW_STEP), F32),
            pltpu.VMEM((1, ROW_STEP), F32),
            pltpu.VMEM((cnt_here, ROW_STEP), BF16),
            pltpu.VMEM((cnt_here, ROW_STEP), BF16),
            pltpu.VMEM((cnt_here, p_size), F32),
            pltpu.VMEM((2 * n_hi, LANES), F32),
            pltpu.VMEM(state_coef.shape, F32),
        ]
        + [pltpu.VMEM((per, p_size), F32)] * n_row
        + [pltpu.VMEM((share + n_hi, p_size), F32)] * n_row
        + [
            pltpu.SemaphoreType.DMA((SMALL,)),
            pltpu.SemaphoreType.DMA((steps,)),
            pltpu.SemaphoreType.DMA((2 * n_row,)),
        ],
        compiler_params=pltpu.CompilerParams(vmem_limit_bytes=VMEM_LIMIT),
        name="local_sums",
    )(row_counts.reshape(1, 1, 1), features, *small)

    near = 1 << (n_grp.bit_length() // 2 - 1)
    state_parts = [outs[0]] + [swap(outs[d], "row", d) for d in range(1, n_row)]
    state_piece = total_of(state_parts)
    county_parts = [outs[n_row]] + [swap(outs[n_row + d], "row", d) for d in range(1, n_row)]
    state_piece = total_of(gather_by(state_piece, "grp", range(1, near)))
    state_piece, *county_parts = lax.optimization_barrier((state_piece, *county_parts))
    county_grad, precinct_grad, prior, nation_hot = pl.pallas_call(
        county_end_kernel,
        out_shape=[
            jax.ShapeDtypeStruct((share, p_size), F32),
            jax.ShapeDtypeStruct((n_hi, LANES), F32),
            jax.ShapeDtypeStruct((n_states + n_nations + 1, p_size), F32),
            jax.ShapeDtypeStruct((n_nations, n_states), F32),
        ],
        compiler_params=pltpu.CompilerParams(vmem_limit_bytes=END_LIMIT),
        name="county_totals",
    )(nation_row, state_coef, nation_coef, beta2, *county_parts)

    state_piece = total_of(gather_by(state_piece, "grp", range(near, n_grp, near)))
    gathered = gather_by(state_piece, "row", range(1, n_row))
    state_grad, nation_grad, beta_grad = pl.pallas_call(
        end_kernel,
        out_shape=[
            jax.ShapeDtypeStruct(state_coef.shape, F32),
            jax.ShapeDtypeStruct(nation_coef.shape, F32),
            jax.ShapeDtypeStruct((1, p_size), F32),
        ],
        scratch_shapes=[pltpu.VMEM(state_coef.shape, F32)],
        compiler_params=pltpu.CompilerParams(vmem_limit_bytes=END_LIMIT),
        name="upper_totals",
    )(prior, nation_hot, *gathered)
    return county_grad, precinct_grad.reshape(prec_here), state_grad, nation_grad, beta_grad.reshape(p_size)


def solution(mesh):
    placed = (
        P(("grp", "row"), None),
        P(("grp", "row")),
        P(("grp", "row")),
        P("grp", "row"),
        P(),
        P(),
        P(),
        P("grp", None),
        P("grp"),
        P("grp"),
        P(),
        P(),
    )
    return jax.shard_map(
        on_device,
        mesh=mesh,
        in_specs=placed,
        out_specs=(P(("grp", "row"), None), P("grp"), P(), P(), P()),
        check_vma=False,
    )
```

```python
import functools

import jax
import jax.numpy as jnp
from jax import lax
from jax.experimental import pallas as pl
from jax.experimental.pallas import tpu as pltpu
from jax.sharding import PartitionSpec as P

LANES = 128
ROW_STEP = 512
SMALL = 10
VMEM_LIMIT = 60 * 1024 * 1024
END_LIMIT = 16 * 1024 * 1024
F32 = jnp.float32
BF16 = jnp.bfloat16


def split3(x):
    a = x.astype(BF16)
    r = x - a.astype(F32)
    b = r.astype(BF16)
    c = (r - b.astype(F32)).astype(BF16)
    return a, b, c


def hot_dot(hot, x, dims):
    out = None
    for part in reversed(split3(x)):
        term = lax.dot_general(hot, part, (dims, ((), ())), preferred_element_type=F32)
        out = term if out is None else out + term
    return out


def iota_rows(n):
    return lax.broadcasted_iota(jnp.int32, (n, 1), 0)


def small_hot(n, ids, value):
    rows = lax.broadcasted_iota(jnp.int32, (n, ids.shape[1]), 0).astype(F32).astype(BF16)
    return jnp.where(rows == ids.astype(F32).astype(BF16), value.astype(BF16), jnp.zeros((), BF16))


def pick(values, low, high_hot):
    found = []
    for at in range(0, low.shape[1], LANES):
        index = jnp.broadcast_to(low[:, at : at + LANES], values.shape)
        found.append(jnp.take_along_axis(values, index, axis=1, mode="promise_in_bounds"))
    return jnp.sum(
        jnp.where(high_hot, jnp.concatenate(found, axis=1), jnp.zeros((), values.dtype)),
        axis=0,
        keepdims=True,
    )


def main_kernel(n_out, count_ref, features_ref, *args):
    small = args[:SMALL]
    out_refs = args[SMALL : SMALL + n_out]
    held = args[SMALL + n_out : 2 * SMALL + n_out]
    feats, table, s0, s1, h0, h1, b0, b1, r0, r1, w0, w1, county_acc, prec_acc, state_acc, *outs, small_sems, sems, out_sems = (
        args[2 * SMALL + n_out :]
    )
    (
        state_nation_ref,
        nation_ref,
        state_ref,
        county_state_ref,
        county_ref,
        beta_ref,
        precinct_ref,
        prec_ref,
        map_ref,
        outcome_ref,
    ) = held
    scores, hot_rows, bases, residuals, weights = (s0, s1), (h0, h1), (b0, b1), (r0, r1), (w0, w1)
    n_row = len(outs) // 2
    state_outs, county_outs = outs[:n_row], outs[n_row:]
    n_states = state_ref.shape[0]
    n_nations = nation_ref.shape[0]
    n_cnt, p_size = county_ref.shape
    n_hi = prec_ref.shape[0]
    chunks = precinct_ref.shape[0]
    size = precinct_ref.shape[2]

    def fetch(j):
        rows = pl.ds(pl.multiple_of(j * size, size), size)
        return pltpu.make_async_copy(features_ref.at[rows], feats.at[rows], sems.at[j])

    small_copies = [
        pltpu.make_async_copy(source, target, small_sems.at[k])
        for k, (source, target) in enumerate(zip(small, held))
    ]
    for copy in small_copies:
        copy.start()
    for j in range(2):
        fetch(j).start()
    for copy in small_copies:
        copy.wait()
    for j in range(2, 4):
        fetch(j).start()

    states = county_state_ref[lax.axis_index("grp")]
    state_hot = (iota_rows(n_states) == states).astype(F32).astype(BF16)
    nation_hot = (iota_rows(n_nations) == state_nation_ref[...]).astype(F32).astype(BF16)
    upper = state_ref[...] + hot_dot(nation_hot, nation_ref[...], ((0,), (0,)))
    table[...] = (county_ref[...] + hot_dot(state_hot, upper, ((0,), (0,))) + beta_ref[...]).astype(BF16)
    county_acc[...] = jnp.zeros_like(county_acc)
    prec_acc[...] = jnp.zeros_like(prec_acc)

    def block(j):
        return feats[pl.ds(pl.multiple_of(j * size, size), size), :]

    def parts_of(j):
        prec = precinct_ref[j]
        return jnp.bitwise_and(prec, LANES - 1), iota_rows(n_hi) == jnp.right_shift(prec, 7)

    def score(j, k):
        low, high_hot = parts_of(j)
        bases[k][...] = pick(prec_ref[...], low, high_hot)
        hot_rows[k][...] = pick(map_ref[...], low, high_hot)
        scores[k][...] = lax.dot_general(
            table[...], block(j), (((1,), (1,)), ((), ())), preferred_element_type=F32
        )

    def residue(j, k):
        county_hot = iota_rows(n_cnt) == hot_rows[k][...]
        linear = jnp.sum(jnp.where(county_hot, scores[k][...], 0.0), axis=0, keepdims=True)
        linear = linear + bases[k][...]
        row = j * size + lax.broadcasted_iota(jnp.int32, (1, size), 1)
        count = outcome_ref[j].astype(F32)
        residual = jnp.where(row < count_ref[0], count - jnp.exp(linear), 0.0)
        residuals[k][...] = residual
        weights[k][...] = small_hot(n_cnt, hot_rows[k][...], residual)

    def collect(j, k):
        county_acc[...] += jnp.dot(weights[k][...], block(j), preferred_element_type=F32)
        low, high_hot = parts_of(j)
        low_hot = small_hot(LANES, low, jnp.ones((), F32))
        by_high = jnp.concatenate(
            [jnp.where(high_hot, x.astype(F32), 0.0) for x in split3(residuals[k][...])[:2]], axis=0
        ).astype(BF16)
        prec_acc[...] += lax.dot_general(
            by_high, low_hot, (((1,), (1,)), ((), ())), preferred_element_type=F32
        )

    fetch(0).wait()
    score(0, 0)
    fetch(1).wait()
    score(1, 1)
    residue(0, 0)

    def body(t, carry):
        j = 2 * t
        fetch(j).wait()
        fetch(j + 1).wait()

        @pl.when(j + 2 < chunks)
        def _():
            fetch(j + 2).start()
            fetch(j + 3).start()

        residue(j - 1, 1)
        score(j, 0)
        collect(j - 2, 0)
        residue(j, 0)
        score(j + 1, 1)
        collect(j - 1, 1)
        return carry

    lax.fori_loop(1, chunks // 2, body, 0)
    residue(chunks - 1, 1)
    collect(chunks - 2, 0)
    collect(chunks - 1, 1)

    me = lax.axis_index("row")
    share = n_cnt // n_row
    per = n_states // n_row
    prec_sum = prec_acc[:n_hi] + prec_acc[n_hi:]
    own_rows = pl.ds(pl.multiple_of(me * share, share), share)

    def send(k):
        copy = pltpu.make_async_copy(outs[k], out_refs[k], out_sems.at[k])
        copy.start()
        return copy

    copies = []
    for d in range(n_row):
        peer = jnp.bitwise_xor(me, d)
        sums = county_acc[pl.ds(pl.multiple_of(peer * share, share), share), :]
        county_outs[d][:share, :] = sums if d else sums - county_ref[own_rows, :]
        county_outs[d][share:, :LANES] = prec_sum if d else prec_sum - prec_ref[...]
        county_outs[d][share:, LANES:] = jnp.zeros((n_hi, p_size - LANES), F32)
        copies.append(send(n_row + d))
    state_acc[...] = hot_dot(state_hot, county_acc[...], ((1,), (0,)))
    for d in range(n_row):
        peer = jnp.bitwise_xor(me, d)
        state_outs[d][...] = state_acc[pl.ds(pl.multiple_of(peer * per, per), per), :]
        copies.append(send(d))
    for copy in copies:
        copy.wait()


def county_end_kernel(state_nation_ref, state_ref, nation_ref, beta_ref, *refs):
    *parts, county_out, prec_out, prior_out, hot_out = refs
    share = county_out.shape[0]
    n_states = state_ref.shape[0]
    n_nations = nation_ref.shape[0]
    prior_out[:n_states, :] = state_ref[...]
    prior_out[n_states : n_states + n_nations, :] = nation_ref[...]
    prior_out[n_states + n_nations :, :] = beta_ref[...]
    hot_out[...] = (iota_rows(n_nations) == state_nation_ref[...]).astype(F32)
    county_out[...] = total_of([part[:share, :] for part in parts])
    prec_out[...] = total_of([part[share:, :LANES] for part in parts])


def end_kernel(prior_ref, hot_ref, *refs):
    *gathered, state_out, nation_out, beta_out, total = refs
    me = lax.axis_index("row")
    per = gathered[0].shape[0]
    n_states = state_out.shape[0]
    n_nations = nation_out.shape[0]
    for d, part in enumerate(gathered):
        peer = jnp.bitwise_xor(me, d)
        total[pl.ds(pl.multiple_of(peer * per, per), per), :] = part[...]
    sums = total[...]
    nation_total = hot_dot(hot_ref[...].astype(BF16), sums, ((1,), (0,)))
    state_out[...] = sums - prior_ref[:n_states, :]
    nation_out[...] = nation_total - prior_ref[n_states : n_states + n_nations, :]
    beta_out[...] = jnp.sum(nation_total, axis=0, keepdims=True) - prior_ref[n_states + n_nations :, :]


def swap(x, axis, d):
    n = lax.axis_size(axis)
    return lax.ppermute(x, axis, [(i, i ^ d) for i in range(n)])


def gather_by(x, axis, distances):
    return [x] + [swap(x, axis, d) for d in distances]


def total_of(parts):
    while len(parts) > 1:
        parts = [sum(parts[i : i + 2][1:], parts[i]) for i in range(0, len(parts), 2)]
    return parts[0]


def on_device(
    features,
    precinct,
    outcome,
    row_counts,
    beta,
    nation_coef,
    state_coef,
    county_coef,
    precinct_coef,
    precinct_county,
    county_state,
    state_nation,
):
    rows_here, p_size = features.shape
    cnt_here = county_coef.shape[0]
    prec_here = precinct_coef.shape[0]
    n_states = state_coef.shape[0]
    n_row = lax.axis_size("row")
    n_grp = lax.axis_size("grp")
    share = cnt_here // n_row
    n_hi = prec_here // LANES
    steps = rows_here // ROW_STEP
    per = n_states // n_row

    precinct3 = precinct.reshape(steps, 1, ROW_STEP)
    outcome3 = outcome.reshape(steps, 1, ROW_STEP)
    states3 = county_state.reshape(n_grp, 1, cnt_here)
    prec2 = precinct_coef.reshape(n_hi, LANES)
    map2 = precinct_county.reshape(n_hi, LANES)
    beta2 = beta.reshape(1, p_size)
    nation_row = state_nation.reshape(1, n_states)

    n_nations = nation_coef.shape[0]
    small = (
        nation_row,
        nation_coef,
        state_coef,
        states3,
        county_coef,
        beta2,
        precinct3,
        prec2,
        map2,
        outcome3,
    )
    outs = pl.pallas_call(
        functools.partial(main_kernel, 2 * n_row),
        in_specs=[pl.BlockSpec(memory_space=pltpu.VMEM)]
        + [pl.BlockSpec(memory_space=pltpu.HBM)] * (SMALL + 1),
        out_specs=[pl.BlockSpec(memory_space=pltpu.HBM)] * (2 * n_row),
        out_shape=[jax.ShapeDtypeStruct((per, p_size), F32)] * n_row
        + [jax.ShapeDtypeStruct((share + n_hi, p_size), F32)] * n_row,
        scratch_shapes=[pltpu.VMEM(x.shape, x.dtype) for x in small]
        + [
            pltpu.VMEM((rows_here, p_size), BF16),
            pltpu.VMEM((cnt_here, p_size), BF16),
            pltpu.VMEM((cnt_here, ROW_STEP), F32),
            pltpu.VMEM((cnt_here, ROW_STEP), F32),
            pltpu.VMEM((1, ROW_STEP), jnp.int32),
            pltpu.VMEM((1, ROW_STEP), jnp.int32),
            pltpu.VMEM((1, ROW_STEP), F32),
            pltpu.VMEM((1, ROW_STEP), F32),
            pltpu.VMEM((1, ROW_STEP), F32),
            pltpu.VMEM((1, ROW_STEP), F32),
            pltpu.VMEM((cnt_here, ROW_STEP), BF16),
            pltpu.VMEM((cnt_here, ROW_STEP), BF16),
            pltpu.VMEM((cnt_here, p_size), F32),
            pltpu.VMEM((2 * n_hi, LANES), F32),
            pltpu.VMEM(state_coef.shape, F32),
        ]
        + [pltpu.VMEM((per, p_size), F32)] * n_row
        + [pltpu.VMEM((share + n_hi, p_size), F32)] * n_row
        + [
            pltpu.SemaphoreType.DMA((SMALL,)),
            pltpu.SemaphoreType.DMA((steps,)),
            pltpu.SemaphoreType.DMA((2 * n_row,)),
        ],
        compiler_params=pltpu.CompilerParams(vmem_limit_bytes=VMEM_LIMIT),
        name="local_sums",
    )(row_counts.reshape(1, 1, 1), features, *small)

    near = 1 << (n_grp.bit_length() // 2 - 1)
    state_parts = [outs[0]] + [swap(outs[d], "row", d) for d in range(1, n_row)]
    state_piece = total_of(state_parts)
    county_outs = outs[n_row:]
    from_core = [swap(county_outs[d ^ 1], "row", 1) for d in range(0, n_row, 2)]
    state_piece, *from_core = lax.optimization_barrier((state_piece, *from_core))
    chip_sums = [county_outs[d] + from_core[d // 2] for d in range(2, n_row, 2)]
    county_parts = [county_outs[0], from_core[0]] + [
        swap(x, "row", d) for x, d in zip(chip_sums, range(2, n_row, 2))
    ]
    state_piece = total_of(gather_by(state_piece, "grp", range(1, near)))
    county_grad, precinct_grad, prior, nation_hot = pl.pallas_call(
        county_end_kernel,
        out_shape=[
            jax.ShapeDtypeStruct((share, p_size), F32),
            jax.ShapeDtypeStruct((n_hi, LANES), F32),
            jax.ShapeDtypeStruct((n_states + n_nations + 1, p_size), F32),
            jax.ShapeDtypeStruct((n_nations, n_states), F32),
        ],
        compiler_params=pltpu.CompilerParams(vmem_limit_bytes=END_LIMIT),
        name="county_totals",
    )(nation_row, state_coef, nation_coef, beta2, *county_parts)

    state_piece = total_of(gather_by(state_piece, "grp", range(near, n_grp, near)))
    gathered = gather_by(state_piece, "row", range(1, n_row))
    state_grad, nation_grad, beta_grad = pl.pallas_call(
        end_kernel,
        out_shape=[
            jax.ShapeDtypeStruct(state_coef.shape, F32),
            jax.ShapeDtypeStruct(nation_coef.shape, F32),
            jax.ShapeDtypeStruct((1, p_size), F32),
        ],
        scratch_shapes=[pltpu.VMEM(state_coef.shape, F32)],
        compiler_params=pltpu.CompilerParams(vmem_limit_bytes=END_LIMIT),
        name="upper_totals",
    )(prior, nation_hot, *gathered)
    return county_grad, precinct_grad.reshape(prec_here), state_grad, nation_grad, beta_grad.reshape(p_size)


def solution(mesh):
    placed = (
        P(("grp", "row"), None),
        P(("grp", "row")),
        P(("grp", "row")),
        P("grp", "row"),
        P(),
        P(),
        P(),
        P("grp", None),
        P("grp"),
        P("grp"),
        P(),
        P(),
    )
    return jax.shard_map(
        on_device,
        mesh=mesh,
        in_specs=placed,
        out_specs=(P(("grp", "row"), None), P("grp"), P(), P(), P()),
        check_vma=False,
    )
```

```python
import functools

import jax
import jax.numpy as jnp
from jax import lax
from jax.experimental import pallas as pl
from jax.experimental.pallas import tpu as pltpu
from jax.sharding import PartitionSpec as P

LANES = 128
ROW_STEP = 1024
SMALL = 10
VMEM_LIMIT = 60 * 1024 * 1024
END_LIMIT = 16 * 1024 * 1024
F32 = jnp.float32
BF16 = jnp.bfloat16


def split3(x):
    a = x.astype(BF16)
    r = x - a.astype(F32)
    b = r.astype(BF16)
    c = (r - b.astype(F32)).astype(BF16)
    return a, b, c


def hot_dot(hot, x, dims):
    out = None
    for part in reversed(split3(x)):
        term = lax.dot_general(hot, part, (dims, ((), ())), preferred_element_type=F32)
        out = term if out is None else out + term
    return out


def iota_rows(n):
    return lax.broadcasted_iota(jnp.int32, (n, 1), 0)


def pick(values, low, high_hot):
    found = []
    for at in range(0, low.shape[1], LANES):
        index = jnp.broadcast_to(low[:, at : at + LANES], values.shape)
        found.append(jnp.take_along_axis(values, index, axis=1, mode="promise_in_bounds"))
    return jnp.sum(
        jnp.where(high_hot, jnp.concatenate(found, axis=1), jnp.zeros((), values.dtype)),
        axis=0,
        keepdims=True,
    )


def main_kernel(n_out, count_ref, features_ref, *args):
    small = args[:SMALL]
    out_refs = args[SMALL : SMALL + n_out]
    held = args[SMALL + n_out : 2 * SMALL + n_out]
    feats, table, s0, s1, h0, h1, b0, b1, r0, r1, w0, w1, county_acc, prec_acc, state_acc, *outs, small_sems, sems, out_sems = (
        args[2 * SMALL + n_out :]
    )
    (
        state_nation_ref,
        nation_ref,
        state_ref,
        county_state_ref,
        county_ref,
        beta_ref,
        precinct_ref,
        prec_ref,
        map_ref,
        outcome_ref,
    ) = held
    scores, hot_rows, bases, residuals, weights = (s0, s1), (h0, h1), (b0, b1), (r0, r1), (w0, w1)
    n_row = len(outs) // 2
    state_outs, county_outs = outs[:n_row], outs[n_row:]
    n_states = state_ref.shape[0]
    n_nations = nation_ref.shape[0]
    n_cnt, p_size = county_ref.shape
    n_hi = prec_ref.shape[0]
    chunks = precinct_ref.shape[0]
    size = precinct_ref.shape[2]

    def fetch(j):
        rows = pl.ds(pl.multiple_of(j * size, size), size)
        return pltpu.make_async_copy(features_ref.at[rows], feats.at[rows], sems.at[j])

    small_copies = [
        pltpu.make_async_copy(source, target, small_sems.at[k])
        for k, (source, target) in enumerate(zip(small, held))
    ]
    for copy in small_copies:
        copy.start()
    for j in range(2):
        fetch(j).start()
    for copy in small_copies:
        copy.wait()
    for j in range(2, 4):
        fetch(j).start()

    states = county_state_ref[lax.axis_index("grp")]
    state_hot = (iota_rows(n_states) == states).astype(F32).astype(BF16)
    nation_hot = (iota_rows(n_nations) == state_nation_ref[...]).astype(F32).astype(BF16)
    upper = state_ref[...] + hot_dot(nation_hot, nation_ref[...], ((0,), (0,)))
    table[...] = (county_ref[...] + hot_dot(state_hot, upper, ((0,), (0,))) + beta_ref[...]).astype(BF16)
    county_acc[...] = jnp.zeros_like(county_acc)
    prec_acc[...] = jnp.zeros_like(prec_acc)

    def block(j):
        return feats[pl.ds(pl.multiple_of(j * size, size), size), :]

    def parts_of(j):
        prec = precinct_ref[j]
        return jnp.bitwise_and(prec, LANES - 1), iota_rows(n_hi) == jnp.right_shift(prec, 7)

    def score(j, k):
        low, high_hot = parts_of(j)
        bases[k][...] = pick(prec_ref[...], low, high_hot)
        hot_rows[k][...] = pick(map_ref[...], low, high_hot)
        scores[k][...] = lax.dot_general(
            block(j), table[...], (((1,), (1,)), ((), ())), preferred_element_type=F32
        ).T

    def residue(j, k):
        county_hot = iota_rows(n_cnt) == hot_rows[k][...]
        linear = jnp.sum(jnp.where(county_hot, scores[k][...], 0.0), axis=0, keepdims=True)
        linear = linear + bases[k][...]
        row = j * size + lax.broadcasted_iota(jnp.int32, (1, size), 1)
        count = outcome_ref[j].astype(F32)
        residual = jnp.where(row < count_ref[0], count - jnp.exp(linear), 0.0)
        residuals[k][...] = residual
        rounded = residual.astype(BF16).astype(F32)
        weights[k][...] = jnp.where(county_hot, rounded, 0.0).astype(BF16)

    def collect(j, k):
        county_acc[...] += jnp.dot(weights[k][...], block(j), preferred_element_type=F32)
        low, high_hot = parts_of(j)
        low_hot = (iota_rows(LANES) == low).astype(F32).astype(BF16)
        by_high = jnp.concatenate(
            [jnp.where(high_hot, x.astype(F32), 0.0) for x in split3(residuals[k][...])[:2]], axis=0
        ).astype(BF16)
        prec_acc[...] += lax.dot_general(
            by_high, low_hot, (((1,), (1,)), ((), ())), preferred_element_type=F32
        )

    fetch(0).wait()
    score(0, 0)
    fetch(1).wait()
    score(1, 1)
    residue(0, 0)

    def body(t, carry):
        j = 2 * t
        fetch(j).wait()
        fetch(j + 1).wait()

        @pl.when(j + 2 < chunks)
        def _():
            fetch(j + 2).start()
            fetch(j + 3).start()

        residue(j - 1, 1)
        score(j, 0)
        collect(j - 2, 0)
        residue(j, 0)
        score(j + 1, 1)
        collect(j - 1, 1)
        return carry

    lax.fori_loop(1, chunks // 2, body, 0)
    residue(chunks - 1, 1)
    collect(chunks - 2, 0)
    collect(chunks - 1, 1)

    me = lax.axis_index("row")
    share = n_cnt // n_row
    per = n_states // n_row
    prec_sum = prec_acc[:n_hi] + prec_acc[n_hi:]
    own_rows = pl.ds(pl.multiple_of(me * share, share), share)

    def send(k):
        copy = pltpu.make_async_copy(outs[k], out_refs[k], out_sems.at[k])
        copy.start()
        return copy

    copies = []
    for d in range(n_row):
        peer = jnp.bitwise_xor(me, d)
        sums = county_acc[pl.ds(pl.multiple_of(peer * share, share), share), :]
        county_outs[d][:share, :] = sums if d else sums - county_ref[own_rows, :]
        county_outs[d][share:, :LANES] = prec_sum if d else prec_sum - prec_ref[...]
        county_outs[d][share:, LANES:] = jnp.zeros((n_hi, p_size - LANES), F32)
        copies.append(send(n_row + d))
    state_acc[...] = hot_dot(state_hot, county_acc[...], ((1,), (0,)))
    for d in range(n_row):
        peer = jnp.bitwise_xor(me, d)
        state_outs[d][...] = state_acc[pl.ds(pl.multiple_of(peer * per, per), per), :]
        copies.append(send(d))
    for copy in copies:
        copy.wait()


def county_end_kernel(state_nation_ref, state_ref, nation_ref, beta_ref, *refs):
    *parts, county_out, prec_out, prior_out, hot_out = refs
    share = county_out.shape[0]
    n_states = state_ref.shape[0]
    n_nations = nation_ref.shape[0]
    prior_out[:n_states, :] = state_ref[...]
    prior_out[n_states : n_states + n_nations, :] = nation_ref[...]
    prior_out[n_states + n_nations :, :] = beta_ref[...]
    hot_out[...] = (iota_rows(n_nations) == state_nation_ref[...]).astype(F32)
    county_out[...] = total_of([part[:share, :] for part in parts])
    prec_out[...] = total_of([part[share:, :LANES] for part in parts])


def end_kernel(prior_ref, hot_ref, *refs):
    *gathered, state_out, nation_out, beta_out, total = refs
    me = lax.axis_index("row")
    per = gathered[0].shape[0]
    n_states = state_out.shape[0]
    n_nations = nation_out.shape[0]
    for d, part in enumerate(gathered):
        peer = jnp.bitwise_xor(me, d)
        total[pl.ds(pl.multiple_of(peer * per, per), per), :] = part[...]
    sums = total[...]
    nation_total = hot_dot(hot_ref[...].astype(BF16), sums, ((1,), (0,)))
    state_out[...] = sums - prior_ref[:n_states, :]
    nation_out[...] = nation_total - prior_ref[n_states : n_states + n_nations, :]
    beta_out[...] = jnp.sum(nation_total, axis=0, keepdims=True) - prior_ref[n_states + n_nations :, :]


def swap(x, axis, d):
    n = lax.axis_size(axis)
    return lax.ppermute(x, axis, [(i, i ^ d) for i in range(n)])


def gather_by(x, axis, distances):
    return [x] + [swap(x, axis, d) for d in distances]


def total_of(parts):
    while len(parts) > 1:
        parts = [sum(parts[i : i + 2][1:], parts[i]) for i in range(0, len(parts), 2)]
    return parts[0]


def on_device(
    features,
    precinct,
    outcome,
    row_counts,
    beta,
    nation_coef,
    state_coef,
    county_coef,
    precinct_coef,
    precinct_county,
    county_state,
    state_nation,
):
    rows_here, p_size = features.shape
    cnt_here = county_coef.shape[0]
    prec_here = precinct_coef.shape[0]
    n_states = state_coef.shape[0]
    n_row = lax.axis_size("row")
    n_grp = lax.axis_size("grp")
    share = cnt_here // n_row
    n_hi = prec_here // LANES
    steps = rows_here // ROW_STEP
    per = n_states // n_row

    precinct3 = precinct.reshape(steps, 1, ROW_STEP)
    outcome3 = outcome.reshape(steps, 1, ROW_STEP)
    states3 = county_state.reshape(n_grp, 1, cnt_here)
    prec2 = precinct_coef.reshape(n_hi, LANES)
    map2 = precinct_county.reshape(n_hi, LANES)
    beta2 = beta.reshape(1, p_size)
    nation_row = state_nation.reshape(1, n_states)

    n_nations = nation_coef.shape[0]
    small = (
        nation_row,
        nation_coef,
        state_coef,
        states3,
        county_coef,
        beta2,
        precinct3,
        prec2,
        map2,
        outcome3,
    )
    outs = pl.pallas_call(
        functools.partial(main_kernel, 2 * n_row),
        in_specs=[pl.BlockSpec(memory_space=pltpu.VMEM)]
        + [pl.BlockSpec(memory_space=pltpu.HBM)] * (SMALL + 1),
        out_specs=[pl.BlockSpec(memory_space=pltpu.HBM)] * (2 * n_row),
        out_shape=[jax.ShapeDtypeStruct((per, p_size), F32)] * n_row
        + [jax.ShapeDtypeStruct((share + n_hi, p_size), F32)] * n_row,
        scratch_shapes=[pltpu.VMEM(x.shape, x.dtype) for x in small]
        + [
            pltpu.VMEM((rows_here, p_size), BF16),
            pltpu.VMEM((cnt_here, p_size), BF16),
            pltpu.VMEM((cnt_here, ROW_STEP), F32),
            pltpu.VMEM((cnt_here, ROW_STEP), F32),
            pltpu.VMEM((1, ROW_STEP), jnp.int32),
            pltpu.VMEM((1, ROW_STEP), jnp.int32),
            pltpu.VMEM((1, ROW_STEP), F32),
            pltpu.VMEM((1, ROW_STEP), F32),
            pltpu.VMEM((1, ROW_STEP), F32),
            pltpu.VMEM((1, ROW_STEP), F32),
            pltpu.VMEM((cnt_here, ROW_STEP), BF16),
            pltpu.VMEM((cnt_here, ROW_STEP), BF16),
            pltpu.VMEM((cnt_here, p_size), F32),
            pltpu.VMEM((2 * n_hi, LANES), F32),
            pltpu.VMEM(state_coef.shape, F32),
        ]
        + [pltpu.VMEM((per, p_size), F32)] * n_row
        + [pltpu.VMEM((share + n_hi, p_size), F32)] * n_row
        + [
            pltpu.SemaphoreType.DMA((SMALL,)),
            pltpu.SemaphoreType.DMA((steps,)),
            pltpu.SemaphoreType.DMA((2 * n_row,)),
        ],
        compiler_params=pltpu.CompilerParams(vmem_limit_bytes=VMEM_LIMIT),
        name="local_sums",
    )(row_counts.reshape(1, 1, 1), features, *small)

    near = 1 << (n_grp.bit_length() // 2 - 1)
    state_parts = [outs[0]] + [swap(outs[d], "row", d) for d in range(1, n_row)]
    state_piece = total_of(state_parts)
    county_outs = outs[n_row:]
    from_core = [swap(county_outs[d ^ 1], "row", 1) for d in range(0, n_row, 2)]
    state_piece, *from_core = lax.optimization_barrier((state_piece, *from_core))
    chip_sums = [county_outs[d] + from_core[d // 2] for d in range(2, n_row, 2)]
    county_parts = [county_outs[0], from_core[0]] + [
        swap(x, "row", d) for x, d in zip(chip_sums, range(2, n_row, 2))
    ]
    state_piece = total_of(gather_by(state_piece, "grp", range(1, near)))
    county_grad, precinct_grad, prior, nation_hot = pl.pallas_call(
        county_end_kernel,
        out_shape=[
            jax.ShapeDtypeStruct((share, p_size), F32),
            jax.ShapeDtypeStruct((n_hi, LANES), F32),
            jax.ShapeDtypeStruct((n_states + n_nations + 1, p_size), F32),
            jax.ShapeDtypeStruct((n_nations, n_states), F32),
        ],
        compiler_params=pltpu.CompilerParams(vmem_limit_bytes=END_LIMIT),
        name="county_totals",
    )(nation_row, state_coef, nation_coef, beta2, *county_parts)

    state_piece = total_of(gather_by(state_piece, "grp", range(near, n_grp, near)))
    gathered = gather_by(state_piece, "row", range(1, n_row))
    state_grad, nation_grad, beta_grad = pl.pallas_call(
        end_kernel,
        out_shape=[
            jax.ShapeDtypeStruct(state_coef.shape, F32),
            jax.ShapeDtypeStruct(nation_coef.shape, F32),
            jax.ShapeDtypeStruct((1, p_size), F32),
        ],
        scratch_shapes=[pltpu.VMEM(state_coef.shape, F32)],
        compiler_params=pltpu.CompilerParams(vmem_limit_bytes=END_LIMIT),
        name="upper_totals",
    )(prior, nation_hot, *gathered)
    return county_grad, precinct_grad.reshape(prec_here), state_grad, nation_grad, beta_grad.reshape(p_size)


def solution(mesh):
    placed = (
        P(("grp", "row"), None),
        P(("grp", "row")),
        P(("grp", "row")),
        P("grp", "row"),
        P(),
        P(),
        P(),
        P("grp", None),
        P("grp"),
        P("grp"),
        P(),
        P(),
    )
    return jax.shard_map(
        on_device,
        mesh=mesh,
        in_specs=placed,
        out_specs=(P(("grp", "row"), None), P("grp"), P(), P(), P()),
        check_vma=False,
    )
```

```python
import functools

import jax
import jax.numpy as jnp
from jax import lax
from jax.experimental import pallas as pl
from jax.experimental.pallas import tpu as pltpu
from jax.sharding import PartitionSpec as P

LANES = 128
ROW_STEP = 1024
SMALL = 10
VMEM_LIMIT = 60 * 1024 * 1024
END_LIMIT = 16 * 1024 * 1024
F32 = jnp.float32
BF16 = jnp.bfloat16


def split3(x):
    a = x.astype(BF16)
    r = x - a.astype(F32)
    b = r.astype(BF16)
    c = (r - b.astype(F32)).astype(BF16)
    return a, b, c


def hot_dot(hot, x, dims):
    (left,), (right,) = dims
    return lax.dot_general(
        jnp.concatenate([hot] * 3, axis=left),
        jnp.concatenate(split3(x), axis=right),
        (dims, ((), ())),
        preferred_element_type=F32,
    )


def iota_rows(n):
    return lax.broadcasted_iota(jnp.int32, (n, 1), 0)


def pick(values, low, high_hot):
    found = []
    for at in range(0, low.shape[1], LANES):
        index = jnp.broadcast_to(low[:, at : at + LANES], values.shape)
        found.append(jnp.take_along_axis(values, index, axis=1, mode="promise_in_bounds"))
    return jnp.sum(
        jnp.where(high_hot, jnp.concatenate(found, axis=1), jnp.zeros((), values.dtype)),
        axis=0,
        keepdims=True,
    )


def main_kernel(n_out, count_ref, features_ref, *args):
    small = args[:SMALL]
    out_refs = args[SMALL : SMALL + n_out]
    held = args[SMALL + n_out : 2 * SMALL + n_out]
    feats, table, s0, s1, h0, h1, b0, b1, r0, r1, w0, w1, county_acc, prec_acc, state_acc, *outs, small_sems, sems, out_sems = (
        args[2 * SMALL + n_out :]
    )
    (
        state_nation_ref,
        nation_ref,
        state_ref,
        county_state_ref,
        county_ref,
        beta_ref,
        precinct_ref,
        prec_ref,
        map_ref,
        outcome_ref,
    ) = held
    scores, hot_rows, bases, residuals, weights = (s0, s1), (h0, h1), (b0, b1), (r0, r1), (w0, w1)
    state_outs, county_outs = outs[:2], outs[2:]
    n_row = len(county_outs)
    n_states = state_ref.shape[0]
    n_nations = nation_ref.shape[0]
    n_cnt, p_size = county_ref.shape
    n_hi = prec_ref.shape[0]
    chunks = precinct_ref.shape[0]
    size = precinct_ref.shape[2]

    def fetch(j):
        rows = pl.ds(pl.multiple_of(j * size, size), size)
        return pltpu.make_async_copy(features_ref.at[rows], feats.at[rows], sems.at[j])

    small_copies = [
        pltpu.make_async_copy(source, target, small_sems.at[k])
        for k, (source, target) in enumerate(zip(small, held))
    ]
    for copy in small_copies:
        copy.start()
    for j in range(2):
        fetch(j).start()
    for copy in small_copies:
        copy.wait()
    for j in range(2, 4):
        fetch(j).start()

    states = county_state_ref[lax.axis_index("grp")]
    state_hot = (iota_rows(n_states) == states).astype(F32).astype(BF16)
    nation_hot = (iota_rows(n_nations) == state_nation_ref[...]).astype(F32).astype(BF16)
    upper = state_ref[...] + hot_dot(nation_hot, nation_ref[...], ((0,), (0,)))
    table[...] = (county_ref[...] + hot_dot(state_hot, upper, ((0,), (0,))) + beta_ref[...]).astype(BF16)
    county_acc[...] = jnp.zeros_like(county_acc)
    prec_acc[...] = jnp.zeros_like(prec_acc)

    def block(j):
        return feats[pl.ds(pl.multiple_of(j * size, size), size), :]

    def parts_of(j):
        prec = precinct_ref[j]
        return jnp.bitwise_and(prec, LANES - 1), iota_rows(n_hi) == jnp.right_shift(prec, 7)

    def score(j, k):
        low, high_hot = parts_of(j)
        bases[k][...] = pick(prec_ref[...], low, high_hot)
        hot_rows[k][...] = pick(map_ref[...], low, high_hot)
        scores[k][...] = lax.dot_general(
            table[...], block(j), (((1,), (1,)), ((), ())), preferred_element_type=F32
        )

    def residue(j, k):
        county_hot = iota_rows(n_cnt) == hot_rows[k][...]
        linear = jnp.sum(jnp.where(county_hot, scores[k][...], 0.0), axis=0, keepdims=True)
        linear = linear + bases[k][...]
        row = j * size + lax.broadcasted_iota(jnp.int32, (1, size), 1)
        count = outcome_ref[j].astype(F32)
        residual = jnp.where(row < count_ref[0], count - jnp.exp(linear), 0.0)
        residuals[k][...] = residual
        rounded = residual.astype(BF16).astype(F32)
        weights[k][...] = jnp.where(county_hot, rounded, 0.0).astype(BF16)

    def collect(j, k):
        county_acc[...] += jnp.dot(weights[k][...], block(j), preferred_element_type=F32)
        low, high_hot = parts_of(j)
        low_hot = (iota_rows(LANES) == low).astype(F32).astype(BF16)
        by_high = jnp.concatenate(
            [jnp.where(high_hot, x.astype(F32), 0.0) for x in split3(residuals[k][...])[:2]], axis=0
        ).astype(BF16)
        prec_acc[...] += lax.dot_general(
            by_high, low_hot, (((1,), (1,)), ((), ())), preferred_element_type=F32
        )

    fetch(0).wait()
    score(0, 0)
    fetch(1).wait()
    score(1, 1)
    residue(0, 0)

    def body(t, carry):
        j = 2 * t
        fetch(j).wait()
        fetch(j + 1).wait()

        @pl.when(j + 2 < chunks)
        def _():
            fetch(j + 2).start()
            fetch(j + 3).start()

        residue(j - 1, 1)
        score(j, 0)
        collect(j - 2, 0)
        residue(j, 0)
        score(j + 1, 1)
        collect(j - 1, 1)
        return carry

    lax.fori_loop(1, chunks // 2, body, 0)
    residue(chunks - 1, 1)
    collect(chunks - 2, 0)
    collect(chunks - 1, 1)

    me = lax.axis_index("row")
    share = n_cnt // n_row
    half = n_states // 2
    prec_sum = prec_acc[:n_hi] + prec_acc[n_hi:]
    own_rows = pl.ds(pl.multiple_of(me * share, share), share)

    def send(k):
        copy = pltpu.make_async_copy(outs[k], out_refs[k], out_sems.at[k])
        copy.start()
        return copy

    copies = []
    for d in range(n_row):
        peer = jnp.bitwise_xor(me, d)
        sums = county_acc[pl.ds(pl.multiple_of(peer * share, share), share), :]
        county_outs[d][:share, :] = sums if d else sums - county_ref[own_rows, :]
        county_outs[d][share:, :LANES] = prec_sum if d else prec_sum - prec_ref[...]
        county_outs[d][share:, LANES:] = jnp.zeros((n_hi, p_size - LANES), F32)
        copies.append(send(2 + d))
    state_acc[...] = hot_dot(state_hot, county_acc[...], ((1,), (0,)))
    for d in range(2):
        core = jnp.bitwise_xor(jnp.bitwise_and(me, 1), d)
        sums = state_acc[pl.ds(pl.multiple_of(core * half, half), half), :]
        pieces, per, _ = state_outs[d].shape
        for q in range(pieces):
            state_outs[d][q] = sums[q * per : (q + 1) * per, :]
        copies.append(send(d))
    for copy in copies:
        copy.wait()


def plane_index(near, n_row):
    x = jnp.bitwise_and(lax.axis_index("grp"), near - 1)
    return x * (n_row // 2) + jnp.right_shift(lax.axis_index("row"), 1)


def chip_sum_kernel(near, n_row, own_ref, core_ref, *refs):
    *outs, own, sem = refs
    copy = pltpu.make_async_copy(own_ref, own, sem)
    copy.start()
    copy.wait()
    me = plane_index(near, n_row)
    for d, out in enumerate(outs):
        piece = jnp.bitwise_xor(me, d)
        out[...] = own[piece] + core_ref[piece]


def county_end_kernel(state_nation_ref, state_ref, nation_ref, beta_ref, *refs):
    *parts, county_out, prec_out, prior_out, hot_out = refs
    share = county_out.shape[0]
    n_states = state_ref.shape[0]
    n_nations = nation_ref.shape[0]
    prior_out[:n_states, :] = state_ref[...]
    prior_out[n_states : n_states + n_nations, :] = nation_ref[...]
    prior_out[n_states + n_nations :, :] = beta_ref[...]
    hot_out[...] = (iota_rows(n_nations) == state_nation_ref[...]).astype(F32)
    county_out[...] = total_of([part[:share, :] for part in parts])
    prec_out[...] = total_of([part[share:, :LANES] for part in parts])


def end_kernel(near, n_row, prior_ref, hot_ref, *refs):
    *gathered, state_out, nation_out, beta_out, parts, total = refs
    me = plane_index(near, n_row)
    core = jnp.bitwise_and(lax.axis_index("row"), 1)
    per = gathered[0].shape[0]
    n_states = state_out.shape[0]
    n_nations = nation_out.shape[0]
    chips = len(gathered) // 2
    for k, part in enumerate(gathered):
        place = jnp.bitwise_xor(core, k // chips) * chips + jnp.bitwise_xor(me, k % chips)
        parts[place] = part[...]
    for k in range(len(gathered)):
        total[k * per : (k + 1) * per, :] = parts[k]
    sums = total[...]
    nation_total = hot_dot(hot_ref[...].astype(BF16), sums, ((1,), (0,)))
    state_out[...] = sums - prior_ref[:n_states, :]
    nation_out[...] = nation_total - prior_ref[n_states : n_states + n_nations, :]
    beta_out[...] = jnp.sum(nation_total, axis=0, keepdims=True) - prior_ref[n_states + n_nations :, :]


def swap(x, axis, d):
    n = lax.axis_size(axis)
    return lax.ppermute(x, axis, [(i, i ^ d) for i in range(n)])


def gather_by(x, axis, distances):
    return [x] + [swap(x, axis, d) for d in distances]


def swap_plane(x, near, d):
    n_grp, n_row = lax.axis_size("grp"), lax.axis_size("row")
    up, across = d // (n_row // 2), d % (n_row // 2) * 2
    pairs = [
        (g * n_row + r, (g ^ up) * n_row + (r ^ across)) for g in range(n_grp) for r in range(n_row)
    ]
    return lax.ppermute(x, ("grp", "row"), pairs)


def total_of(parts):
    while len(parts) > 1:
        parts = [sum(parts[i : i + 2][1:], parts[i]) for i in range(0, len(parts), 2)]
    return parts[0]


def on_device(
    features,
    precinct,
    outcome,
    row_counts,
    beta,
    nation_coef,
    state_coef,
    county_coef,
    precinct_coef,
    precinct_county,
    county_state,
    state_nation,
):
    rows_here, p_size = features.shape
    cnt_here = county_coef.shape[0]
    prec_here = precinct_coef.shape[0]
    n_states = state_coef.shape[0]
    n_row = lax.axis_size("row")
    n_grp = lax.axis_size("grp")
    share = cnt_here // n_row
    n_hi = prec_here // LANES
    steps = rows_here // ROW_STEP
    near = 1 << (n_grp.bit_length() // 2 - 1)
    chips = near * n_row // 2
    half = n_states // 2
    per = half // chips

    precinct3 = precinct.reshape(steps, 1, ROW_STEP)
    outcome3 = outcome.reshape(steps, 1, ROW_STEP)
    states3 = county_state.reshape(n_grp, 1, cnt_here)
    prec2 = precinct_coef.reshape(n_hi, LANES)
    map2 = precinct_county.reshape(n_hi, LANES)
    beta2 = beta.reshape(1, p_size)
    nation_row = state_nation.reshape(1, n_states)

    n_nations = nation_coef.shape[0]
    small = (
        nation_row,
        nation_coef,
        state_coef,
        states3,
        county_coef,
        beta2,
        precinct3,
        prec2,
        map2,
        outcome3,
    )
    outs = pl.pallas_call(
        functools.partial(main_kernel, 2 + n_row),
        in_specs=[pl.BlockSpec(memory_space=pltpu.VMEM)]
        + [pl.BlockSpec(memory_space=pltpu.HBM)] * (SMALL + 1),
        out_specs=[pl.BlockSpec(memory_space=pltpu.HBM)] * (2 + n_row),
        out_shape=[jax.ShapeDtypeStruct((chips, per, p_size), F32)] * 2
        + [jax.ShapeDtypeStruct((share + n_hi, p_size), F32)] * n_row,
        scratch_shapes=[pltpu.VMEM(x.shape, x.dtype) for x in small]
        + [
            pltpu.VMEM((rows_here, p_size), BF16),
            pltpu.VMEM((cnt_here, p_size), BF16),
            pltpu.VMEM((cnt_here, ROW_STEP), F32),
            pltpu.VMEM((cnt_here, ROW_STEP), F32),
            pltpu.VMEM((1, ROW_STEP), jnp.int32),
            pltpu.VMEM((1, ROW_STEP), jnp.int32),
            pltpu.VMEM((1, ROW_STEP), F32),
            pltpu.VMEM((1, ROW_STEP), F32),
            pltpu.VMEM((1, ROW_STEP), F32),
            pltpu.VMEM((1, ROW_STEP), F32),
            pltpu.VMEM((cnt_here, ROW_STEP), BF16),
            pltpu.VMEM((cnt_here, ROW_STEP), BF16),
            pltpu.VMEM((cnt_here, p_size), F32),
            pltpu.VMEM((2 * n_hi, LANES), F32),
            pltpu.VMEM(state_coef.shape, F32),
        ]
        + [pltpu.VMEM((chips, per, p_size), F32)] * 2
        + [pltpu.VMEM((share + n_hi, p_size), F32)] * n_row
        + [
            pltpu.SemaphoreType.DMA((SMALL,)),
            pltpu.SemaphoreType.DMA((steps,)),
            pltpu.SemaphoreType.DMA((2 + n_row,)),
        ],
        compiler_params=pltpu.CompilerParams(vmem_limit_bytes=VMEM_LIMIT),
        name="local_sums",
    )(row_counts.reshape(1, 1, 1), features, *small)

    state_core = swap(outs[1], "row", 1)
    pieces = pl.pallas_call(
        functools.partial(chip_sum_kernel, near, n_row),
        in_specs=[pl.BlockSpec(memory_space=pl.ANY), pl.BlockSpec(memory_space=pltpu.VMEM)],
        out_shape=[jax.ShapeDtypeStruct((per, p_size), F32)] * chips,
        scratch_shapes=[pltpu.VMEM((chips, per, p_size), F32), pltpu.SemaphoreType.DMA(())],
        compiler_params=pltpu.CompilerParams(vmem_limit_bytes=END_LIMIT),
        name="chip_sums",
    )(outs[0], state_core)
    state_piece = total_of([pieces[0]] + [swap_plane(pieces[d], near, d) for d in range(1, chips)])
    county_outs = outs[2:]
    from_core = [swap(county_outs[d ^ 1], "row", 1) for d in range(0, n_row, 2)]
    state_piece, *from_core = lax.optimization_barrier((state_piece, *from_core))
    chip_sums = [county_outs[d] + from_core[d // 2] for d in range(2, n_row, 2)]
    county_parts = [county_outs[0], from_core[0]] + [
        swap(x, "row", d) for x, d in zip(chip_sums, range(2, n_row, 2))
    ]
    county_grad, precinct_grad, prior, nation_hot = pl.pallas_call(
        county_end_kernel,
        out_shape=[
            jax.ShapeDtypeStruct((share, p_size), F32),
            jax.ShapeDtypeStruct((n_hi, LANES), F32),
            jax.ShapeDtypeStruct((n_states + n_nations + 1, p_size), F32),
            jax.ShapeDtypeStruct((n_nations, n_states), F32),
        ],
        compiler_params=pltpu.CompilerParams(vmem_limit_bytes=END_LIMIT),
        name="county_totals",
    )(nation_row, state_coef, nation_coef, beta2, *county_parts)

    state_piece = total_of(gather_by(state_piece, "grp", range(near, n_grp, near)))
    gathered = [state_piece] + [swap_plane(state_piece, near, d) for d in range(1, chips)]
    gathered += [swap(x, "row", 1) for x in gathered]
    state_grad, nation_grad, beta_grad = pl.pallas_call(
        functools.partial(end_kernel, near, n_row),
        out_shape=[
            jax.ShapeDtypeStruct(state_coef.shape, F32),
            jax.ShapeDtypeStruct(nation_coef.shape, F32),
            jax.ShapeDtypeStruct((1, p_size), F32),
        ],
        scratch_shapes=[
            pltpu.VMEM((2 * chips, per, p_size), F32),
            pltpu.VMEM(state_coef.shape, F32),
        ],
        compiler_params=pltpu.CompilerParams(vmem_limit_bytes=END_LIMIT),
        name="upper_totals",
    )(prior, nation_hot, *gathered)
    return county_grad, precinct_grad.reshape(prec_here), state_grad, nation_grad, beta_grad.reshape(p_size)


def solution(mesh):
    placed = (
        P(("grp", "row"), None),
        P(("grp", "row")),
        P(("grp", "row")),
        P("grp", "row"),
        P(),
        P(),
        P(),
        P("grp", None),
        P("grp"),
        P("grp"),
        P(),
        P(),
    )
    return jax.shard_map(
        on_device,
        mesh=mesh,
        in_specs=placed,
        out_specs=(P(("grp", "row"), None), P("grp"), P(), P(), P()),
        check_vma=False,
    )
```

```python
import functools

import jax
import jax.numpy as jnp
from jax import lax
from jax.experimental import pallas as pl
from jax.experimental.pallas import tpu as pltpu
from jax.sharding import PartitionSpec as P

LANES = 128
ROW_STEP = 1024
SMALL = 10
VMEM_LIMIT = 60 * 1024 * 1024
END_LIMIT = 16 * 1024 * 1024
F32 = jnp.float32
BF16 = jnp.bfloat16


def split3(x):
    a = x.astype(BF16)
    r = x - a.astype(F32)
    b = r.astype(BF16)
    c = (r - b.astype(F32)).astype(BF16)
    return a, b, c


def hot_dot(hot, x, dims):
    (left,), (right,) = dims
    return lax.dot_general(
        jnp.concatenate([hot] * 3, axis=left),
        jnp.concatenate(split3(x), axis=right),
        (dims, ((), ())),
        preferred_element_type=F32,
    )


def iota_rows(n):
    return lax.broadcasted_iota(jnp.int32, (n, 1), 0)


def pick(values, low, high_hot):
    found = []
    for at in range(0, low.shape[1], LANES):
        index = jnp.broadcast_to(low[:, at : at + LANES], values.shape)
        found.append(jnp.take_along_axis(values, index, axis=1, mode="promise_in_bounds"))
    return jnp.sum(
        jnp.where(high_hot, jnp.concatenate(found, axis=1), jnp.zeros((), values.dtype)),
        axis=0,
        keepdims=True,
    )


def main_kernel(n_out, count_ref, features_ref, *args):
    small = args[:SMALL]
    out_refs = args[SMALL : SMALL + n_out]
    held = args[SMALL + n_out : 2 * SMALL + n_out]
    feats, table, s0, s1, h0, h1, b0, b1, r0, r1, w0, w1, county_acc, prec_acc, state_acc, *outs, small_sems, sems, out_sems = (
        args[2 * SMALL + n_out :]
    )
    (
        state_nation_ref,
        nation_ref,
        state_ref,
        county_state_ref,
        county_ref,
        beta_ref,
        precinct_ref,
        prec_ref,
        map_ref,
        outcome_ref,
    ) = held
    scores, hot_rows, bases, residuals, weights = (s0, s1), (h0, h1), (b0, b1), (r0, r1), (w0, w1)
    n_row = len(outs) // 2
    state_outs, county_outs = outs[:n_row], outs[n_row:]
    n_states = state_ref.shape[0]
    n_nations = nation_ref.shape[0]
    n_cnt, p_size = county_ref.shape
    n_hi = prec_ref.shape[0]
    chunks = precinct_ref.shape[0]
    size = precinct_ref.shape[2]

    def fetch(j):
        rows = pl.ds(pl.multiple_of(j * size, size), size)
        return pltpu.make_async_copy(features_ref.at[rows], feats.at[rows], sems.at[j])

    small_copies = [
        pltpu.make_async_copy(source, target, small_sems.at[k])
        for k, (source, target) in enumerate(zip(small, held))
    ]
    for copy in small_copies:
        copy.start()
    for j in range(2):
        fetch(j).start()
    for copy in small_copies:
        copy.wait()
    for j in range(2, 4):
        fetch(j).start()

    states = county_state_ref[lax.axis_index("grp")]
    state_hot = (iota_rows(n_states) == states).astype(F32).astype(BF16)
    nation_hot = (iota_rows(n_nations) == state_nation_ref[...]).astype(F32).astype(BF16)
    upper = state_ref[...] + hot_dot(nation_hot, nation_ref[...], ((0,), (0,)))
    table[...] = (county_ref[...] + hot_dot(state_hot, upper, ((0,), (0,))) + beta_ref[...]).astype(BF16)
    county_acc[...] = jnp.zeros_like(county_acc)
    prec_acc[...] = jnp.zeros_like(prec_acc)

    def block(j):
        return feats[pl.ds(pl.multiple_of(j * size, size), size), :]

    def parts_of(j):
        prec = precinct_ref[j]
        return jnp.bitwise_and(prec, LANES - 1), iota_rows(n_hi) == jnp.right_shift(prec, 7)

    def score(j, k):
        low, high_hot = parts_of(j)
        bases[k][...] = pick(prec_ref[...], low, high_hot)
        hot_rows[k][...] = pick(map_ref[...], low, high_hot)
        scores[k][...] = lax.dot_general(
            table[...], block(j), (((1,), (1,)), ((), ())), preferred_element_type=F32
        )

    def residue(j, k):
        county_hot = iota_rows(n_cnt) == hot_rows[k][...]
        linear = jnp.sum(jnp.where(county_hot, scores[k][...], 0.0), axis=0, keepdims=True)
        linear = linear + bases[k][...]
        row = j * size + lax.broadcasted_iota(jnp.int32, (1, size), 1)
        count = outcome_ref[j].astype(F32)
        residual = jnp.where(row < count_ref[0], count - jnp.exp(linear), 0.0)
        residuals[k][...] = residual
        rounded = residual.astype(BF16).astype(F32)
        weights[k][...] = jnp.where(county_hot, rounded, 0.0).astype(BF16)

    def collect(j, k):
        county_acc[...] += jnp.dot(weights[k][...], block(j), preferred_element_type=F32)
        low, high_hot = parts_of(j)
        low_hot = (iota_rows(LANES) == low).astype(F32).astype(BF16)
        by_high = jnp.concatenate(
            [jnp.where(high_hot, x.astype(F32), 0.0) for x in split3(residuals[k][...])[:2]], axis=0
        ).astype(BF16)
        prec_acc[...] += lax.dot_general(
            by_high, low_hot, (((1,), (1,)), ((), ())), preferred_element_type=F32
        )

    fetch(0).wait()
    score(0, 0)
    fetch(1).wait()
    score(1, 1)
    residue(0, 0)

    def body(t, carry):
        j = 2 * t
        fetch(j).wait()
        fetch(j + 1).wait()

        @pl.when(j + 2 < chunks)
        def _():
            fetch(j + 2).start()
            fetch(j + 3).start()

        residue(j - 1, 1)
        score(j, 0)
        collect(j - 2, 0)
        residue(j, 0)
        score(j + 1, 1)
        collect(j - 1, 1)
        return carry

    lax.fori_loop(1, chunks // 2, body, 0)
    residue(chunks - 1, 1)
    collect(chunks - 2, 0)
    collect(chunks - 1, 1)

    me = lax.axis_index("row")
    share = n_cnt // n_row
    per = n_states // n_row
    prec_sum = prec_acc[:n_hi] + prec_acc[n_hi:]
    own_rows = pl.ds(pl.multiple_of(me * share, share), share)

    def send(k):
        copy = pltpu.make_async_copy(outs[k], out_refs[k], out_sems.at[k])
        copy.start()
        return copy

    copies = []
    for d in range(n_row):
        peer = jnp.bitwise_xor(me, d)
        sums = county_acc[pl.ds(pl.multiple_of(peer * share, share), share), :]
        county_outs[d][:share, :] = sums if d else sums - county_ref[own_rows, :]
        county_outs[d][share:, :LANES] = prec_sum if d else prec_sum - prec_ref[...]
        county_outs[d][share:, LANES:] = jnp.zeros((n_hi, p_size - LANES), F32)
        copies.append(send(n_row + d))
    state_acc[...] = hot_dot(state_hot, county_acc[...], ((1,), (0,)))
    for d in range(n_row):
        peer = jnp.bitwise_xor(me, d)
        state_outs[d][...] = state_acc[pl.ds(pl.multiple_of(peer * per, per), per), :]
        copies.append(send(d))
    for copy in copies:
        copy.wait()


def county_end_kernel(state_nation_ref, state_ref, nation_ref, beta_ref, *refs):
    *parts, county_out, prec_out, prior_out, hot_out = refs
    share = county_out.shape[0]
    n_states = state_ref.shape[0]
    n_nations = nation_ref.shape[0]
    prior_out[:n_states, :] = state_ref[...]
    prior_out[n_states : n_states + n_nations, :] = nation_ref[...]
    prior_out[n_states + n_nations :, :] = beta_ref[...]
    hot_out[...] = (iota_rows(n_nations) == state_nation_ref[...]).astype(F32)
    county_out[...] = total_of([part[:share, :] for part in parts])
    prec_out[...] = total_of([part[share:, :LANES] for part in parts])


def end_kernel(prior_ref, hot_ref, *refs):
    *gathered, state_out, nation_out, beta_out, total = refs
    me = lax.axis_index("row")
    per = gathered[0].shape[0]
    n_states = state_out.shape[0]
    n_nations = nation_out.shape[0]
    for d, part in enumerate(gathered):
        peer = jnp.bitwise_xor(me, d)
        total[pl.ds(pl.multiple_of(peer * per, per), per), :] = part[...]
    sums = total[...]
    nation_total = hot_dot(hot_ref[...].astype(BF16), sums, ((1,), (0,)))
    state_out[...] = sums - prior_ref[:n_states, :]
    nation_out[...] = nation_total - prior_ref[n_states : n_states + n_nations, :]
    beta_out[...] = jnp.sum(nation_total, axis=0, keepdims=True) - prior_ref[n_states + n_nations :, :]


def swap(x, axis, d):
    n = lax.axis_size(axis)
    return lax.ppermute(x, axis, [(i, i ^ d) for i in range(n)])


def gather_by(x, axis, distances):
    return [x] + [swap(x, axis, d) for d in distances]


def total_of(parts):
    while len(parts) > 1:
        parts = [sum(parts[i : i + 2][1:], parts[i]) for i in range(0, len(parts), 2)]
    return parts[0]


def on_device(
    features,
    precinct,
    outcome,
    row_counts,
    beta,
    nation_coef,
    state_coef,
    county_coef,
    precinct_coef,
    precinct_county,
    county_state,
    state_nation,
):
    rows_here, p_size = features.shape
    cnt_here = county_coef.shape[0]
    prec_here = precinct_coef.shape[0]
    n_states = state_coef.shape[0]
    n_row = lax.axis_size("row")
    n_grp = lax.axis_size("grp")
    share = cnt_here // n_row
    n_hi = prec_here // LANES
    steps = rows_here // ROW_STEP
    per = n_states // n_row

    precinct3 = precinct.reshape(steps, 1, ROW_STEP)
    outcome3 = outcome.reshape(steps, 1, ROW_STEP)
    states3 = county_state.reshape(n_grp, 1, cnt_here)
    prec2 = precinct_coef.reshape(n_hi, LANES)
    map2 = precinct_county.reshape(n_hi, LANES)
    beta2 = beta.reshape(1, p_size)
    nation_row = state_nation.reshape(1, n_states)

    n_nations = nation_coef.shape[0]
    small = (
        nation_row,
        nation_coef,
        state_coef,
        states3,
        county_coef,
        beta2,
        precinct3,
        prec2,
        map2,
        outcome3,
    )
    outs = pl.pallas_call(
        functools.partial(main_kernel, 2 * n_row),
        in_specs=[pl.BlockSpec(memory_space=pltpu.VMEM)]
        + [pl.BlockSpec(memory_space=pltpu.HBM)] * (SMALL + 1),
        out_specs=[pl.BlockSpec(memory_space=pltpu.HBM)] * (2 * n_row),
        out_shape=[jax.ShapeDtypeStruct((per, p_size), F32)] * n_row
        + [jax.ShapeDtypeStruct((share + n_hi, p_size), F32)] * n_row,
        scratch_shapes=[pltpu.VMEM(x.shape, x.dtype) for x in small]
        + [
            pltpu.VMEM((rows_here, p_size), BF16),
            pltpu.VMEM((cnt_here, p_size), BF16),
            pltpu.VMEM((cnt_here, ROW_STEP), F32),
            pltpu.VMEM((cnt_here, ROW_STEP), F32),
            pltpu.VMEM((1, ROW_STEP), jnp.int32),
            pltpu.VMEM((1, ROW_STEP), jnp.int32),
            pltpu.VMEM((1, ROW_STEP), F32),
            pltpu.VMEM((1, ROW_STEP), F32),
            pltpu.VMEM((1, ROW_STEP), F32),
            pltpu.VMEM((1, ROW_STEP), F32),
            pltpu.VMEM((cnt_here, ROW_STEP), BF16),
            pltpu.VMEM((cnt_here, ROW_STEP), BF16),
            pltpu.VMEM((cnt_here, p_size), F32),
            pltpu.VMEM((2 * n_hi, LANES), F32),
            pltpu.VMEM(state_coef.shape, F32),
        ]
        + [pltpu.VMEM((per, p_size), F32)] * n_row
        + [pltpu.VMEM((share + n_hi, p_size), F32)] * n_row
        + [
            pltpu.SemaphoreType.DMA((SMALL,)),
            pltpu.SemaphoreType.DMA((steps,)),
            pltpu.SemaphoreType.DMA((2 * n_row,)),
        ],
        compiler_params=pltpu.CompilerParams(vmem_limit_bytes=VMEM_LIMIT),
        name="local_sums",
    )(row_counts.reshape(1, 1, 1), features, *small)

    near = 1 << (n_grp.bit_length() // 2 - 1)
    state_parts = [outs[0]] + [swap(outs[d], "row", d) for d in range(1, n_row)]
    state_piece = total_of(state_parts)
    county_outs = outs[n_row:]
    from_core = [swap(county_outs[d ^ 1], "row", 1) for d in range(0, n_row, 2)]
    state_piece, *from_core = lax.optimization_barrier((state_piece, *from_core))
    chip_sums = [county_outs[d] + from_core[d // 2] for d in range(2, n_row, 2)]
    county_parts = [county_outs[0], from_core[0]] + [
        swap(x, "row", d) for x, d in zip(chip_sums, range(2, n_row, 2))
    ]
    pairs = [[g + d for d in range(near)] for g in range(0, n_grp, near)]
    state_piece = lax.psum(state_piece, "grp", axis_index_groups=pairs)
    county_grad, precinct_grad, prior, nation_hot = pl.pallas_call(
        county_end_kernel,
        out_shape=[
            jax.ShapeDtypeStruct((share, p_size), F32),
            jax.ShapeDtypeStruct((n_hi, LANES), F32),
            jax.ShapeDtypeStruct((n_states + n_nations + 1, p_size), F32),
            jax.ShapeDtypeStruct((n_nations, n_states), F32),
        ],
        compiler_params=pltpu.CompilerParams(vmem_limit_bytes=END_LIMIT),
        name="county_totals",
    )(nation_row, state_coef, nation_coef, beta2, *county_parts)

    lines = [list(range(d, n_grp, near)) for d in range(near)]
    state_piece = lax.psum(state_piece, "grp", axis_index_groups=lines)
    gathered = gather_by(state_piece, "row", range(1, n_row))
    state_grad, nation_grad, beta_grad = pl.pallas_call(
        end_kernel,
        out_shape=[
            jax.ShapeDtypeStruct(state_coef.shape, F32),
            jax.ShapeDtypeStruct(nation_coef.shape, F32),
            jax.ShapeDtypeStruct((1, p_size), F32),
        ],
        scratch_shapes=[pltpu.VMEM(state_coef.shape, F32)],
        compiler_params=pltpu.CompilerParams(vmem_limit_bytes=END_LIMIT),
        name="upper_totals",
    )(prior, nation_hot, *gathered)
    return county_grad, precinct_grad.reshape(prec_here), state_grad, nation_grad, beta_grad.reshape(p_size)


def solution(mesh):
    placed = (
        P(("grp", "row"), None),
        P(("grp", "row")),
        P(("grp", "row")),
        P("grp", "row"),
        P(),
        P(),
        P(),
        P("grp", None),
        P("grp"),
        P("grp"),
        P(),
        P(),
    )
    return jax.shard_map(
        on_device,
        mesh=mesh,
        in_specs=placed,
        out_specs=(P(("grp", "row"), None), P("grp"), P(), P(), P()),
        check_vma=False,
    )
```

```python
import functools

import jax
import jax.numpy as jnp
from jax import lax
from jax.experimental import pallas as pl
from jax.experimental.pallas import tpu as pltpu
from jax.sharding import PartitionSpec as P

LANES = 128
ROW_STEP = 2048
SMALL = 10
VMEM_LIMIT = 60 * 1024 * 1024
END_LIMIT = 16 * 1024 * 1024
F32 = jnp.float32
BF16 = jnp.bfloat16


def split3(x):
    a = x.astype(BF16)
    r = x - a.astype(F32)
    b = r.astype(BF16)
    c = (r - b.astype(F32)).astype(BF16)
    return a, b, c


def hot_dot(hot, x, dims):
    (left,), (right,) = dims
    return lax.dot_general(
        jnp.concatenate([hot] * 3, axis=left),
        jnp.concatenate(split3(x), axis=right),
        (dims, ((), ())),
        preferred_element_type=F32,
    )


def iota_rows(n):
    return lax.broadcasted_iota(jnp.int32, (n, 1), 0)


def pick(values, low, high_hot):
    found = []
    for at in range(0, low.shape[1], LANES):
        index = jnp.broadcast_to(low[:, at : at + LANES], values.shape)
        found.append(jnp.take_along_axis(values, index, axis=1, mode="promise_in_bounds"))
    return jnp.sum(
        jnp.where(high_hot, jnp.concatenate(found, axis=1), jnp.zeros((), values.dtype)),
        axis=0,
        keepdims=True,
    )


def main_kernel(n_out, count_ref, features_ref, *args):
    small = args[:SMALL]
    out_refs = args[SMALL : SMALL + n_out]
    held = args[SMALL + n_out : 2 * SMALL + n_out]
    feats, table, s0, s1, h0, h1, b0, b1, r0, r1, w0, w1, county_acc, prec_acc, state_acc, *outs, small_sems, sems, out_sems = (
        args[2 * SMALL + n_out :]
    )
    (
        state_nation_ref,
        nation_ref,
        state_ref,
        county_state_ref,
        county_ref,
        beta_ref,
        precinct_ref,
        prec_ref,
        map_ref,
        outcome_ref,
    ) = held
    scores, hot_rows, bases, residuals, weights = (s0, s1), (h0, h1), (b0, b1), (r0, r1), (w0, w1)
    n_row = len(outs) // 2
    state_outs, county_outs = outs[:n_row], outs[n_row:]
    n_states = state_ref.shape[0]
    n_nations = nation_ref.shape[0]
    n_cnt, p_size = county_ref.shape
    n_hi = prec_ref.shape[0]
    chunks = precinct_ref.shape[0]
    size = precinct_ref.shape[2]

    def fetch(j):
        rows = pl.ds(pl.multiple_of(j * size, size), size)
        return pltpu.make_async_copy(features_ref.at[rows], feats.at[rows], sems.at[j])

    small_copies = [
        pltpu.make_async_copy(source, target, small_sems.at[k])
        for k, (source, target) in enumerate(zip(small, held))
    ]
    for copy in small_copies:
        copy.start()
    for j in range(2):
        fetch(j).start()
    for copy in small_copies:
        copy.wait()
    for j in range(2, 4):
        fetch(j).start()

    states = county_state_ref[lax.axis_index("grp")]
    state_hot = (iota_rows(n_states) == states).astype(F32).astype(BF16)
    nation_hot = (iota_rows(n_nations) == state_nation_ref[...]).astype(F32).astype(BF16)
    upper = state_ref[...] + hot_dot(nation_hot, nation_ref[...], ((0,), (0,)))
    table[...] = (county_ref[...] + hot_dot(state_hot, upper, ((0,), (0,))) + beta_ref[...]).astype(BF16)
    county_acc[...] = jnp.zeros_like(county_acc)
    prec_acc[...] = jnp.zeros_like(prec_acc)

    def block(j):
        return feats[pl.ds(pl.multiple_of(j * size, size), size), :]

    def parts_of(j):
        prec = precinct_ref[j]
        return jnp.bitwise_and(prec, LANES - 1), iota_rows(n_hi) == jnp.right_shift(prec, 7)

    def score(j, k):
        low, high_hot = parts_of(j)
        bases[k][...] = pick(prec_ref[...], low, high_hot)
        hot_rows[k][...] = pick(map_ref[...], low, high_hot)
        scores[k][...] = lax.dot_general(
            table[...], block(j), (((1,), (1,)), ((), ())), preferred_element_type=F32
        )

    def residue(j, k):
        county_hot = iota_rows(n_cnt) == hot_rows[k][...]
        linear = jnp.sum(jnp.where(county_hot, scores[k][...], 0.0), axis=0, keepdims=True)
        linear = linear + bases[k][...]
        row = j * size + lax.broadcasted_iota(jnp.int32, (1, size), 1)
        count = outcome_ref[j].astype(F32)
        residual = jnp.where(row < count_ref[0], count - jnp.exp(linear), 0.0)
        residuals[k][...] = residual
        rounded = residual.astype(BF16).astype(F32)
        weights[k][...] = jnp.where(county_hot, rounded, 0.0).astype(BF16)

    def collect(j, k):
        county_acc[...] += jnp.dot(weights[k][...], block(j), preferred_element_type=F32)
        low, high_hot = parts_of(j)
        low_hot = (iota_rows(LANES) == low).astype(F32).astype(BF16)
        by_high = jnp.concatenate(
            [jnp.where(high_hot, x.astype(F32), 0.0) for x in split3(residuals[k][...])[:2]], axis=0
        ).astype(BF16)
        prec_acc[...] += lax.dot_general(
            by_high, low_hot, (((1,), (1,)), ((), ())), preferred_element_type=F32
        )

    fetch(0).wait()
    score(0, 0)
    fetch(1).wait()
    score(1, 1)
    residue(0, 0)

    def body(t, carry):
        j = 2 * t
        fetch(j).wait()
        fetch(j + 1).wait()

        @pl.when(j + 2 < chunks)
        def _():
            fetch(j + 2).start()
            fetch(j + 3).start()

        residue(j - 1, 1)
        score(j, 0)
        collect(j - 2, 0)
        residue(j, 0)
        score(j + 1, 1)
        collect(j - 1, 1)
        return carry

    lax.fori_loop(1, chunks // 2, body, 0)
    residue(chunks - 1, 1)
    collect(chunks - 2, 0)
    collect(chunks - 1, 1)

    me = lax.axis_index("row")
    share = n_cnt // n_row
    per = n_states // n_row
    prec_sum = prec_acc[:n_hi] + prec_acc[n_hi:]
    own_rows = pl.ds(pl.multiple_of(me * share, share), share)

    def send(k):
        copy = pltpu.make_async_copy(outs[k], out_refs[k], out_sems.at[k])
        copy.start()
        return copy

    copies = []
    for d in range(n_row):
        peer = jnp.bitwise_xor(me, d)
        sums = county_acc[pl.ds(pl.multiple_of(peer * share, share), share), :]
        county_outs[d][:share, :] = sums if d else sums - county_ref[own_rows, :]
        county_outs[d][share:, :LANES] = prec_sum if d else prec_sum - prec_ref[...]
        county_outs[d][share:, LANES:] = jnp.zeros((n_hi, p_size - LANES), F32)
        copies.append(send(n_row + d))
    state_acc[...] = hot_dot(state_hot, county_acc[...], ((1,), (0,)))
    for d in range(n_row):
        peer = jnp.bitwise_xor(me, d)
        state_outs[d][...] = state_acc[pl.ds(pl.multiple_of(peer * per, per), per), :]
        copies.append(send(d))
    for copy in copies:
        copy.wait()


def county_end_kernel(state_nation_ref, state_ref, nation_ref, beta_ref, *refs):
    *parts, county_out, prec_out, prior_out, hot_out = refs
    share = county_out.shape[0]
    n_states = state_ref.shape[0]
    n_nations = nation_ref.shape[0]
    prior_out[:n_states, :] = state_ref[...]
    prior_out[n_states : n_states + n_nations, :] = nation_ref[...]
    prior_out[n_states + n_nations :, :] = beta_ref[...]
    hot_out[...] = (iota_rows(n_nations) == state_nation_ref[...]).astype(F32)
    county_out[...] = total_of([part[:share, :] for part in parts])
    prec_out[...] = total_of([part[share:, :LANES] for part in parts])


def end_kernel(prior_ref, hot_ref, *refs):
    *gathered, state_out, nation_out, beta_out, total = refs
    me = lax.axis_index("row")
    per = gathered[0].shape[0]
    n_states = state_out.shape[0]
    n_nations = nation_out.shape[0]
    for d, part in enumerate(gathered):
        peer = jnp.bitwise_xor(me, d)
        total[pl.ds(pl.multiple_of(peer * per, per), per), :] = part[...]
    sums = total[...]
    nation_total = hot_dot(hot_ref[...].astype(BF16), sums, ((1,), (0,)))
    state_out[...] = sums - prior_ref[:n_states, :]
    nation_out[...] = nation_total - prior_ref[n_states : n_states + n_nations, :]
    beta_out[...] = jnp.sum(nation_total, axis=0, keepdims=True) - prior_ref[n_states + n_nations :, :]


def swap(x, axis, d):
    n = lax.axis_size(axis)
    return lax.ppermute(x, axis, [(i, i ^ d) for i in range(n)])


def gather_by(x, axis, distances):
    return [x] + [swap(x, axis, d) for d in distances]


def total_of(parts):
    while len(parts) > 1:
        parts = [sum(parts[i : i + 2][1:], parts[i]) for i in range(0, len(parts), 2)]
    return parts[0]


def on_device(
    features,
    precinct,
    outcome,
    row_counts,
    beta,
    nation_coef,
    state_coef,
    county_coef,
    precinct_coef,
    precinct_county,
    county_state,
    state_nation,
):
    rows_here, p_size = features.shape
    cnt_here = county_coef.shape[0]
    prec_here = precinct_coef.shape[0]
    n_states = state_coef.shape[0]
    n_row = lax.axis_size("row")
    n_grp = lax.axis_size("grp")
    share = cnt_here // n_row
    n_hi = prec_here // LANES
    steps = rows_here // ROW_STEP
    per = n_states // n_row

    precinct3 = precinct.reshape(steps, 1, ROW_STEP)
    outcome3 = outcome.reshape(steps, 1, ROW_STEP)
    states3 = county_state.reshape(n_grp, 1, cnt_here)
    prec2 = precinct_coef.reshape(n_hi, LANES)
    map2 = precinct_county.reshape(n_hi, LANES)
    beta2 = beta.reshape(1, p_size)
    nation_row = state_nation.reshape(1, n_states)

    n_nations = nation_coef.shape[0]
    small = (
        nation_row,
        nation_coef,
        state_coef,
        states3,
        county_coef,
        beta2,
        precinct3,
        prec2,
        map2,
        outcome3,
    )
    outs = pl.pallas_call(
        functools.partial(main_kernel, 2 * n_row),
        in_specs=[pl.BlockSpec(memory_space=pltpu.VMEM)]
        + [pl.BlockSpec(memory_space=pltpu.HBM)] * (SMALL + 1),
        out_specs=[pl.BlockSpec(memory_space=pltpu.HBM)] * (2 * n_row),
        out_shape=[jax.ShapeDtypeStruct((per, p_size), F32)] * n_row
        + [jax.ShapeDtypeStruct((share + n_hi, p_size), F32)] * n_row,
        scratch_shapes=[pltpu.VMEM(x.shape, x.dtype) for x in small]
        + [
            pltpu.VMEM((rows_here, p_size), BF16),
            pltpu.VMEM((cnt_here, p_size), BF16),
            pltpu.VMEM((cnt_here, ROW_STEP), F32),
            pltpu.VMEM((cnt_here, ROW_STEP), F32),
            pltpu.VMEM((1, ROW_STEP), jnp.int32),
            pltpu.VMEM((1, ROW_STEP), jnp.int32),
            pltpu.VMEM((1, ROW_STEP), F32),
            pltpu.VMEM((1, ROW_STEP), F32),
            pltpu.VMEM((1, ROW_STEP), F32),
            pltpu.VMEM((1, ROW_STEP), F32),
            pltpu.VMEM((cnt_here, ROW_STEP), BF16),
            pltpu.VMEM((cnt_here, ROW_STEP), BF16),
            pltpu.VMEM((cnt_here, p_size), F32),
            pltpu.VMEM((2 * n_hi, LANES), F32),
            pltpu.VMEM(state_coef.shape, F32),
        ]
        + [pltpu.VMEM((per, p_size), F32)] * n_row
        + [pltpu.VMEM((share + n_hi, p_size), F32)] * n_row
        + [
            pltpu.SemaphoreType.DMA((SMALL,)),
            pltpu.SemaphoreType.DMA((steps,)),
            pltpu.SemaphoreType.DMA((2 * n_row,)),
        ],
        compiler_params=pltpu.CompilerParams(vmem_limit_bytes=VMEM_LIMIT),
        name="local_sums",
    )(row_counts.reshape(1, 1, 1), features, *small)

    near = 1 << (n_grp.bit_length() // 2 - 1)
    state_parts = [swap(outs[d], "row", d) for d in range(n_row)]
    state_piece = total_of(state_parts)
    county_outs = outs[n_row:]
    from_core = [swap(county_outs[d ^ 1], "row", 1) for d in range(0, n_row, 2)]
    state_piece, *from_core = lax.optimization_barrier((state_piece, *from_core))
    chip_sums = [county_outs[d] + from_core[d // 2] for d in range(2, n_row, 2)]
    county_parts = [swap(county_outs[0], "row", 0), from_core[0]] + [
        swap(x, "row", d) for x, d in zip(chip_sums, range(2, n_row, 2))
    ]
    state_piece = total_of(gather_by(state_piece, "grp", range(1, near)))
    county_grad, precinct_grad, prior, nation_hot = pl.pallas_call(
        county_end_kernel,
        out_shape=[
            jax.ShapeDtypeStruct((share, p_size), F32),
            jax.ShapeDtypeStruct((n_hi, LANES), F32),
            jax.ShapeDtypeStruct((n_states + n_nations + 1, p_size), F32),
            jax.ShapeDtypeStruct((n_nations, n_states), F32),
        ],
        compiler_params=pltpu.CompilerParams(vmem_limit_bytes=END_LIMIT),
        name="county_totals",
    )(nation_row, state_coef, nation_coef, beta2, *county_parts)

    state_piece = total_of(gather_by(state_piece, "grp", range(near, n_grp, near)))
    gathered = gather_by(state_piece, "row", range(1, n_row))
    state_grad, nation_grad, beta_grad = pl.pallas_call(
        end_kernel,
        out_shape=[
            jax.ShapeDtypeStruct(state_coef.shape, F32),
            jax.ShapeDtypeStruct(nation_coef.shape, F32),
            jax.ShapeDtypeStruct((1, p_size), F32),
        ],
        scratch_shapes=[pltpu.VMEM(state_coef.shape, F32)],
        compiler_params=pltpu.CompilerParams(vmem_limit_bytes=END_LIMIT),
        name="upper_totals",
    )(prior, nation_hot, *gathered)
    return county_grad, precinct_grad.reshape(prec_here), state_grad, nation_grad, beta_grad.reshape(p_size)


def solution(mesh):
    placed = (
        P(("grp", "row"), None),
        P(("grp", "row")),
        P(("grp", "row")),
        P("grp", "row"),
        P(),
        P(),
        P(),
        P("grp", None),
        P("grp"),
        P("grp"),
        P(),
        P(),
    )
    return jax.shard_map(
        on_device,
        mesh=mesh,
        in_specs=placed,
        out_specs=(P(("grp", "row"), None), P("grp"), P(), P(), P()),
        check_vma=False,
    )
```

```python
import functools

import jax
import jax.numpy as jnp
from jax import lax
from jax.experimental import pallas as pl
from jax.experimental.pallas import tpu as pltpu
from jax.sharding import PartitionSpec as P

LANES = 128
ROW_STEP = 2048
PIECE = 1024
SMALL = 10
VMEM_LIMIT = 60 * 1024 * 1024
END_LIMIT = 16 * 1024 * 1024
F32 = jnp.float32
BF16 = jnp.bfloat16


def split3(x):
    a = x.astype(BF16)
    r = x - a.astype(F32)
    b = r.astype(BF16)
    c = (r - b.astype(F32)).astype(BF16)
    return a, b, c


def hot_dot(hot, x, dims):
    (left,), (right,) = dims
    return lax.dot_general(
        jnp.concatenate([hot] * 3, axis=left),
        jnp.concatenate(split3(x), axis=right),
        (dims, ((), ())),
        preferred_element_type=F32,
    )


def iota_rows(n):
    return lax.broadcasted_iota(jnp.int32, (n, 1), 0)


def pick(values, low, high_hot):
    found = []
    for at in range(0, low.shape[1], LANES):
        index = jnp.broadcast_to(low[:, at : at + LANES], values.shape)
        found.append(jnp.take_along_axis(values, index, axis=1, mode="promise_in_bounds"))
    return jnp.sum(
        jnp.where(high_hot, jnp.concatenate(found, axis=1), jnp.zeros((), values.dtype)),
        axis=0,
        keepdims=True,
    )


def main_kernel(n_out, count_ref, features_ref, *args):
    small = args[:SMALL]
    out_refs = args[SMALL : SMALL + n_out]
    held = args[SMALL + n_out : 2 * SMALL + n_out]
    feats, table, s0, s1, h0, h1, b0, b1, r0, r1, w0, w1, county_acc, prec_acc, state_acc, *outs, small_sems, sems, out_sems = (
        args[2 * SMALL + n_out :]
    )
    (
        state_nation_ref,
        nation_ref,
        state_ref,
        county_state_ref,
        county_ref,
        beta_ref,
        precinct_ref,
        prec_ref,
        map_ref,
        outcome_ref,
    ) = held
    scores, hot_rows, bases, residuals, weights = (s0, s1), (h0, h1), (b0, b1), (r0, r1), (w0, w1)
    n_row = len(outs) // 2
    state_outs, county_outs = outs[:n_row], outs[n_row:]
    n_states = state_ref.shape[0]
    n_nations = nation_ref.shape[0]
    n_cnt, p_size = county_ref.shape
    n_hi = prec_ref.shape[0]
    chunks = precinct_ref.shape[0]
    size = precinct_ref.shape[2]

    def fetch(j):
        copies = []
        for k in range(size // PIECE):
            piece = j * (size // PIECE) + k
            rows = pl.ds(pl.multiple_of(piece * PIECE, PIECE), PIECE)
            copies.append(
                pltpu.make_async_copy(features_ref.at[rows], feats.at[rows], sems.at[piece])
            )
        return copies

    def start(j):
        for copy in fetch(j):
            copy.start()

    def wait(j):
        for copy in fetch(j):
            copy.wait()

    small_copies = [
        pltpu.make_async_copy(source, target, small_sems.at[k])
        for k, (source, target) in enumerate(zip(small, held))
    ]
    for copy in small_copies:
        copy.start()
    start(0)
    for copy in small_copies:
        copy.wait()
    start(1)

    states = county_state_ref[lax.axis_index("grp")]
    state_hot = (iota_rows(n_states) == states).astype(F32).astype(BF16)
    nation_hot = (iota_rows(n_nations) == state_nation_ref[...]).astype(F32).astype(BF16)
    upper = state_ref[...] + hot_dot(nation_hot, nation_ref[...], ((0,), (0,)))
    table[...] = (county_ref[...] + hot_dot(state_hot, upper, ((0,), (0,))) + beta_ref[...]).astype(BF16)
    county_acc[...] = jnp.zeros_like(county_acc)
    prec_acc[...] = jnp.zeros_like(prec_acc)

    def block(j):
        return feats[pl.ds(pl.multiple_of(j * size, size), size), :]

    def parts_of(j):
        prec = precinct_ref[j]
        return jnp.bitwise_and(prec, LANES - 1), iota_rows(n_hi) == jnp.right_shift(prec, 7)

    def score(j, k):
        low, high_hot = parts_of(j)
        bases[k][...] = pick(prec_ref[...], low, high_hot)
        hot_rows[k][...] = pick(map_ref[...], low, high_hot)
        scores[k][...] = lax.dot_general(
            table[...], block(j), (((1,), (1,)), ((), ())), preferred_element_type=F32
        )

    def residue(j, k):
        county_hot = iota_rows(n_cnt) == hot_rows[k][...]
        linear = jnp.sum(jnp.where(county_hot, scores[k][...], 0.0), axis=0, keepdims=True)
        linear = linear + bases[k][...]
        row = j * size + lax.broadcasted_iota(jnp.int32, (1, size), 1)
        count = outcome_ref[j].astype(F32)
        residual = jnp.where(row < count_ref[0], count - jnp.exp(linear), 0.0)
        residuals[k][...] = residual
        rounded = residual.astype(BF16).astype(F32)
        weights[k][...] = jnp.where(county_hot, rounded, 0.0).astype(BF16)

    def collect(j, k):
        county_acc[...] += jnp.dot(weights[k][...], block(j), preferred_element_type=F32)
        low, high_hot = parts_of(j)
        low_hot = (iota_rows(LANES) == low).astype(F32).astype(BF16)
        by_high = jnp.concatenate(
            [jnp.where(high_hot, x.astype(F32), 0.0) for x in split3(residuals[k][...])[:2]], axis=0
        ).astype(BF16)
        prec_acc[...] += lax.dot_general(
            by_high, low_hot, (((1,), (1,)), ((), ())), preferred_element_type=F32
        )

    wait(0)
    score(0, 0)
    wait(1)
    start(2)
    start(3)
    score(1, 1)
    residue(0, 0)

    def body(t, carry):
        j = 2 * t
        wait(j)
        wait(j + 1)

        @pl.when(j + 2 < chunks)
        def _():
            start(j + 2)
            start(j + 3)

        residue(j - 1, 1)
        score(j, 0)
        collect(j - 2, 0)
        residue(j, 0)
        score(j + 1, 1)
        collect(j - 1, 1)
        return carry

    lax.fori_loop(1, chunks // 2, body, 0)
    residue(chunks - 1, 1)
    collect(chunks - 2, 0)
    collect(chunks - 1, 1)

    me = lax.axis_index("row")
    share = n_cnt // n_row
    per = n_states // n_row
    prec_sum = prec_acc[:n_hi] + prec_acc[n_hi:]
    own_rows = pl.ds(pl.multiple_of(me * share, share), share)

    def send(k):
        copy = pltpu.make_async_copy(outs[k], out_refs[k], out_sems.at[k])
        copy.start()
        return copy

    copies = []
    for d in range(n_row):
        peer = jnp.bitwise_xor(me, d)
        sums = county_acc[pl.ds(pl.multiple_of(peer * share, share), share), :]
        county_outs[d][:share, :] = sums if d else sums - county_ref[own_rows, :]
        county_outs[d][share:, :LANES] = prec_sum if d else prec_sum - prec_ref[...]
        county_outs[d][share:, LANES:] = jnp.zeros((n_hi, p_size - LANES), F32)
        copies.append(send(n_row + d))
    state_acc[...] = hot_dot(state_hot, county_acc[...], ((1,), (0,)))
    for d in range(n_row):
        peer = jnp.bitwise_xor(me, d)
        state_outs[d][...] = state_acc[pl.ds(pl.multiple_of(peer * per, per), per), :]
        copies.append(send(d))
    for copy in copies:
        copy.wait()


def county_end_kernel(state_nation_ref, state_ref, nation_ref, beta_ref, *refs):
    *parts, county_out, prec_out, prior_out, hot_out = refs
    share = county_out.shape[0]
    n_states = state_ref.shape[0]
    n_nations = nation_ref.shape[0]
    prior_out[:n_states, :] = state_ref[...]
    prior_out[n_states : n_states + n_nations, :] = nation_ref[...]
    prior_out[n_states + n_nations :, :] = beta_ref[...]
    hot_out[...] = (iota_rows(n_nations) == state_nation_ref[...]).astype(F32)
    county_out[...] = total_of([part[:share, :] for part in parts])
    prec_out[...] = total_of([part[share:, :LANES] for part in parts])


def end_kernel(prior_ref, hot_ref, *refs):
    *gathered, state_out, nation_out, beta_out, total = refs
    me = lax.axis_index("row")
    per = gathered[0].shape[0]
    n_states = state_out.shape[0]
    n_nations = nation_out.shape[0]
    for d, part in enumerate(gathered):
        peer = jnp.bitwise_xor(me, d)
        total[pl.ds(pl.multiple_of(peer * per, per), per), :] = part[...]
    sums = total[...]
    nation_total = hot_dot(hot_ref[...].astype(BF16), sums, ((1,), (0,)))
    state_out[...] = sums - prior_ref[:n_states, :]
    nation_out[...] = nation_total - prior_ref[n_states : n_states + n_nations, :]
    beta_out[...] = jnp.sum(nation_total, axis=0, keepdims=True) - prior_ref[n_states + n_nations :, :]


def swap(x, axis, d):
    n = lax.axis_size(axis)
    return lax.ppermute(x, axis, [(i, i ^ d) for i in range(n)])


def gather_by(x, axis, distances):
    return [x] + [swap(x, axis, d) for d in distances]


def total_of(parts):
    while len(parts) > 1:
        parts = [sum(parts[i : i + 2][1:], parts[i]) for i in range(0, len(parts), 2)]
    return parts[0]


def on_device(
    features,
    precinct,
    outcome,
    row_counts,
    beta,
    nation_coef,
    state_coef,
    county_coef,
    precinct_coef,
    precinct_county,
    county_state,
    state_nation,
):
    rows_here, p_size = features.shape
    cnt_here = county_coef.shape[0]
    prec_here = precinct_coef.shape[0]
    n_states = state_coef.shape[0]
    n_row = lax.axis_size("row")
    n_grp = lax.axis_size("grp")
    share = cnt_here // n_row
    n_hi = prec_here // LANES
    steps = rows_here // ROW_STEP
    per = n_states // n_row

    precinct3 = precinct.reshape(steps, 1, ROW_STEP)
    outcome3 = outcome.reshape(steps, 1, ROW_STEP)
    states3 = county_state.reshape(n_grp, 1, cnt_here)
    prec2 = precinct_coef.reshape(n_hi, LANES)
    map2 = precinct_county.reshape(n_hi, LANES)
    beta2 = beta.reshape(1, p_size)
    nation_row = state_nation.reshape(1, n_states)

    n_nations = nation_coef.shape[0]
    small = (
        nation_row,
        nation_coef,
        state_coef,
        states3,
        county_coef,
        beta2,
        precinct3,
        prec2,
        map2,
        outcome3,
    )
    outs = pl.pallas_call(
        functools.partial(main_kernel, 2 * n_row),
        in_specs=[pl.BlockSpec(memory_space=pltpu.VMEM)]
        + [pl.BlockSpec(memory_space=pltpu.HBM)] * (SMALL + 1),
        out_specs=[pl.BlockSpec(memory_space=pltpu.HBM)] * (2 * n_row),
        out_shape=[jax.ShapeDtypeStruct((per, p_size), F32)] * n_row
        + [jax.ShapeDtypeStruct((share + n_hi, p_size), F32)] * n_row,
        scratch_shapes=[pltpu.VMEM(x.shape, x.dtype) for x in small]
        + [
            pltpu.VMEM((rows_here, p_size), BF16),
            pltpu.VMEM((cnt_here, p_size), BF16),
            pltpu.VMEM((cnt_here, ROW_STEP), F32),
            pltpu.VMEM((cnt_here, ROW_STEP), F32),
            pltpu.VMEM((1, ROW_STEP), jnp.int32),
            pltpu.VMEM((1, ROW_STEP), jnp.int32),
            pltpu.VMEM((1, ROW_STEP), F32),
            pltpu.VMEM((1, ROW_STEP), F32),
            pltpu.VMEM((1, ROW_STEP), F32),
            pltpu.VMEM((1, ROW_STEP), F32),
            pltpu.VMEM((cnt_here, ROW_STEP), BF16),
            pltpu.VMEM((cnt_here, ROW_STEP), BF16),
            pltpu.VMEM((cnt_here, p_size), F32),
            pltpu.VMEM((2 * n_hi, LANES), F32),
            pltpu.VMEM(state_coef.shape, F32),
        ]
        + [pltpu.VMEM((per, p_size), F32)] * n_row
        + [pltpu.VMEM((share + n_hi, p_size), F32)] * n_row
        + [
            pltpu.SemaphoreType.DMA((SMALL,)),
            pltpu.SemaphoreType.DMA((rows_here // PIECE,)),
            pltpu.SemaphoreType.DMA((2 * n_row,)),
        ],
        compiler_params=pltpu.CompilerParams(vmem_limit_bytes=VMEM_LIMIT),
        name="local_sums",
    )(row_counts.reshape(1, 1, 1), features, *small)

    near = 1 << (n_grp.bit_length() // 2 - 1)
    own_sum = lax.optimization_barrier(outs[0] + swap(outs[1], "row", 1))
    state_piece = total_of([swap(outs[d], "row", d) for d in range(2, n_row)]) + own_sum
    county_outs = outs[n_row:]
    from_core = [swap(county_outs[d ^ 1], "row", 1) for d in range(0, n_row, 2)]
    state_piece, *from_core = lax.optimization_barrier((state_piece, *from_core))
    chip_sums = [county_outs[d] + from_core[d // 2] for d in range(2, n_row, 2)]
    state_piece = total_of(gather_by(state_piece, "grp", range(1, near)))
    state_piece, *chip_sums = lax.optimization_barrier((state_piece, *chip_sums))
    county_parts = [county_outs[0], from_core[0]] + [
        swap(x, "row", d) for x, d in zip(chip_sums, range(2, n_row, 2))
    ]
    county_grad, precinct_grad, prior, nation_hot = pl.pallas_call(
        county_end_kernel,
        out_shape=[
            jax.ShapeDtypeStruct((share, p_size), F32),
            jax.ShapeDtypeStruct((n_hi, LANES), F32),
            jax.ShapeDtypeStruct((n_states + n_nations + 1, p_size), F32),
            jax.ShapeDtypeStruct((n_nations, n_states), F32),
        ],
        compiler_params=pltpu.CompilerParams(vmem_limit_bytes=END_LIMIT),
        name="county_totals",
    )(nation_row, state_coef, nation_coef, beta2, *county_parts)

    state_piece = total_of(gather_by(state_piece, "grp", range(near, n_grp, near)))
    gathered = gather_by(state_piece, "row", range(1, n_row))
    state_grad, nation_grad, beta_grad = pl.pallas_call(
        end_kernel,
        out_shape=[
            jax.ShapeDtypeStruct(state_coef.shape, F32),
            jax.ShapeDtypeStruct(nation_coef.shape, F32),
            jax.ShapeDtypeStruct((1, p_size), F32),
        ],
        scratch_shapes=[pltpu.VMEM(state_coef.shape, F32)],
        compiler_params=pltpu.CompilerParams(vmem_limit_bytes=END_LIMIT),
        name="upper_totals",
    )(prior, nation_hot, *gathered)
    return county_grad, precinct_grad.reshape(prec_here), state_grad, nation_grad, beta_grad.reshape(p_size)


def solution(mesh):
    placed = (
        P(("grp", "row"), None),
        P(("grp", "row")),
        P(("grp", "row")),
        P("grp", "row"),
        P(),
        P(),
        P(),
        P("grp", None),
        P("grp"),
        P("grp"),
        P(),
        P(),
    )
    return jax.shard_map(
        on_device,
        mesh=mesh,
        in_specs=placed,
        out_specs=(P(("grp", "row"), None), P("grp"), P(), P(), P()),
        check_vma=False,
    )
```

```python
import functools

import jax
import jax.numpy as jnp
from jax import lax
from jax.experimental import pallas as pl
from jax.experimental.pallas import tpu as pltpu
from jax.sharding import PartitionSpec as P

LANES = 128
ROW_STEP = 2048
SMALL = 10
VMEM_LIMIT = 60 * 1024 * 1024
END_LIMIT = 16 * 1024 * 1024
F32 = jnp.float32
BF16 = jnp.bfloat16


def split3(x):
    a = x.astype(BF16)
    r = x - a.astype(F32)
    b = r.astype(BF16)
    c = (r - b.astype(F32)).astype(BF16)
    return a, b, c


def hot_dot(hot, x, dims):
    (left,), (right,) = dims
    return lax.dot_general(
        jnp.concatenate([hot] * 3, axis=left),
        jnp.concatenate(split3(x), axis=right),
        (dims, ((), ())),
        preferred_element_type=F32,
    )


def iota_rows(n):
    return lax.broadcasted_iota(jnp.int32, (n, 1), 0)


def pick(values, low, high_hot):
    found = []
    for at in range(0, low.shape[1], LANES):
        index = jnp.broadcast_to(low[:, at : at + LANES], values.shape)
        found.append(jnp.take_along_axis(values, index, axis=1, mode="promise_in_bounds"))
    return jnp.sum(
        jnp.where(high_hot, jnp.concatenate(found, axis=1), jnp.zeros((), values.dtype)),
        axis=0,
        keepdims=True,
    )


def main_kernel(n_out, count_ref, features_ref, *args):
    small = args[:SMALL]
    out_refs = args[SMALL : SMALL + n_out]
    held = args[SMALL + n_out : 2 * SMALL + n_out]
    feats, table, s0, s1, h0, h1, b0, b1, r0, r1, w0, w1, county_acc, prec_acc, state_acc, *outs, small_sems, sems, out_sems = (
        args[2 * SMALL + n_out :]
    )
    (
        state_nation_ref,
        nation_ref,
        state_ref,
        county_state_ref,
        county_ref,
        beta_ref,
        precinct_ref,
        prec_ref,
        map_ref,
        outcome_ref,
    ) = held
    scores, hot_rows, bases, residuals, weights = (s0, s1), (h0, h1), (b0, b1), (r0, r1), (w0, w1)
    n_row = len(outs) // 2
    state_outs, county_outs = outs[:n_row], outs[n_row:]
    n_states = state_ref.shape[0]
    n_nations = nation_ref.shape[0]
    n_cnt, p_size = county_ref.shape
    n_hi = prec_ref.shape[0]
    chunks = precinct_ref.shape[0]
    size = precinct_ref.shape[2]

    def fetch(j):
        rows = pl.ds(pl.multiple_of(j * size, size), size)
        return pltpu.make_async_copy(features_ref.at[rows], feats.at[rows], sems.at[j])

    small_copies = [
        pltpu.make_async_copy(source, target, small_sems.at[k])
        for k, (source, target) in enumerate(zip(small, held))
    ]
    for copy in small_copies:
        copy.start()
    for j in range(2):
        fetch(j).start()
    for copy in small_copies:
        copy.wait()
    for j in range(2, 4):
        fetch(j).start()

    states = county_state_ref[lax.axis_index("grp")]
    state_hot = (iota_rows(n_states) == states).astype(F32).astype(BF16)
    nation_hot = (iota_rows(n_nations) == state_nation_ref[...]).astype(F32).astype(BF16)
    upper = state_ref[...] + hot_dot(nation_hot, nation_ref[...], ((0,), (0,)))
    table[...] = (county_ref[...] + hot_dot(state_hot, upper, ((0,), (0,))) + beta_ref[...]).astype(BF16)
    county_acc[...] = jnp.zeros_like(county_acc)
    prec_acc[...] = jnp.zeros_like(prec_acc)

    def block(j):
        return feats[pl.ds(pl.multiple_of(j * size, size), size), :]

    def parts_of(j):
        prec = precinct_ref[j]
        return jnp.bitwise_and(prec, LANES - 1), iota_rows(n_hi) == jnp.right_shift(prec, 7)

    def score(j, k):
        low, high_hot = parts_of(j)
        bases[k][...] = pick(prec_ref[...], low, high_hot)
        hot_rows[k][...] = pick(map_ref[...], low, high_hot)
        scores[k][...] = lax.dot_general(
            table[...], block(j), (((1,), (1,)), ((), ())), preferred_element_type=F32
        )

    def residue(j, k):
        county_hot = iota_rows(n_cnt) == hot_rows[k][...]
        linear = jnp.sum(jnp.where(county_hot, scores[k][...], 0.0), axis=0, keepdims=True)
        linear = linear + bases[k][...]
        row = j * size + lax.broadcasted_iota(jnp.int32, (1, size), 1)
        count = outcome_ref[j].astype(F32)
        residual = jnp.where(row < count_ref[0], count - jnp.exp(linear), 0.0)
        residuals[k][...] = residual
        rounded = residual.astype(BF16).astype(F32)
        weights[k][...] = jnp.where(county_hot, rounded, 0.0).astype(BF16)

    def collect(j, k):
        county_acc[...] += jnp.dot(weights[k][...], block(j), preferred_element_type=F32)
        low, high_hot = parts_of(j)
        low_hot = (iota_rows(LANES) == low).astype(F32).astype(BF16)
        by_high = jnp.concatenate(
            [jnp.where(high_hot, x.astype(F32), 0.0) for x in split3(residuals[k][...])[:2]], axis=0
        ).astype(BF16)
        prec_acc[...] += lax.dot_general(
            by_high, low_hot, (((1,), (1,)), ((), ())), preferred_element_type=F32
        )

    fetch(0).wait()
    score(0, 0)
    fetch(1).wait()
    score(1, 1)
    residue(0, 0)

    def body(t, carry):
        j = 2 * t
        fetch(j).wait()
        fetch(j + 1).wait()

        @pl.when(j + 2 < chunks)
        def _():
            fetch(j + 2).start()
            fetch(j + 3).start()

        residue(j - 1, 1)
        score(j, 0)
        collect(j - 2, 0)
        residue(j, 0)
        score(j + 1, 1)
        collect(j - 1, 1)
        return carry

    lax.fori_loop(1, chunks // 2, body, 0)
    residue(chunks - 1, 1)
    collect(chunks - 2, 0)
    collect(chunks - 1, 1)

    me = lax.axis_index("row")
    share = n_cnt // n_row
    per = n_states // n_row
    prec_sum = prec_acc[:n_hi] + prec_acc[n_hi:]
    own_rows = pl.ds(pl.multiple_of(me * share, share), share)

    def send(k):
        copy = pltpu.make_async_copy(outs[k], out_refs[k], out_sems.at[k])
        copy.start()
        return copy

    copies = []
    for d in range(n_row):
        peer = jnp.bitwise_xor(me, d)
        sums = county_acc[pl.ds(pl.multiple_of(peer * share, share), share), :]
        county_outs[d][:share, :] = sums if d else sums - county_ref[own_rows, :]
        county_outs[d][share:, :LANES] = prec_sum if d else prec_sum - prec_ref[...]
        county_outs[d][share:, LANES:] = jnp.zeros((n_hi, p_size - LANES), F32)
        copies.append(send(n_row + d))
    state_acc[...] = hot_dot(state_hot, county_acc[...], ((1,), (0,)))
    for d in range(n_row):
        peer = jnp.bitwise_xor(me, d)
        state_outs[d][...] = state_acc[pl.ds(pl.multiple_of(peer * per, per), per), :]
        copies.append(send(d))
    for copy in copies:
        copy.wait()


def county_end_kernel(state_nation_ref, state_ref, nation_ref, beta_ref, *refs):
    *parts, county_out, prec_out, prior_out, hot_out = refs
    share = county_out.shape[0]
    n_states = state_ref.shape[0]
    n_nations = nation_ref.shape[0]
    prior_out[:n_states, :] = state_ref[...]
    prior_out[n_states : n_states + n_nations, :] = nation_ref[...]
    prior_out[n_states + n_nations :, :] = beta_ref[...]
    hot_out[...] = (iota_rows(n_nations) == state_nation_ref[...]).astype(F32)
    county_out[...] = total_of([part[:share, :] for part in parts])
    prec_out[...] = total_of([part[share:, :LANES] for part in parts])


def end_kernel(prior_ref, hot_ref, *refs):
    *gathered, state_out, nation_out, beta_out, total = refs
    me = lax.axis_index("row")
    per = gathered[0].shape[0]
    n_states = state_out.shape[0]
    n_nations = nation_out.shape[0]
    for d, part in enumerate(gathered):
        peer = jnp.bitwise_xor(me, d)
        total[pl.ds(pl.multiple_of(peer * per, per), per), :] = part[...]
    sums = total[...]
    nation_total = hot_dot(hot_ref[...].astype(BF16), sums, ((1,), (0,)))
    state_out[...] = sums - prior_ref[:n_states, :]
    nation_out[...] = nation_total - prior_ref[n_states : n_states + n_nations, :]
    beta_out[...] = jnp.sum(nation_total, axis=0, keepdims=True) - prior_ref[n_states + n_nations :, :]


def swap(x, axis, d):
    n = lax.axis_size(axis)
    return lax.ppermute(x, axis, [(i, i ^ d) for i in range(n)])


def gather_by(x, axis, distances):
    return [x] + [swap(x, axis, d) for d in distances]


def total_of(parts):
    while len(parts) > 1:
        parts = [sum(parts[i : i + 2][1:], parts[i]) for i in range(0, len(parts), 2)]
    return parts[0]


def on_device(
    features,
    precinct,
    outcome,
    row_counts,
    beta,
    nation_coef,
    state_coef,
    county_coef,
    precinct_coef,
    precinct_county,
    county_state,
    state_nation,
):
    rows_here, p_size = features.shape
    cnt_here = county_coef.shape[0]
    prec_here = precinct_coef.shape[0]
    n_states = state_coef.shape[0]
    n_row = lax.axis_size("row")
    n_grp = lax.axis_size("grp")
    share = cnt_here // n_row
    n_hi = prec_here // LANES
    steps = rows_here // ROW_STEP
    per = n_states // n_row

    precinct3 = precinct.reshape(steps, 1, ROW_STEP)
    outcome3 = outcome.reshape(steps, 1, ROW_STEP)
    states3 = county_state.reshape(n_grp, 1, cnt_here)
    prec2 = precinct_coef.reshape(n_hi, LANES)
    map2 = precinct_county.reshape(n_hi, LANES)
    beta2 = beta.reshape(1, p_size)
    nation_row = state_nation.reshape(1, n_states)

    n_nations = nation_coef.shape[0]
    small = (
        nation_row,
        nation_coef,
        state_coef,
        states3,
        county_coef,
        beta2,
        precinct3,
        prec2,
        map2,
        outcome3,
    )
    outs = pl.pallas_call(
        functools.partial(main_kernel, 2 * n_row),
        in_specs=[pl.BlockSpec(memory_space=pltpu.VMEM)]
        + [pl.BlockSpec(memory_space=pltpu.HBM)] * (SMALL + 1),
        out_specs=[pl.BlockSpec(memory_space=pltpu.HBM)] * (2 * n_row),
        out_shape=[jax.ShapeDtypeStruct((per, p_size), F32)] * n_row
        + [jax.ShapeDtypeStruct((share + n_hi, p_size), F32)] * n_row,
        scratch_shapes=[pltpu.VMEM(x.shape, x.dtype) for x in small]
        + [
            pltpu.VMEM((rows_here, p_size), BF16),
            pltpu.VMEM((cnt_here, p_size), BF16),
            pltpu.VMEM((cnt_here, ROW_STEP), F32),
            pltpu.VMEM((cnt_here, ROW_STEP), F32),
            pltpu.VMEM((1, ROW_STEP), jnp.int32),
            pltpu.VMEM((1, ROW_STEP), jnp.int32),
            pltpu.VMEM((1, ROW_STEP), F32),
            pltpu.VMEM((1, ROW_STEP), F32),
            pltpu.VMEM((1, ROW_STEP), F32),
            pltpu.VMEM((1, ROW_STEP), F32),
            pltpu.VMEM((cnt_here, ROW_STEP), BF16),
            pltpu.VMEM((cnt_here, ROW_STEP), BF16),
            pltpu.VMEM((cnt_here, p_size), F32),
            pltpu.VMEM((2 * n_hi, LANES), F32),
            pltpu.VMEM(state_coef.shape, F32),
        ]
        + [pltpu.VMEM((per, p_size), F32)] * n_row
        + [pltpu.VMEM((share + n_hi, p_size), F32)] * n_row
        + [
            pltpu.SemaphoreType.DMA((SMALL,)),
            pltpu.SemaphoreType.DMA((steps,)),
            pltpu.SemaphoreType.DMA((2 * n_row,)),
        ],
        compiler_params=pltpu.CompilerParams(vmem_limit_bytes=VMEM_LIMIT),
        name="local_sums",
    )(row_counts.reshape(1, 1, 1), features, *small)

    near = 1 << (n_grp.bit_length() // 2 - 1)
    own_sum = lax.optimization_barrier(outs[0] + swap(outs[1], "row", 1))
    state_piece = total_of([swap(outs[d], "row", d) for d in range(2, n_row)]) + own_sum
    county_outs = outs[n_row:]
    from_core = [swap(county_outs[d ^ 1], "row", 1) for d in range(0, n_row, 2)]
    state_piece, *from_core = lax.optimization_barrier((state_piece, *from_core))
    chip_sums = [county_outs[d] + from_core[d // 2] for d in range(2, n_row, 2)]
    state_piece = total_of(gather_by(state_piece, "grp", range(1, near)))
    state_piece, *chip_sums = lax.optimization_barrier((state_piece, *chip_sums))
    county_parts = [county_outs[0], from_core[0]] + [
        swap(x, "row", d) for x, d in zip(chip_sums, range(2, n_row, 2))
    ]
    county_grad, precinct_grad, prior, nation_hot = pl.pallas_call(
        county_end_kernel,
        out_shape=[
            jax.ShapeDtypeStruct((share, p_size), F32),
            jax.ShapeDtypeStruct((n_hi, LANES), F32),
            jax.ShapeDtypeStruct((n_states + n_nations + 1, p_size), F32),
            jax.ShapeDtypeStruct((n_nations, n_states), F32),
        ],
        compiler_params=pltpu.CompilerParams(vmem_limit_bytes=END_LIMIT),
        name="county_totals",
    )(nation_row, state_coef, nation_coef, beta2, *county_parts)

    state_piece = total_of(gather_by(state_piece, "grp", range(near, n_grp, near)))
    gathered = gather_by(state_piece, "row", range(1, n_row))
    state_grad, nation_grad, beta_grad = pl.pallas_call(
        end_kernel,
        out_shape=[
            jax.ShapeDtypeStruct(state_coef.shape, F32),
            jax.ShapeDtypeStruct(nation_coef.shape, F32),
            jax.ShapeDtypeStruct((1, p_size), F32),
        ],
        scratch_shapes=[pltpu.VMEM(state_coef.shape, F32)],
        compiler_params=pltpu.CompilerParams(vmem_limit_bytes=END_LIMIT),
        name="upper_totals",
    )(prior, nation_hot, *gathered)
    return county_grad, precinct_grad.reshape(prec_here), state_grad, nation_grad, beta_grad.reshape(p_size)


def solution(mesh):
    placed = (
        P(("grp", "row"), None),
        P(("grp", "row")),
        P(("grp", "row")),
        P("grp", "row"),
        P(),
        P(),
        P(),
        P("grp", None),
        P("grp"),
        P("grp"),
        P(),
        P(),
    )
    return jax.shard_map(
        on_device,
        mesh=mesh,
        in_specs=placed,
        out_specs=(P(("grp", "row"), None), P("grp"), P(), P(), P()),
        check_vma=False,
    )
```

```python
import functools

import jax
import jax.numpy as jnp
from jax import lax
from jax.experimental import pallas as pl
from jax.experimental.pallas import tpu as pltpu
from jax.sharding import PartitionSpec as P

LANES = 128
ROW_STEP = 2048
SMALL = 10
VMEM_LIMIT = 60 * 1024 * 1024
END_LIMIT = 16 * 1024 * 1024
F32 = jnp.float32
BF16 = jnp.bfloat16


def split3(x):
    a = x.astype(BF16)
    r = x - a.astype(F32)
    b = r.astype(BF16)
    c = (r - b.astype(F32)).astype(BF16)
    return a, b, c


def hot_dot(hot, x, dims):
    (left,), (right,) = dims
    return lax.dot_general(
        jnp.concatenate([hot] * 3, axis=left),
        jnp.concatenate(split3(x), axis=right),
        (dims, ((), ())),
        preferred_element_type=F32,
    )


def iota_rows(n):
    return lax.broadcasted_iota(jnp.int32, (n, 1), 0)


def pick(values, low, high_hot):
    found = []
    for at in range(0, low.shape[1], LANES):
        index = jnp.broadcast_to(low[:, at : at + LANES], values.shape)
        found.append(jnp.take_along_axis(values, index, axis=1, mode="promise_in_bounds"))
    return jnp.sum(
        jnp.where(high_hot, jnp.concatenate(found, axis=1), jnp.zeros((), values.dtype)),
        axis=0,
        keepdims=True,
    )


def main_kernel(n_out, count_ref, features_ref, *args):
    small = args[:SMALL]
    out_refs = args[SMALL : SMALL + n_out]
    held = args[SMALL + n_out : 2 * SMALL + n_out]
    feats, table, s0, s1, h0, h1, b0, b1, r0, r1, w0, w1, county_acc, prec_acc, state_acc, *outs, small_sems, sems, out_sems = (
        args[2 * SMALL + n_out :]
    )
    (
        state_nation_ref,
        nation_ref,
        state_ref,
        county_state_ref,
        county_ref,
        beta_ref,
        precinct_ref,
        prec_ref,
        map_ref,
        outcome_ref,
    ) = held
    scores, hot_rows, bases, residuals, weights = (s0, s1), (h0, h1), (b0, b1), (r0, r1), (w0, w1)
    n_row = len(outs) // 2
    state_outs, county_outs = outs[:n_row], outs[n_row:]
    n_states = state_ref.shape[0]
    n_nations = nation_ref.shape[0]
    n_cnt, p_size = county_ref.shape
    n_hi = prec_ref.shape[0]
    chunks = precinct_ref.shape[0]
    size = precinct_ref.shape[2]

    def fetch(j):
        rows = pl.ds(pl.multiple_of(j * size, size), size)
        return pltpu.make_async_copy(features_ref.at[rows], feats.at[rows], sems.at[j])

    small_copies = [
        pltpu.make_async_copy(source, target, small_sems.at[k])
        for k, (source, target) in enumerate(zip(small, held))
    ]
    for copy in small_copies:
        copy.start()
    fetch(0).start()
    for copy in small_copies:
        copy.wait()
    fetch(1).start()

    states = county_state_ref[lax.axis_index("grp")]
    state_hot = (iota_rows(n_states) == states).astype(F32).astype(BF16)
    nation_hot = (iota_rows(n_nations) == state_nation_ref[...]).astype(F32).astype(BF16)
    upper = state_ref[...] + hot_dot(nation_hot, nation_ref[...], ((0,), (0,)))
    table[...] = (county_ref[...] + hot_dot(state_hot, upper, ((0,), (0,))) + beta_ref[...]).astype(BF16)
    county_acc[...] = jnp.zeros_like(county_acc)
    prec_acc[...] = jnp.zeros_like(prec_acc)

    def block(j):
        return feats[pl.ds(pl.multiple_of(j * size, size), size), :]

    def parts_of(j):
        prec = precinct_ref[j]
        return jnp.bitwise_and(prec, LANES - 1), iota_rows(n_hi) == jnp.right_shift(prec, 7)

    def score(j, k):
        low, high_hot = parts_of(j)
        bases[k][...] = pick(prec_ref[...], low, high_hot)
        hot_rows[k][...] = pick(map_ref[...], low, high_hot)
        scores[k][...] = lax.dot_general(
            table[...], block(j), (((1,), (1,)), ((), ())), preferred_element_type=F32
        )

    def residue(j, k):
        county_hot = iota_rows(n_cnt) == hot_rows[k][...]
        linear = jnp.sum(jnp.where(county_hot, scores[k][...], 0.0), axis=0, keepdims=True)
        linear = linear + bases[k][...]
        row = j * size + lax.broadcasted_iota(jnp.int32, (1, size), 1)
        count = outcome_ref[j].astype(F32)
        residual = jnp.where(row < count_ref[0], count - jnp.exp(linear), 0.0)
        residuals[k][...] = residual
        rounded = residual.astype(BF16).astype(F32)
        weights[k][...] = jnp.where(county_hot, rounded, 0.0).astype(BF16)

    def collect(j, k):
        county_acc[...] += jnp.dot(weights[k][...], block(j), preferred_element_type=F32)
        low, high_hot = parts_of(j)
        low_hot = (iota_rows(LANES) == low).astype(F32).astype(BF16)
        by_high = jnp.concatenate(
            [jnp.where(high_hot, x.astype(F32), 0.0) for x in split3(residuals[k][...])[:2]], axis=0
        ).astype(BF16)
        prec_acc[...] += lax.dot_general(
            by_high, low_hot, (((1,), (1,)), ((), ())), preferred_element_type=F32
        )

    fetch(0).wait()
    for j in range(2, 4):
        fetch(j).start()
    score(0, 0)
    fetch(1).wait()
    score(1, 1)
    residue(0, 0)

    def body(t, carry):
        j = 2 * t
        fetch(j).wait()
        fetch(j + 1).wait()

        @pl.when(j + 2 < chunks)
        def _():
            fetch(j + 2).start()
            fetch(j + 3).start()

        residue(j - 1, 1)
        score(j, 0)
        collect(j - 2, 0)
        residue(j, 0)
        score(j + 1, 1)
        collect(j - 1, 1)
        return carry

    lax.fori_loop(1, chunks // 2, body, 0)
    residue(chunks - 1, 1)
    collect(chunks - 2, 0)
    collect(chunks - 1, 1)

    me = lax.axis_index("row")
    share = n_cnt // n_row
    per = n_states // n_row
    prec_sum = prec_acc[:n_hi] + prec_acc[n_hi:]
    own_rows = pl.ds(pl.multiple_of(me * share, share), share)

    def send(source, target):
        copy = pltpu.make_async_copy(source, target, out_sems.at[len(copies)])
        copy.start()
        copies.append(copy)

    copies = []
    for d in range(1, n_row):
        rows = pl.ds(pl.multiple_of(jnp.bitwise_xor(me, d) * share, share), share)
        send(county_acc.at[rows], out_refs[n_row + d].at[pl.ds(0, share)])
    for d in range(2):
        county_outs[d][share:, :LANES] = prec_sum if d else prec_sum - prec_ref[...]
        county_outs[d][share:, LANES:] = jnp.zeros((n_hi, p_size - LANES), F32)
    for d in range(1, n_row):
        send(county_outs[1].at[pl.ds(share, n_hi)], out_refs[n_row + d].at[pl.ds(share, n_hi)])
    county_outs[0][:share, :] = county_acc[own_rows, :] - county_ref[own_rows, :]
    send(county_outs[0], out_refs[n_row])
    state_acc[...] = hot_dot(state_hot, county_acc[...], ((1,), (0,)))
    for d in range(n_row):
        peer = jnp.bitwise_xor(me, d)
        state_outs[d][...] = state_acc[pl.ds(pl.multiple_of(peer * per, per), per), :]
        send(outs[d], out_refs[d])
    for copy in copies:
        copy.wait()


def county_end_kernel(state_nation_ref, state_ref, nation_ref, beta_ref, *refs):
    *parts, county_out, prec_out, prior_out, hot_out = refs
    share = county_out.shape[0]
    n_states = state_ref.shape[0]
    n_nations = nation_ref.shape[0]
    prior_out[:n_states, :] = state_ref[...]
    prior_out[n_states : n_states + n_nations, :] = nation_ref[...]
    prior_out[n_states + n_nations :, :] = beta_ref[...]
    hot_out[...] = (iota_rows(n_nations) == state_nation_ref[...]).astype(F32)
    county_out[...] = total_of([part[:share, :] for part in parts])
    prec_out[...] = total_of([part[share:, :LANES] for part in parts])


def end_kernel(prior_ref, hot_ref, *refs):
    *gathered, state_out, nation_out, beta_out, total = refs
    me = lax.axis_index("row")
    per = gathered[0].shape[0]
    n_states = state_out.shape[0]
    n_nations = nation_out.shape[0]
    for d, part in enumerate(gathered):
        peer = jnp.bitwise_xor(me, d)
        total[pl.ds(pl.multiple_of(peer * per, per), per), :] = part[...]
    sums = total[...]
    nation_total = hot_dot(hot_ref[...].astype(BF16), sums, ((1,), (0,)))
    state_out[...] = sums - prior_ref[:n_states, :]
    nation_out[...] = nation_total - prior_ref[n_states : n_states + n_nations, :]
    beta_out[...] = jnp.sum(nation_total, axis=0, keepdims=True) - prior_ref[n_states + n_nations :, :]


def swap(x, axis, d):
    n = lax.axis_size(axis)
    return lax.ppermute(x, axis, [(i, i ^ d) for i in range(n)])


def gather_by(x, axis, distances):
    return [x] + [swap(x, axis, d) for d in distances]


def total_of(parts):
    while len(parts) > 1:
        parts = [sum(parts[i : i + 2][1:], parts[i]) for i in range(0, len(parts), 2)]
    return parts[0]


def on_device(
    features,
    precinct,
    outcome,
    row_counts,
    beta,
    nation_coef,
    state_coef,
    county_coef,
    precinct_coef,
    precinct_county,
    county_state,
    state_nation,
):
    rows_here, p_size = features.shape
    cnt_here = county_coef.shape[0]
    prec_here = precinct_coef.shape[0]
    n_states = state_coef.shape[0]
    n_row = lax.axis_size("row")
    n_grp = lax.axis_size("grp")
    share = cnt_here // n_row
    n_hi = prec_here // LANES
    steps = rows_here // ROW_STEP
    per = n_states // n_row

    precinct3 = precinct.reshape(steps, 1, ROW_STEP)
    outcome3 = outcome.reshape(steps, 1, ROW_STEP)
    states3 = county_state.reshape(n_grp, 1, cnt_here)
    prec2 = precinct_coef.reshape(n_hi, LANES)
    map2 = precinct_county.reshape(n_hi, LANES)
    beta2 = beta.reshape(1, p_size)
    nation_row = state_nation.reshape(1, n_states)

    n_nations = nation_coef.shape[0]
    small = (
        nation_row,
        nation_coef,
        state_coef,
        states3,
        county_coef,
        beta2,
        precinct3,
        prec2,
        map2,
        outcome3,
    )
    outs = pl.pallas_call(
        functools.partial(main_kernel, 2 * n_row),
        in_specs=[pl.BlockSpec(memory_space=pltpu.VMEM)]
        + [pl.BlockSpec(memory_space=pltpu.HBM)] * (SMALL + 1),
        out_specs=[pl.BlockSpec(memory_space=pltpu.HBM)] * (2 * n_row),
        out_shape=[jax.ShapeDtypeStruct((per, p_size), F32)] * n_row
        + [jax.ShapeDtypeStruct((share + n_hi, p_size), F32)] * n_row,
        scratch_shapes=[pltpu.VMEM(x.shape, x.dtype) for x in small]
        + [
            pltpu.VMEM((rows_here, p_size), BF16),
            pltpu.VMEM((cnt_here, p_size), BF16),
            pltpu.VMEM((cnt_here, ROW_STEP), F32),
            pltpu.VMEM((cnt_here, ROW_STEP), F32),
            pltpu.VMEM((1, ROW_STEP), jnp.int32),
            pltpu.VMEM((1, ROW_STEP), jnp.int32),
            pltpu.VMEM((1, ROW_STEP), F32),
            pltpu.VMEM((1, ROW_STEP), F32),
            pltpu.VMEM((1, ROW_STEP), F32),
            pltpu.VMEM((1, ROW_STEP), F32),
            pltpu.VMEM((cnt_here, ROW_STEP), BF16),
            pltpu.VMEM((cnt_here, ROW_STEP), BF16),
            pltpu.VMEM((cnt_here, p_size), F32),
            pltpu.VMEM((2 * n_hi, LANES), F32),
            pltpu.VMEM(state_coef.shape, F32),
        ]
        + [pltpu.VMEM((per, p_size), F32)] * n_row
        + [pltpu.VMEM((share + n_hi, p_size), F32)] * n_row
        + [
            pltpu.SemaphoreType.DMA((SMALL,)),
            pltpu.SemaphoreType.DMA((steps,)),
            pltpu.SemaphoreType.DMA((3 * n_row,)),
        ],
        compiler_params=pltpu.CompilerParams(vmem_limit_bytes=VMEM_LIMIT),
        name="local_sums",
    )(row_counts.reshape(1, 1, 1), features, *small)

    near = 1 << (n_grp.bit_length() // 2 - 1)
    own_sum = lax.optimization_barrier(outs[0] + swap(outs[1], "row", 1))
    state_piece = total_of([swap(outs[d], "row", d) for d in range(2, n_row)]) + own_sum
    county_outs = outs[n_row:]
    from_core = [swap(county_outs[d ^ 1], "row", 1) for d in range(0, n_row, 2)]
    state_piece, *from_core = lax.optimization_barrier((state_piece, *from_core))
    chip_sums = [county_outs[d] + from_core[d // 2] for d in range(2, n_row, 2)]
    state_piece = total_of(gather_by(state_piece, "grp", range(1, near)))
    state_piece, *chip_sums = lax.optimization_barrier((state_piece, *chip_sums))
    county_parts = [county_outs[0], from_core[0]] + [
        swap(x, "row", d) for x, d in zip(chip_sums, range(2, n_row, 2))
    ]
    county_grad, precinct_grad, prior, nation_hot = pl.pallas_call(
        county_end_kernel,
        out_shape=[
            jax.ShapeDtypeStruct((share, p_size), F32),
            jax.ShapeDtypeStruct((n_hi, LANES), F32),
            jax.ShapeDtypeStruct((n_states + n_nations + 1, p_size), F32),
            jax.ShapeDtypeStruct((n_nations, n_states), F32),
        ],
        compiler_params=pltpu.CompilerParams(vmem_limit_bytes=END_LIMIT),
        name="county_totals",
    )(nation_row, state_coef, nation_coef, beta2, *county_parts)

    state_piece = total_of(gather_by(state_piece, "grp", range(near, n_grp, near)))
    gathered = gather_by(state_piece, "row", range(1, n_row))
    state_grad, nation_grad, beta_grad = pl.pallas_call(
        end_kernel,
        out_shape=[
            jax.ShapeDtypeStruct(state_coef.shape, F32),
            jax.ShapeDtypeStruct(nation_coef.shape, F32),
            jax.ShapeDtypeStruct((1, p_size), F32),
        ],
        scratch_shapes=[pltpu.VMEM(state_coef.shape, F32)],
        compiler_params=pltpu.CompilerParams(vmem_limit_bytes=END_LIMIT),
        name="upper_totals",
    )(prior, nation_hot, *gathered)
    return county_grad, precinct_grad.reshape(prec_here), state_grad, nation_grad, beta_grad.reshape(p_size)


def solution(mesh):
    placed = (
        P(("grp", "row"), None),
        P(("grp", "row")),
        P(("grp", "row")),
        P("grp", "row"),
        P(),
        P(),
        P(),
        P("grp", None),
        P("grp"),
        P("grp"),
        P(),
        P(),
    )
    return jax.shard_map(
        on_device,
        mesh=mesh,
        in_specs=placed,
        out_specs=(P(("grp", "row"), None), P("grp"), P(), P(), P()),
        check_vma=False,
    )
```

```python
import functools

import jax
import jax.numpy as jnp
from jax import lax
from jax.experimental import pallas as pl
from jax.experimental.pallas import tpu as pltpu
from jax.sharding import PartitionSpec as P

LANES = 128
ROW_STEP = 2048
SMALL = 10
VMEM_LIMIT = 60 * 1024 * 1024
END_LIMIT = 16 * 1024 * 1024
F32 = jnp.float32
BF16 = jnp.bfloat16


def split3(x):
    a = x.astype(BF16)
    r = x - a.astype(F32)
    b = r.astype(BF16)
    c = (r - b.astype(F32)).astype(BF16)
    return a, b, c


def hot_dot(hot, x, dims):
    (left,), (right,) = dims
    return lax.dot_general(
        jnp.concatenate([hot] * 3, axis=left),
        jnp.concatenate(split3(x), axis=right),
        (dims, ((), ())),
        preferred_element_type=F32,
    )


def iota_rows(n):
    return lax.broadcasted_iota(jnp.int32, (n, 1), 0)


def pick(values, low, high_hot):
    found = []
    for at in range(0, low.shape[1], LANES):
        index = jnp.broadcast_to(low[:, at : at + LANES], values.shape)
        found.append(jnp.take_along_axis(values, index, axis=1, mode="promise_in_bounds"))
    return jnp.sum(
        jnp.where(high_hot, jnp.concatenate(found, axis=1), jnp.zeros((), values.dtype)),
        axis=0,
        keepdims=True,
    )


def main_kernel(n_out, count_ref, features_ref, *args):
    small = args[:SMALL]
    out_refs = args[SMALL : SMALL + n_out]
    held = args[SMALL + n_out : 2 * SMALL + n_out]
    feats, table, s0, s1, h0, h1, b0, b1, r0, r1, w0, w1, county_acc, prec_acc, state_acc, *outs, small_sems, sems, out_sems = (
        args[2 * SMALL + n_out :]
    )
    (
        state_nation_ref,
        nation_ref,
        state_ref,
        county_state_ref,
        county_ref,
        beta_ref,
        precinct_ref,
        prec_ref,
        map_ref,
        outcome_ref,
    ) = held
    scores, hot_rows, bases, residuals, weights = (s0, s1), (h0, h1), (b0, b1), (r0, r1), (w0, w1)
    n_row = len(outs) // 2
    state_outs, county_outs = outs[:n_row], outs[n_row:]
    n_states = state_ref.shape[0]
    n_nations = nation_ref.shape[0]
    n_cnt, p_size = county_ref.shape
    n_hi = prec_ref.shape[0]
    chunks = precinct_ref.shape[0]
    size = precinct_ref.shape[2]

    def fetch(j):
        rows = pl.ds(pl.multiple_of(j * size, size), size)
        return pltpu.make_async_copy(features_ref.at[rows], feats.at[rows], sems.at[j])

    small_copies = [
        pltpu.make_async_copy(source, target, small_sems.at[k])
        for k, (source, target) in enumerate(zip(small, held))
    ]
    for copy in small_copies:
        copy.start()
    for j in range(2):
        fetch(j).start()
    for copy in small_copies:
        copy.wait()
    for j in range(2, 4):
        fetch(j).start()

    states = county_state_ref[lax.axis_index("grp")]
    state_hot = (iota_rows(n_states) == states).astype(F32).astype(BF16)
    nation_hot = (iota_rows(n_nations) == state_nation_ref[...]).astype(F32).astype(BF16)
    upper = state_ref[...] + hot_dot(nation_hot, nation_ref[...], ((0,), (0,)))
    table[...] = (county_ref[...] + hot_dot(state_hot, upper, ((0,), (0,))) + beta_ref[...]).astype(BF16)
    county_acc[...] = jnp.zeros_like(county_acc)
    prec_acc[...] = jnp.zeros_like(prec_acc)

    def block(j):
        return feats[pl.ds(pl.multiple_of(j * size, size), size), :]

    def parts_of(j):
        prec = precinct_ref[j]
        return jnp.bitwise_and(prec, LANES - 1), iota_rows(n_hi) == jnp.right_shift(prec, 7)

    def score(j, k):
        low, high_hot = parts_of(j)
        bases[k][...] = pick(prec_ref[...], low, high_hot)
        hot_rows[k][...] = pick(map_ref[...], low, high_hot)
        scores[k][...] = lax.dot_general(
            table[...], block(j), (((1,), (1,)), ((), ())), preferred_element_type=F32
        )

    def residue(j, k):
        county_hot = iota_rows(n_cnt) == hot_rows[k][...]
        linear = jnp.sum(jnp.where(county_hot, scores[k][...], 0.0), axis=0, keepdims=True)
        linear = linear + bases[k][...]
        row = j * size + lax.broadcasted_iota(jnp.int32, (1, size), 1)
        count = outcome_ref[j].astype(F32)
        residual = jnp.where(row < count_ref[0], count - jnp.exp(linear), 0.0)
        residuals[k][...] = residual
        rounded = residual.astype(BF16).astype(F32)
        weights[k][...] = jnp.where(county_hot, rounded, 0.0).astype(BF16)

    def collect(j, k):
        county_acc[...] += jnp.dot(weights[k][...], block(j), preferred_element_type=F32)
        low, high_hot = parts_of(j)
        low_hot = (iota_rows(LANES) == low).astype(F32).astype(BF16)
        by_high = jnp.concatenate(
            [jnp.where(high_hot, x.astype(F32), 0.0) for x in split3(residuals[k][...])[:2]], axis=0
        ).astype(BF16)
        prec_acc[...] += lax.dot_general(
            by_high, low_hot, (((1,), (1,)), ((), ())), preferred_element_type=F32
        )

    fetch(0).wait()
    score(0, 0)
    fetch(1).wait()
    score(1, 1)
    residue(0, 0)

    def body(t, carry):
        j = 2 * t
        fetch(j).wait()
        fetch(j + 1).wait()

        @pl.when(j + 2 < chunks)
        def _():
            fetch(j + 2).start()
            fetch(j + 3).start()

        residue(j - 1, 1)
        score(j, 0)
        collect(j - 2, 0)
        residue(j, 0)
        score(j + 1, 1)
        collect(j - 1, 1)
        return carry

    lax.fori_loop(1, chunks // 2, body, 0)
    residue(chunks - 1, 1)
    collect(chunks - 2, 0)
    collect(chunks - 1, 1)

    me = lax.axis_index("row")
    share = n_cnt // n_row
    per = n_states // n_row
    prec_sum = prec_acc[:n_hi] + prec_acc[n_hi:]
    own_rows = pl.ds(pl.multiple_of(me * share, share), share)

    def send(source, target):
        copy = pltpu.make_async_copy(source, target, out_sems.at[len(copies)])
        copy.start()
        copies.append(copy)

    copies = []
    for d in range(1, n_row):
        rows = pl.ds(pl.multiple_of(jnp.bitwise_xor(me, d) * share, share), share)
        send(county_acc.at[rows], out_refs[n_row + d].at[pl.ds(0, share)])
    for d in range(2):
        county_outs[d][share:, :LANES] = prec_sum if d else prec_sum - prec_ref[...]
        county_outs[d][share:, LANES:] = jnp.zeros((n_hi, p_size - LANES), F32)
    for d in range(1, n_row):
        send(county_outs[1].at[pl.ds(share, n_hi)], out_refs[n_row + d].at[pl.ds(share, n_hi)])
    county_outs[0][:share, :] = county_acc[own_rows, :] - county_ref[own_rows, :]
    send(county_outs[0], out_refs[n_row])
    state_acc[...] = hot_dot(state_hot, county_acc[...], ((1,), (0,)))
    for d in range(n_row):
        peer = jnp.bitwise_xor(me, d)
        state_outs[d][...] = state_acc[pl.ds(pl.multiple_of(peer * per, per), per), :]
        send(outs[d], out_refs[d])
    for copy in copies:
        copy.wait()


def county_end_kernel(state_nation_ref, state_ref, nation_ref, beta_ref, *refs):
    *parts, county_out, prec_out, prior_out, hot_out = refs
    share = county_out.shape[0]
    n_states = state_ref.shape[0]
    n_nations = nation_ref.shape[0]
    prior_out[:n_states, :] = state_ref[...]
    prior_out[n_states : n_states + n_nations, :] = nation_ref[...]
    prior_out[n_states + n_nations :, :] = beta_ref[...]
    hot_out[...] = (iota_rows(n_nations) == state_nation_ref[...]).astype(F32)
    county_out[...] = total_of([part[:share, :] for part in parts])
    prec_out[...] = total_of([part[share:, :LANES] for part in parts])


def end_kernel(prior_ref, hot_ref, *refs):
    *gathered, state_out, nation_out, beta_out, total = refs
    me = lax.axis_index("row")
    per = gathered[0].shape[0]
    n_states = state_out.shape[0]
    n_nations = nation_out.shape[0]
    for d, part in enumerate(gathered):
        peer = jnp.bitwise_xor(me, d)
        total[pl.ds(pl.multiple_of(peer * per, per), per), :] = part[...]
    sums = total[...]
    nation_total = hot_dot(hot_ref[...].astype(BF16), sums, ((1,), (0,)))
    state_out[...] = sums - prior_ref[:n_states, :]
    nation_out[...] = nation_total - prior_ref[n_states : n_states + n_nations, :]
    beta_out[...] = jnp.sum(nation_total, axis=0, keepdims=True) - prior_ref[n_states + n_nations :, :]


def swap(x, axis, d):
    n = lax.axis_size(axis)
    return lax.ppermute(x, axis, [(i, i ^ d) for i in range(n)])


def gather_by(x, axis, distances):
    return [x] + [swap(x, axis, d) for d in distances]


def total_of(parts):
    while len(parts) > 1:
        parts = [sum(parts[i : i + 2][1:], parts[i]) for i in range(0, len(parts), 2)]
    return parts[0]


def on_device(
    features,
    precinct,
    outcome,
    row_counts,
    beta,
    nation_coef,
    state_coef,
    county_coef,
    precinct_coef,
    precinct_county,
    county_state,
    state_nation,
):
    rows_here, p_size = features.shape
    cnt_here = county_coef.shape[0]
    prec_here = precinct_coef.shape[0]
    n_states = state_coef.shape[0]
    n_row = lax.axis_size("row")
    n_grp = lax.axis_size("grp")
    share = cnt_here // n_row
    n_hi = prec_here // LANES
    steps = rows_here // ROW_STEP
    per = n_states // n_row

    precinct3 = precinct.reshape(steps, 1, ROW_STEP)
    outcome3 = outcome.reshape(steps, 1, ROW_STEP)
    states3 = county_state.reshape(n_grp, 1, cnt_here)
    prec2 = precinct_coef.reshape(n_hi, LANES)
    map2 = precinct_county.reshape(n_hi, LANES)
    beta2 = beta.reshape(1, p_size)
    nation_row = state_nation.reshape(1, n_states)

    n_nations = nation_coef.shape[0]
    small = (
        nation_row,
        nation_coef,
        state_coef,
        states3,
        county_coef,
        beta2,
        precinct3,
        prec2,
        map2,
        outcome3,
    )
    outs = pl.pallas_call(
        functools.partial(main_kernel, 2 * n_row),
        in_specs=[pl.BlockSpec(memory_space=pltpu.VMEM)]
        + [pl.BlockSpec(memory_space=pltpu.HBM)] * (SMALL + 1),
        out_specs=[pl.BlockSpec(memory_space=pltpu.HBM)] * (2 * n_row),
        out_shape=[jax.ShapeDtypeStruct((per, p_size), F32)] * n_row
        + [jax.ShapeDtypeStruct((share + n_hi, p_size), F32)] * n_row,
        scratch_shapes=[pltpu.VMEM(x.shape, x.dtype) for x in small]
        + [
            pltpu.VMEM((rows_here, p_size), BF16),
            pltpu.VMEM((cnt_here, p_size), BF16),
            pltpu.VMEM((cnt_here, ROW_STEP), F32),
            pltpu.VMEM((cnt_here, ROW_STEP), F32),
            pltpu.VMEM((1, ROW_STEP), jnp.int32),
            pltpu.VMEM((1, ROW_STEP), jnp.int32),
            pltpu.VMEM((1, ROW_STEP), F32),
            pltpu.VMEM((1, ROW_STEP), F32),
            pltpu.VMEM((1, ROW_STEP), F32),
            pltpu.VMEM((1, ROW_STEP), F32),
            pltpu.VMEM((cnt_here, ROW_STEP), BF16),
            pltpu.VMEM((cnt_here, ROW_STEP), BF16),
            pltpu.VMEM((cnt_here, p_size), F32),
            pltpu.VMEM((2 * n_hi, LANES), F32),
            pltpu.VMEM(state_coef.shape, F32),
        ]
        + [pltpu.VMEM((per, p_size), F32)] * n_row
        + [pltpu.VMEM((share + n_hi, p_size), F32)] * n_row
        + [
            pltpu.SemaphoreType.DMA((SMALL,)),
            pltpu.SemaphoreType.DMA((steps,)),
            pltpu.SemaphoreType.DMA((3 * n_row,)),
        ],
        compiler_params=pltpu.CompilerParams(vmem_limit_bytes=VMEM_LIMIT),
        name="local_sums",
    )(row_counts.reshape(1, 1, 1), features, *small)

    near = 1 << (n_grp.bit_length() // 2 - 1)
    own_sum = lax.optimization_barrier(outs[0] + swap(outs[1], "row", 1))
    state_piece = total_of([swap(outs[d], "row", d) for d in range(2, n_row)]) + own_sum
    county_outs = outs[n_row:]
    from_core = [swap(county_outs[d ^ 1], "row", 1) for d in range(0, n_row, 2)]
    state_piece, *from_core = lax.optimization_barrier((state_piece, *from_core))
    chip_sums = [county_outs[d] + from_core[d // 2] for d in range(2, n_row, 2)]
    state_piece = total_of(gather_by(state_piece, "grp", range(1, near)))
    state_piece, *chip_sums = lax.optimization_barrier((state_piece, *chip_sums))
    county_parts = [county_outs[0], from_core[0]] + [
        swap(x, "row", d) for x, d in zip(chip_sums, range(2, n_row, 2))
    ]
    county_grad, precinct_grad, prior, nation_hot = pl.pallas_call(
        county_end_kernel,
        out_shape=[
            jax.ShapeDtypeStruct((share, p_size), F32),
            jax.ShapeDtypeStruct((n_hi, LANES), F32),
            jax.ShapeDtypeStruct((n_states + n_nations + 1, p_size), F32),
            jax.ShapeDtypeStruct((n_nations, n_states), F32),
        ],
        compiler_params=pltpu.CompilerParams(vmem_limit_bytes=END_LIMIT),
        name="county_totals",
    )(nation_row, state_coef, nation_coef, beta2, *county_parts)

    state_piece = total_of(gather_by(state_piece, "grp", range(near, n_grp, near)))
    gathered = gather_by(state_piece, "row", range(1, n_row))
    state_grad, nation_grad, beta_grad = pl.pallas_call(
        end_kernel,
        out_shape=[
            jax.ShapeDtypeStruct(state_coef.shape, F32),
            jax.ShapeDtypeStruct(nation_coef.shape, F32),
            jax.ShapeDtypeStruct((1, p_size), F32),
        ],
        scratch_shapes=[pltpu.VMEM(state_coef.shape, F32)],
        compiler_params=pltpu.CompilerParams(vmem_limit_bytes=END_LIMIT),
        name="upper_totals",
    )(prior, nation_hot, *gathered)
    return county_grad, precinct_grad.reshape(prec_here), state_grad, nation_grad, beta_grad.reshape(p_size)


def solution(mesh):
    placed = (
        P(("grp", "row"), None),
        P(("grp", "row")),
        P(("grp", "row")),
        P("grp", "row"),
        P(),
        P(),
        P(),
        P("grp", None),
        P("grp"),
        P("grp"),
        P(),
        P(),
    )
    return jax.shard_map(
        on_device,
        mesh=mesh,
        in_specs=placed,
        out_specs=(P(("grp", "row"), None), P("grp"), P(), P(), P()),
        check_vma=False,
    )
```
